32 devices in a mesh: lat: 4 (over x, core), lon: 8 (over z, y).
Axes of the slice: x: 2, y: 2, z: 4, core: 2. Of those that a mesh axis runs over, the one named last changes fastest.
Arguments:
- tracers: float32 [256, 1152, 256], P(('lat', 'lon')), may hold values from 0.1 to 3
- phys_fine: bfloat16 [192, 3072, 144], P('lat', 'lon'), may hold values from -2 to 30, as said below
- mix_coarse: bfloat16 [64, 1024, 48], P('lat', 'lon'), may hold values from 0.0049743652 to 0.19921875
- surf_light: float32 [192, 3072], P('lat', 'lon'), may hold values from 0.5 to 4
- land_mask: int32 [64, 1024], P('lat', 'lon'), may hold values from 0 to 1, as said below
- owner_map: int32 [4, 64], P('lat'), may hold values from -1 to 255, as said below
Outputs:
- tracers_out: float32 [256, 1152, 256], P(('lat', 'lon'))
- heating: bfloat16 [48, 192, 3072], P(None, 'lat', 'lon')
The draws below stay inside these ranges and needn't reach their ends.
Inputs may be any that keep to these rules, and one draw needn't show every extreme that they name: `owner_map`: -1 marks a block whose columns are all land, any other value is the slot that holds the block. Slots are numbered band by band, 64 to a band, owner by owner within a band with 8 slots each, and a block's slot lies in its own band. Every band has a multiple of 8 wet blocks. The wet blocks of a band, taken in order of longitude, are held by the owners in turn: the next wet block after one held by owner o is held by owner o + 1 (after 8 - 1 comes 0), also from the band's last wet block to its first; the r-th wet block of a band (from 0) lies in slot r // 8 of its owner. In some band every slot holds a block. `land_mask`: 1 for an ocean column, 0 for land; every column of a block that owner_map marks -1 is land. `phys_fine`: channel c * 48 + l holds level l of: c = 0 the eastward velocity on a fine cell's east face and c = 1 the northward velocity on its north face, as fractions of a cell per step within -0.15 to 0.15; c = 2 temperature within -2 to 30.
All inputs are finite; a program needn't handle non-finite values.
Results may differ from the reference program's by a relative error of at most 0.001.
Values sent between devices are 32-bit elements; how exact they have to be, the bound alone decides.
No kernel may reach another device: no remote copies, remote signals or barrier semaphores. Data moves between devices by JAX's collectives and lax.ppermute only.
A program may use at most 192 MiB of HBM per device.

```python
import math
from functools import partial
import jax
import jax.numpy as jnp
from jax import lax

NTR = 24
NLEV = 48
BLK = 16
CF = 3
BPD = 8
ITERS = 2
NBY = 4
NBX = 64
NYC = 64
NXC = 1024
NYF = 192
NXF = 3072
WETMAX = 64
SLOTS = 256


def band_layout(key):
    base_key = jax.random.fold_in(key, 7)
    count_key, pick_key, turn_key, order_key, column_key = jax.random.split(base_key, 5)
    owner_count = WETMAX // BPD
    lowest = max(1, BPD - BPD // 4)
    wet_counts = owner_count * jax.random.randint(count_key, (NBY,), lowest, BPD + 1)
    full_band = jax.random.randint(pick_key, (), 0, NBY)
    wet_counts = jnp.where(jnp.arange(NBY) == full_band, WETMAX, wet_counts)
    order_keys = jax.random.split(order_key, NBY)

    def inverse_order(row_key):
        return jnp.argsort(jax.random.permutation(row_key, NBX))
    orders = jax.vmap(inverse_order)(order_keys)
    wet_blocks = orders < wet_counts[:, None]
    wet_ranks = jnp.cumsum(wet_blocks.astype(jnp.int32), axis=1) - 1
    shifts = jax.random.randint(turn_key, (NBY, 1), 0, owner_count)
    owners = (wet_ranks + shifts) % owner_count
    slot_codes = (jnp.arange(NBY)[:, None] * owner_count + owners) * BPD + wet_ranks // owner_count
    owner_table = jnp.where(wet_blocks, slot_codes, -1).astype(jnp.int32)
    column_bits = jax.random.randint(column_key, (NBY * BLK, NBX * BLK), 0, 8) < 7
    block_wet = jnp.repeat(jnp.repeat(wet_blocks, BLK, axis=0), BLK, axis=1)
    land_cells = (column_bits & block_wet).astype(jnp.int32)
    return (owner_table, land_cells)


def draw_owner_map(key, part):
    return band_layout(key)[0]


def draw_land_mask(key, part):
    return band_layout(key)[1]


def draw_phys_fine(key, part):
    sub_keys = jax.random.split(jax.random.fold_in(key, 3), 3)
    cell_shape = (NYF, NXF, NLEV)
    east_flow = jax.random.uniform(sub_keys[0], cell_shape, minval=-0.15, maxval=0.15)
    north_flow = jax.random.uniform(sub_keys[1], cell_shape, minval=-0.15, maxval=0.15)
    warmth = jax.random.uniform(sub_keys[2], cell_shape, minval=-2.0, maxval=30.0)
    return jnp.concatenate([east_flow, north_flow, warmth], axis=2).astype(jnp.bfloat16)


def level_of(key, shape, shards, low, high):
    factor_of, own = 1.0, jax.random.fold_in(key, 6)
    for dim, blocks in shards:
        steps = jnp.exp(jax.random.uniform(jax.random.fold_in(own, dim), (blocks,), jnp.float32, low / len(shards), high / len(shards)))
        factor_of = factor_of * jnp.repeat(steps, shape[dim] // blocks).reshape([-1 if axis == dim else 1 for axis in range(len(shape))])
    return factor_of


def setup_inputs(seed: int = 0) -> dict:
    arg_keys = jax.random.split(jax.random.key(seed), 7)
    tracers = jnp.clip(jnp.exp(math.log(3.0) - 3.4011974 * jax.random.uniform(arg_keys[0], (SLOTS, NTR * NLEV, BLK * BLK), jnp.float32) ** level_of(arg_keys[0], (SLOTS, NTR * NLEV, BLK * BLK), ((0, 32),), -0.2, 0.2)), 0.1, 3.0)
    phys_fine = draw_phys_fine(jax.random.fold_in(arg_keys[6], 71), 0)
    mix_coarse = jnp.clip(jnp.exp(math.log(0.19921875) - 3.6901057 * jax.random.uniform(arg_keys[2], (NYC, NXC, NLEV), jnp.float32) ** level_of(arg_keys[2], (NYC, NXC, NLEV), ((0, 4), (1, 8)), -0.2, 0.2)), 0.0049743652, 0.19921875).astype(jnp.bfloat16)
    surf_light = jnp.clip(jnp.exp(math.log(4.0) - 2.0794415 * jax.random.uniform(arg_keys[3], (NYF, NXF), jnp.float32) ** level_of(arg_keys[3], (NYF, NXF), ((0, 4), (1, 8)), -0.2, 0.2)), 0.5, 4.0)
    land_mask = draw_land_mask(jax.random.fold_in(arg_keys[6], 71), 0)
    owner_map = draw_owner_map(jax.random.fold_in(arg_keys[6], 71), 0)
    return {"tracers": tracers, "phys_fine": phys_fine, "mix_coarse": mix_coarse, "surf_light": surf_light, "land_mask": land_mask, "owner_map": owner_map}


diffuse_rate = 0.08
nano_chl_index = 10
diat_chl_index = 11


def positive(value):
    return jnp.maximum(value, 0.0)


def strict_upper(levels):
    level_ids = jnp.arange(levels)
    return (level_ids[:, None] < level_ids[None, :]).astype(jnp.float32)


def depth_sums(absorb, levels):
    flat_rows = absorb.reshape(-1, levels)
    summed = jnp.dot(flat_rows, strict_upper(levels), precision=lax.Precision.HIGHEST, preferred_element_type=jnp.float32)
    return summed.reshape(absorb.shape)


def coarsen(fine_band, light_fine, levels, factor):
    row_count = fine_band.shape[0] // factor
    col_count = fine_band.shape[1] // factor
    fine_grid = fine_band.reshape(row_count, factor, col_count, factor, 3, levels)
    east_face = jnp.mean(fine_grid[:, :, :, factor - 1, 0, :].astype(jnp.float32), axis=1)
    north_face = jnp.mean(fine_grid[:, factor - 1, :, :, 1, :].astype(jnp.float32), axis=2)
    temp_mean = jnp.mean(fine_grid[:, :, :, :, 2, :].astype(jnp.float32), axis=(1, 3))
    light_mean = jnp.mean(light_fine.reshape(row_count, factor, col_count, factor), axis=(1, 3))
    return east_face, north_face, temp_mean, light_mean


def open_faces(east_face, north_face, wet_cells, wet_north, wet_east):
    open_east = wet_cells * jnp.concatenate([wet_cells[:, 1:], wet_east[:, None]], axis=1)
    open_north = wet_cells * jnp.concatenate([wet_cells[1:], wet_north[None]], axis=0)
    flow_east = east_face * open_east[:, :, None]
    flow_north = north_face * open_north[:, :, None]
    return open_east, open_north, flow_east, flow_north


def back_faces(open_east, open_north, flow_east, flow_north, open_west_col, open_south_row, flow_west_col, flow_south_row):
    open_west = jnp.concatenate([open_west_col[:, None], open_east[:, :-1]], axis=1)
    open_south = jnp.concatenate([open_south_row[None], open_north[:-1]], axis=0)
    flow_west = jnp.concatenate([flow_west_col[:, None], flow_east[:, :-1]], axis=1)
    flow_south = jnp.concatenate([flow_south_row[None], flow_north[:-1]], axis=0)
    return open_west, open_south, flow_west, flow_south


def react(mixed_cells, temp_mean, light_top, levels):
    def tracer_at(tracer_number):
        return mixed_cells[:, :, tracer_number * levels:(tracer_number + 1) * levels]

    carbon_dis = tracer_at(0)
    alkalinity = tracer_at(1)
    oxygen = tracer_at(2)
    nitrate = tracer_at(3)
    ammonium = tracer_at(4)
    phosphate = tracer_at(5)
    silicate = tracer_at(6)
    iron_free = tracer_at(7)
    nano_carbon = tracer_at(8)
    diat_carbon = tracer_at(9)
    nano_chl = tracer_at(10)
    diat_chl = tracer_at(11)
    nano_iron = tracer_at(12)
    diat_iron = tracer_at(13)
    diat_silica = tracer_at(14)
    micro_zoo = tracer_at(15)
    meso_zoo = tracer_at(16)
    dissolved_org = tracer_at(17)
    small_part = tracer_at(18)
    big_part = tracer_at(19)
    small_iron = tracer_at(20)
    big_iron = tracer_at(21)
    big_silica = tracer_at(22)
    calcite = tracer_at(23)
    absorb = 0.04 + 0.02 * (positive(nano_chl) + positive(diat_chl))
    depth_sum = depth_sums(absorb, levels)
    par_light = light_top[:, :, None] * jnp.exp(-(depth_sum + 0.5 * absorb))
    warm_factor = jnp.exp(0.0639 * temp_mean)
    nitrogen = positive(nitrate) + positive(ammonium)
    limit_nitro = nitrogen / (0.5 + nitrogen)
    limit_phos = positive(phosphate) / (0.3 + positive(phosphate))
    limit_iron = positive(iron_free) / (0.2 + positive(iron_free))
    limit_sil = positive(silicate) / (1.0 + positive(silicate))
    nutr_nano = jnp.minimum(jnp.minimum(limit_nitro, limit_phos), limit_iron)
    nutr_diat = jnp.minimum(nutr_nano, limit_sil)
    prod_nano = 0.1 * warm_factor * par_light / (par_light + 0.5) * nutr_nano * nano_carbon
    prod_diat = 0.12 * warm_factor * par_light / (par_light + 1.0) * nutr_diat * diat_carbon
    ammon_share = (positive(ammonium) + 0.01) / (nitrogen + 0.02)
    graze_nano = 0.08 * warm_factor * micro_zoo / (1.0 + positive(nano_carbon))
    graze_diat = 0.06 * warm_factor * meso_zoo / (1.0 + positive(diat_carbon))
    loss_nano = graze_nano + 0.02
    loss_diat = graze_diat + 0.02
    eaten_nano = graze_nano * nano_carbon
    eaten_diat = graze_diat * diat_carbon
    death_micro = 0.03 * micro_zoo * positive(micro_zoo)
    death_meso = 0.03 * meso_zoo * positive(meso_zoo)
    remin_doc = 0.03 * warm_factor * dissolved_org
    remin_poc = 0.02 * warm_factor * small_part
    remin_goc = 0.01 * warm_factor * big_part
    nitrify = 0.05 * ammonium
    melt_si = 0.02 * big_silica
    melt_cal = 0.01 * calcite
    melt_sfe = 0.02 * small_iron
    melt_bfe = 0.01 * big_iron
    uptake = prod_nano + prod_diat
    remin_total = remin_doc + remin_poc + remin_goc
    calcify = 0.02 * prod_nano
    updated = [
        carbon_dis + remin_total - uptake + melt_cal - calcify,
        alkalinity + 2.0 * (melt_cal - calcify) + 0.16 * ((1.0 - ammon_share) * uptake - nitrify),
        oxygen + 1.3 * (uptake - remin_total) - 0.32 * nitrify,
        nitrate + 0.16 * (nitrify - (1.0 - ammon_share) * uptake),
        ammonium + 0.16 * (remin_total - ammon_share * uptake - nitrify),
        phosphate + 0.01 * (remin_total - uptake),
        silicate + melt_si - 0.15 * prod_diat,
        iron_free + melt_sfe + melt_bfe - 0.005 * uptake,
        nano_carbon + prod_nano - loss_nano * nano_carbon,
        diat_carbon + prod_diat - loss_diat * diat_carbon,
        nano_chl + 0.03 * prod_nano - loss_nano * nano_chl,
        diat_chl + 0.03 * prod_diat - loss_diat * diat_chl,
        nano_iron + 0.005 * prod_nano - loss_nano * nano_iron,
        diat_iron + 0.005 * prod_diat - loss_diat * diat_iron,
        diat_silica + 0.15 * prod_diat - loss_diat * diat_silica,
        micro_zoo + 0.3 * eaten_nano - death_micro,
        meso_zoo + 0.3 * eaten_diat - death_meso,
        dissolved_org + 0.3 * eaten_nano + 0.02 * nano_carbon - remin_doc,
        small_part + 0.4 * eaten_nano + death_micro - remin_poc,
        big_part + 0.4 * eaten_diat + 0.02 * diat_carbon + death_meso - remin_goc,
        small_iron + loss_nano * nano_iron - melt_sfe,
        big_iron + loss_diat * diat_iron - melt_bfe,
        big_silica + loss_diat * diat_silica - melt_si,
        calcite + calcify - melt_cal,
    ]
    return jnp.concatenate(updated, axis=2)


def advance(current, halo_sides, physics, cell_flags, levels, tracer_count):
    def widen(level_part):
        return jnp.tile(level_part, (1, 1, tracer_count))

    flow_west = widen(physics[:, :, 0:levels])
    flow_east = widen(physics[:, :, levels:2 * levels])
    flow_south = widen(physics[:, :, 2 * levels:3 * levels])
    flow_north = widen(physics[:, :, 3 * levels:4 * levels])
    temp_mean = physics[:, :, 4 * levels:5 * levels]
    mixing = widen(physics[:, :, 5 * levels:6 * levels])
    south_cell = jnp.concatenate([halo_sides[0][None], current[:-1]], axis=0)
    north_cell = jnp.concatenate([current[1:], halo_sides[1][None]], axis=0)
    west_cell = jnp.concatenate([halo_sides[2][:, None], current[:, :-1]], axis=1)
    east_cell = jnp.concatenate([current[:, 1:], halo_sides[3][:, None]], axis=1)
    flux_east = jnp.maximum(flow_east, 0.0) * current + jnp.minimum(flow_east, 0.0) * east_cell
    flux_west = jnp.maximum(flow_west, 0.0) * west_cell + jnp.minimum(flow_west, 0.0) * current
    flux_north = jnp.maximum(flow_north, 0.0) * current + jnp.minimum(flow_north, 0.0) * north_cell
    flux_south = jnp.maximum(flow_south, 0.0) * south_cell + jnp.minimum(flow_south, 0.0) * current
    spread = diffuse_rate * (cell_flags[:, :, 0:1] * (west_cell - current) + cell_flags[:, :, 1:2] * (east_cell - current) + cell_flags[:, :, 2:3] * (south_cell - current) + cell_flags[:, :, 3:4] * (north_cell - current))
    moved_cells = current - (flux_east - flux_west) - (flux_north - flux_south) + spread
    level_index = jnp.arange(moved_cells.shape[-1]) % levels
    zero_level = jnp.zeros_like(moved_cells[:, :, :1])
    deeper = jnp.concatenate([moved_cells[:, :, 1:], zero_level], axis=2)
    shallower = jnp.concatenate([zero_level, moved_cells[:, :, :-1]], axis=2)
    mixing_upper = jnp.concatenate([zero_level, mixing[:, :, :-1]], axis=2)
    flux_below = jnp.where(level_index < levels - 1, mixing * (deeper - moved_cells), 0.0)
    flux_above = jnp.where(level_index > 0, mixing_upper * (moved_cells - shallower), 0.0)
    mixed_cells = moved_cells + flux_below - flux_above
    reacted = react(mixed_cells, temp_mean, cell_flags[:, :, 4], levels)
    return reacted * cell_flags[:, :, 5:6]


def shortwave(chl_grid, light_fine, wet_cells, levels, factor):
    absorb = 0.04 + 0.02 * chl_grid
    depth_sum = depth_sums(absorb, levels)
    passed = (jnp.exp(-depth_sum) - jnp.exp(-(depth_sum + absorb))) * wet_cells[:, :, None]
    layered = jnp.transpose(passed, (2, 0, 1))
    spread_cells = jnp.repeat(jnp.repeat(layered, factor, axis=1), factor, axis=2)
    return (light_fine[None] * spread_cells).astype(jnp.bfloat16)


def reference(tracers, phys_fine, mix_coarse, surf_light, land_mask, owner_map):
    wet_all = land_mask.astype(jnp.float32)
    fine_rows = CF * BLK
    slot_ids = jnp.arange(WETMAX)
    block_ids = jnp.arange(NBX)

    def band_physics(band_index):
        fine_band = lax.dynamic_slice_in_dim(phys_fine, band_index * fine_rows, fine_rows, 0)
        light_fine = lax.dynamic_slice_in_dim(surf_light, band_index * fine_rows, fine_rows, 0)
        east_face, north_face, temp_mean, light_mean = coarsen(fine_band, light_fine, NLEV, CF)
        mix_mean = lax.dynamic_slice_in_dim(mix_coarse, band_index * BLK, BLK, 0).astype(jnp.float32)
        wet_cells = lax.dynamic_slice_in_dim(wet_all, band_index * BLK, BLK, 0)
        has_north = (band_index < NBY - 1).astype(jnp.float32)
        has_south = (band_index > 0).astype(jnp.float32)
        wet_north = lax.dynamic_index_in_dim(wet_all, jnp.minimum(band_index + 1, NBY - 1) * BLK, 0, keepdims=False) * has_north
        wet_south = lax.dynamic_index_in_dim(wet_all, jnp.maximum(band_index * BLK - 1, 0), 0, keepdims=False) * has_south
        open_east, open_north, flow_east, flow_north = open_faces(east_face, north_face, wet_cells, wet_north, wet_cells[:, 0])
        below_row = lax.dynamic_index_in_dim(phys_fine, jnp.maximum(band_index * fine_rows - 1, 0), 0, keepdims=False)
        north_below = jnp.mean(below_row[:, NLEV:2 * NLEV].reshape(NXC, CF, NLEV).astype(jnp.float32), axis=1)
        open_south_row = wet_south * wet_cells[0]
        open_west_col = wet_cells[:, -1] * wet_cells[:, 0]
        flow_south_row = north_below * open_south_row[:, None]
        open_west, open_south, flow_west, flow_south = back_faces(open_east, open_north, flow_east, flow_north, open_west_col, open_south_row, flow_east[:, -1], flow_south_row)
        physics = jnp.concatenate([flow_west, flow_east, flow_south, flow_north, temp_mean, mix_mean], axis=2)
        cell_flags = jnp.stack([open_west, open_east, open_south, open_north, light_mean, wet_cells], axis=2)
        map_row = lax.dynamic_index_in_dim(owner_map, band_index, 0, keepdims=False)
        slot_codes = band_index * WETMAX + slot_ids
        code_match = map_row[None, :] == slot_codes[:, None]
        block_of = jnp.sum(jnp.where(code_match, block_ids[None, :], 0), axis=1).astype(jnp.int32)
        filled = jnp.any(code_match, axis=1)
        phys_blocks = physics.reshape(BLK, NBX, BLK, 6 * NLEV).transpose(1, 0, 2, 3)
        flag_blocks = cell_flags.reshape(BLK, NBX, BLK, 6).transpose(1, 0, 2, 3)
        slot_phys = jnp.where(filled[:, None, None, None], phys_blocks[block_of], 0.0)
        slot_flags = jnp.where(filled[:, None, None, None], flag_blocks[block_of], 0.0)
        return slot_phys, slot_flags, block_of, filled

    band_phys, band_flags, band_blocks, band_filled = lax.map(band_physics, jnp.arange(NBY))

    def advance_one(items):
        return advance(items[0], items[1], items[2], items[3], NLEV, NTR)

    def band_step(current, items):
        band_index, slot_phys, slot_flags, block_of, filled = items
        own_slots = lax.dynamic_slice_in_dim(current, band_index * WETMAX, WETMAX, 0)
        map_row = lax.dynamic_index_in_dim(owner_map, band_index, 0, keepdims=False)
        south_map = lax.dynamic_index_in_dim(owner_map, jnp.maximum(band_index - 1, 0), 0, keepdims=False)
        north_map = lax.dynamic_index_in_dim(owner_map, jnp.minimum(band_index + 1, NBY - 1), 0, keepdims=False)
        west_slot = map_row[(block_of - 1) % NBX]
        east_slot = map_row[(block_of + 1) % NBX]
        south_slot = jnp.where(band_index > 0, south_map[block_of], -1)
        north_slot = jnp.where(band_index < NBY - 1, north_map[block_of], -1)

        def masked(edge_rows, slot_index):
            return jnp.where((slot_index >= 0)[:, None, None], edge_rows, 0.0)

        halo_south = masked(current[jnp.maximum(south_slot, 0), BLK - 1], south_slot)
        halo_north = masked(current[jnp.maximum(north_slot, 0), 0], north_slot)
        halo_west = masked(current[jnp.maximum(west_slot, 0), :, BLK - 1], west_slot)
        halo_east = masked(current[jnp.maximum(east_slot, 0), :, 0], east_slot)
        halo_sides = jnp.stack([halo_south, halo_north, halo_west, halo_east], axis=1)
        updated = lax.map(advance_one, (own_slots, halo_sides, slot_phys, slot_flags))
        return jnp.where(filled[:, None, None, None], updated, 0.0)

    current = tracers.reshape(SLOTS, NTR * NLEV, BLK, BLK).transpose(0, 2, 3, 1)
    for step_index in range(ITERS):
        stepped = lax.map(partial(band_step, current), (jnp.arange(NBY), band_phys, band_flags, band_blocks, band_filled))
        current = stepped.reshape(SLOTS, BLK, BLK, NTR * NLEV)

    chl_slots = positive(current[..., nano_chl_index * NLEV:(nano_chl_index + 1) * NLEV]) + positive(current[..., diat_chl_index * NLEV:(diat_chl_index + 1) * NLEV])

    def band_heat(band_index):
        map_row = lax.dynamic_index_in_dim(owner_map, band_index, 0, keepdims=False)
        block_chl = jnp.where((map_row >= 0)[:, None, None, None], chl_slots[jnp.maximum(map_row, 0)], 0.0)
        chl_grid = block_chl.transpose(1, 0, 2, 3).reshape(BLK, NXC, NLEV)
        wet_cells = lax.dynamic_slice_in_dim(wet_all, band_index * BLK, BLK, 0)
        light_fine = lax.dynamic_slice_in_dim(surf_light, band_index * fine_rows, fine_rows, 0)
        return shortwave(chl_grid, light_fine, wet_cells, NLEV, CF)

    heat_bands = lax.map(band_heat, jnp.arange(NBY))
    heating = heat_bands.transpose(1, 0, 2, 3).reshape(NLEV, NYF, NXF)
    tracers_out = current.transpose(0, 3, 1, 2).reshape(SLOTS, NTR * NLEV, BLK * BLK)
    return tracers_out, heating
```

```python
import functools

import jax
import jax.numpy as jnp
from jax import lax
from jax.experimental import pallas as pl
from jax.experimental.pallas import tpu as pltpu
from jax.sharding import PartitionSpec as P

ITERS = 2
LANES = 128
SUB = 8

diffuse_rate = 0.08
nano_chl_index = 10
diat_chl_index = 11

SLOT_TILE, SLOT_FULL, SLOT_WEST, SLOT_EAST, TILE_OWNER, TILE_WET, TILE_BASE = range(7)
TABLE_ROWS = 8

OPEN_EAST, OPEN_NORTH, OPEN_WEST, OPEN_SOUTH, LIGHT, WET = range(6)

VMEM_LIMIT = 48 * 1024 * 1024


def positive(value):
    return jnp.maximum(value, 0.0)


def lane_ids(rows=SUB):
    return lax.broadcasted_iota(jnp.int32, (rows, LANES), 1)


def turned(value, by):
    by = by % LANES
    return value if by == 0 else pltpu.roll(value, by, 1)


def along(axis, by, closed):
    size = lax.axis_size(axis)
    pairs = [(i, (i + by) % size) for i in range(size)]
    return [p for p in pairs if closed or p[1] == p[0] + by]


def table_kernel(slot_count, tile_blocks, lon_count, row_ref, out_ref, used_ref):
    me = lax.axis_index("lon")
    block_count = row_ref.shape[1]
    width = out_ref.shape[1]

    def clear(i, carry):
        for r in range(TABLE_ROWS):
            out_ref[r, i] = 0
        return carry

    lax.fori_loop(0, width, clear, 0)

    def unuse(i, carry):
        used_ref[0, i] = 0
        used_ref[1, i] = 0
        return carry

    lax.fori_loop(0, lon_count, unuse, 0)
    out_ref[TILE_BASE, 0] = me * tile_blocks

    def visit(k, carry):
        code = row_ref[0, k]
        safe = jnp.maximum(code, 0)
        owner = lax.rem(lax.div(safe, slot_count), lon_count)
        slot = lax.rem(safe, slot_count)
        tile = lax.div(k, tile_blocks)

        @pl.when((code >= 0) & (owner == me))
        def _():
            west = row_ref[0, lax.rem(k + block_count - 1, block_count)]
            east = row_ref[0, lax.rem(k + 1, block_count)]
            out_ref[SLOT_TILE, slot] = tile
            out_ref[SLOT_FULL, slot] = 1
            out_ref[SLOT_WEST, slot] = lax.rem(jnp.maximum(west, 0), slot_count)
            out_ref[SLOT_EAST, slot] = lax.rem(jnp.maximum(east, 0), slot_count)
            used_ref[0, tile] = 1

        @pl.when((code >= 0) & (tile == me))
        def _():
            local = lax.rem(k, tile_blocks)
            out_ref[TILE_OWNER, local] = owner
            out_ref[TILE_WET, local] = 1
            used_ref[1, owner] = 1

        return carry

    lax.fori_loop(0, block_count, visit, 0)

    def give(target, filled, line, count):
        def one(i, carry):
            def look(j, done):
                take = (done == 0) & (used_ref[line, j] == 0)

                @pl.when(take)
                def _():
                    out_ref[target, i] = j
                    used_ref[line, j] = 1

                return jnp.where(take, 1, done)

            lax.fori_loop(0, lon_count, look, out_ref[filled, i])
            return carry

        lax.fori_loop(0, count, one, 0)

    give(SLOT_TILE, SLOT_FULL, 0, slot_count)
    give(TILE_OWNER, TILE_WET, 1, tile_blocks)


def routing(row, slot_count, tile_blocks):
    lon_count = lax.axis_size("lon")
    width = max(slot_count, tile_blocks, lon_count)
    return pl.pallas_call(
        functools.partial(table_kernel, slot_count, tile_blocks, lon_count),
        out_shape=jax.ShapeDtypeStruct((TABLE_ROWS, width), jnp.int32),
        in_specs=[pl.BlockSpec(memory_space=pltpu.SMEM)],
        out_specs=pl.BlockSpec(memory_space=pltpu.SMEM),
        scratch_shapes=[pltpu.SMEM((2, lon_count), jnp.int32)],
        name="routing",
    )(row)


def pack_row(cells, group, side, start):
    ids = lane_ids() >> (side.bit_length() - 1)
    packed = None
    for g in range(group):
        piece = turned(cells[g], side * g - start)
        packed = piece if packed is None else jnp.where(ids == g, piece, packed)
    return packed


def pack_col(cells, group, side, start, offset, base):
    ids = lane_ids() & (side - 1)
    packed = base
    for g in range(group):
        piece = turned(cells[g], offset + g - start)
        packed = piece if packed is None else jnp.where(ids == offset + g, piece, packed)
    return packed


def edges_kernel(levels, side, table_ref, cell_ref, south_ref, north_ref, west_ref, east_ref):
    group = LANES // side
    halves = cell_ref.shape[2] // LANES
    rounds = cell_ref.shape[1] // levels // group
    level_tiles = levels // SUB

    def body(lt, carry):
        for i in range(rounds):
            row = pl.multiple_of(i * levels + lt * SUB, SUB)
            west = east = None
            for h in range(halves):
                cells = []
                for g in range(group):
                    at = pl.multiple_of((i * group + g) * levels + lt * SUB, SUB)
                    cells.append(cell_ref[0, pl.ds(at, SUB), h * LANES : (h + 1) * LANES])
                west = pack_col(cells, group, side, 0, h * group, west)
                east = pack_col(cells, group, side, side - 1, h * group, east)
                if h == 0:
                    south_ref[0, pl.ds(row, SUB), :] = pack_row(cells, group, side, 0)
                if h == halves - 1:
                    north_ref[0, pl.ds(row, SUB), :] = pack_row(cells, group, side, LANES - side)
            west_ref[0, pl.ds(row, SUB), :] = west
            east_ref[0, pl.ds(row, SUB), :] = east
        return carry

    lax.fori_loop(0, level_tiles, body, 0)


def edge_shapes(slot_count, lon_count, rows):
    f32 = jnp.float32
    shapes = [
        jax.ShapeDtypeStruct((lon_count, rows, LANES), f32),
        jax.ShapeDtypeStruct((lon_count, rows, LANES), f32),
        jax.ShapeDtypeStruct((slot_count, rows, LANES), f32),
        jax.ShapeDtypeStruct((slot_count, rows, LANES), f32),
    ]
    by_tile = pl.BlockSpec((1, rows, LANES), lambda s, t: (t[SLOT_TILE, s], 0, 0))
    by_slot = pl.BlockSpec((1, rows, LANES), lambda s, t: (s, 0, 0))
    return shapes, [by_tile, by_tile, by_slot, by_slot]


def first_edges(table, tracers, levels, side):
    slot_count, channels, cell_count = tracers.shape
    lon_count = lax.axis_size("lon")
    rows = channels * side // LANES
    shapes, specs = edge_shapes(slot_count, lon_count, rows)
    return pl.pallas_call(
        functools.partial(edges_kernel, levels, side),
        out_shape=shapes,
        grid_spec=pltpu.PrefetchScalarGridSpec(
            num_scalar_prefetch=1,
            grid=(slot_count,),
            in_specs=[pl.BlockSpec((1, channels, cell_count), lambda s, t: (s, 0, 0))],
            out_specs=specs,
        ),
        compiler_params=pltpu.CompilerParams(vmem_limit_bytes=VMEM_LIMIT),
        name="first_edges",
    )(table, tracers)


def react(mixed, par_light, warm_factor):
    (
        carbon_dis,
        alkalinity,
        oxygen,
        nitrate,
        ammonium,
        phosphate,
        silicate,
        iron_free,
        nano_carbon,
        diat_carbon,
        nano_chl,
        diat_chl,
        nano_iron,
        diat_iron,
        diat_silica,
        micro_zoo,
        meso_zoo,
        dissolved_org,
        small_part,
        big_part,
        small_iron,
        big_iron,
        big_silica,
        calcite,
    ) = mixed
    nitrogen = positive(nitrate) + positive(ammonium)
    limit_nitro = nitrogen / (0.5 + nitrogen)
    limit_phos = positive(phosphate) / (0.3 + positive(phosphate))
    limit_iron = positive(iron_free) / (0.2 + positive(iron_free))
    limit_sil = positive(silicate) / (1.0 + positive(silicate))
    nutr_nano = jnp.minimum(jnp.minimum(limit_nitro, limit_phos), limit_iron)
    nutr_diat = jnp.minimum(nutr_nano, limit_sil)
    lit = warm_factor * par_light
    prod_nano = 0.1 * lit / (par_light + 0.5) * nutr_nano * nano_carbon
    prod_diat = 0.12 * lit / (par_light + 1.0) * nutr_diat * diat_carbon
    ammon_share = (positive(ammonium) + 0.01) / (nitrogen + 0.02)
    graze_nano = 0.08 * warm_factor * micro_zoo / (1.0 + positive(nano_carbon))
    graze_diat = 0.06 * warm_factor * meso_zoo / (1.0 + positive(diat_carbon))
    loss_nano = graze_nano + 0.02
    loss_diat = graze_diat + 0.02
    eaten_nano = graze_nano * nano_carbon
    eaten_diat = graze_diat * diat_carbon
    death_micro = 0.03 * micro_zoo * positive(micro_zoo)
    death_meso = 0.03 * meso_zoo * positive(meso_zoo)
    remin_doc = 0.03 * warm_factor * dissolved_org
    remin_poc = 0.02 * warm_factor * small_part
    remin_goc = 0.01 * warm_factor * big_part
    nitrify = 0.05 * ammonium
    melt_si = 0.02 * big_silica
    melt_cal = 0.01 * calcite
    melt_sfe = 0.02 * small_iron
    melt_bfe = 0.01 * big_iron
    uptake = prod_nano + prod_diat
    remin_total = remin_doc + remin_poc + remin_goc
    calcify = 0.02 * prod_nano
    gained = remin_total - uptake
    shell = melt_cal - calcify
    by_ammon = ammon_share * uptake
    by_nitrate = 0.16 * (uptake - by_ammon - nitrify)
    return [
        carbon_dis + gained + shell,
        alkalinity + 2.0 * shell + by_nitrate,
        oxygen - 1.3 * gained - 0.32 * nitrify,
        nitrate - by_nitrate,
        ammonium + 0.16 * (remin_total - by_ammon - nitrify),
        phosphate + 0.01 * gained,
        silicate + melt_si - 0.15 * prod_diat,
        iron_free + melt_sfe + melt_bfe - 0.005 * uptake,
        nano_carbon + prod_nano - loss_nano * nano_carbon,
        diat_carbon + prod_diat - loss_diat * diat_carbon,
        nano_chl + 0.03 * prod_nano - loss_nano * nano_chl,
        diat_chl + 0.03 * prod_diat - loss_diat * diat_chl,
        nano_iron + 0.005 * prod_nano - loss_nano * nano_iron,
        diat_iron + 0.005 * prod_diat - loss_diat * diat_iron,
        diat_silica + 0.15 * prod_diat - loss_diat * diat_silica,
        micro_zoo + 0.3 * eaten_nano - death_micro,
        meso_zoo + 0.3 * eaten_diat - death_meso,
        dissolved_org + 0.3 * eaten_nano + 0.02 * nano_carbon - remin_doc,
        small_part + 0.4 * eaten_nano + death_micro - remin_poc,
        big_part + 0.4 * eaten_diat + 0.02 * diat_carbon + death_meso - remin_goc,
        small_iron + loss_nano * nano_iron - melt_sfe,
        big_iron + loss_diat * diat_iron - melt_bfe,
        big_silica + loss_diat * diat_silica - melt_si,
        calcite + calcify - melt_cal,
    ]


def step_kernel(levels, side, last, table_ref, cell_ref, phys_ref, rim_ref, rim_w_ref, rim_e_ref, *refs):
    if last:
        out_ref, chl_ref, coef_ref, moved_ref = refs
        edge_refs = ()
    else:
        out_ref, south_ref, north_ref, west_ref, east_ref, coef_ref, moved_ref = refs
        edge_refs = (south_ref, north_ref, west_ref, east_ref)
    channels, cell_count = cell_ref.shape[1:]
    tracer_count = channels // levels
    group = LANES // side
    halves = cell_count // LANES
    rounds = tracer_count // group
    level_tiles = levels // SUB
    rows = rounds * levels
    slot = pl.program_id(0)
    full = table_ref[SLOT_FULL, slot] == 1
    spans = [slice(h * LANES, (h + 1) * LANES) for h in range(halves)]

    @pl.when(jnp.logical_not(full))
    def _():
        out_ref[...] = jnp.zeros_like(out_ref)
        for ref in edge_refs:
            ref[...] = jnp.zeros_like(ref)
        if last:
            chl_ref[...] = jnp.zeros_like(chl_ref)

    @pl.when(full)
    def _():
        lane = lane_ids()
        sub = lax.broadcasted_iota(jnp.int32, (SUB, LANES), 0)
        col = lane & (side - 1)
        first_col = col == 0
        last_col = col == side - 1
        first_row = lane < side
        last_row = lane >= LANES - side
        flag_row = 4 * levels
        pack_at = flag_row + SUB

        def flag(f, h):
            return phys_ref[0, flag_row + f : flag_row + f + 1, spans[h]]

        def southward(values, edge):
            out = []
            for h in range(halves):
                before = edge if h == 0 else turned(values[h - 1], side)
                out.append(jnp.where(first_row, before, turned(values[h], side)))
            return out

        def northward(values, edge):
            out = []
            for h in range(halves):
                after = edge if h == halves - 1 else turned(values[h + 1], -side)
                out.append(jnp.where(last_row, after, turned(values[h], -side)))
            return out

        above_mix = [jnp.zeros((SUB, LANES), jnp.float32)] * halves
        west_pack = phys_ref[0, pack_at : pack_at + SUB, spans[0]]
        south_pack = phys_ref[0, pack_at : pack_at + SUB, spans[1]]
        for lt in range(level_tiles):
            at = slice(lt * SUB, (lt + 1) * SUB)
            east_face = [phys_ref[0, lt * SUB : (lt + 1) * SUB, spans[h]] for h in range(halves)]
            north_face = [
                phys_ref[0, levels + lt * SUB : levels + (lt + 1) * SUB, spans[h]] for h in range(halves)
            ]
            south_face = southward(north_face, turned(south_pack, -side * lt))
            for h in range(halves):
                open_e, open_n, open_w, open_s = (flag(f, h) for f in range(4))
                west_face = jnp.where(
                    first_col, turned(west_pack, -(h * group + lt)), turned(east_face[h], 1)
                )
                flow_e = east_face[h] * open_e
                flow_n = north_face[h] * open_n
                flow_w = west_face * open_w
                flow_s = south_face[h] * open_s
                out_e, in_e = jnp.maximum(flow_e, 0.0), jnp.minimum(flow_e, 0.0)
                out_n, in_n = jnp.maximum(flow_n, 0.0), jnp.minimum(flow_n, 0.0)
                in_w, out_w = jnp.maximum(flow_w, 0.0), jnp.minimum(flow_w, 0.0)
                in_s, out_s = jnp.maximum(flow_s, 0.0), jnp.minimum(flow_s, 0.0)
                drift = diffuse_rate * (open_w + open_e + open_s + open_n)
                coef_ref[0, at, spans[h]] = 1.0 - (out_e - out_w) - (out_n - out_s) - drift
                coef_ref[1, at, spans[h]] = diffuse_rate * open_e - in_e
                coef_ref[2, at, spans[h]] = diffuse_rate * open_w + in_w
                coef_ref[3, at, spans[h]] = diffuse_rate * open_n - in_n
                coef_ref[4, at, spans[h]] = diffuse_rate * open_s + in_s
                mix = phys_ref[0, 3 * levels + lt * SUB : 3 * levels + (lt + 1) * SUB, spans[h]]
                mix_up = pltpu.roll(jnp.where(sub == SUB - 1, above_mix[h], mix), 1, 0)
                above_mix[h] = mix
                if lt == level_tiles - 1:
                    mix = jnp.where(sub == SUB - 1, 0.0, mix)
                coef_ref[5, at, spans[h]] = 1.0 - mix - mix_up
                coef_ref[6, at, spans[h]] = mix
                coef_ref[7, at, spans[h]] = mix_up

        blank = jnp.zeros((SUB, cell_count), jnp.float32)
        moved_ref[0:SUB, :] = blank
        moved_ref[SUB + channels : 2 * SUB + channels, :] = blank

        def advect(lt, carry):
            at = pl.multiple_of(lt * SUB, SUB)
            coef = [[coef_ref[n, pl.ds(at, SUB), spans[h]] for n in range(5)] for h in range(halves)]
            for i in range(rounds):
                row = pl.multiple_of(i * levels + lt * SUB, SUB)
                rim_s = rim_ref[0, pl.ds(row, SUB), :]
                rim_n = rim_ref[0, pl.ds(pl.multiple_of(rows + row, SUB), SUB), :]
                rim_w = rim_w_ref[0, pl.ds(row, SUB), :]
                rim_e = rim_e_ref[0, pl.ds(row, SUB), :]
                for g in range(group):
                    chan = pl.multiple_of((i * group + g) * levels + lt * SUB, SUB)
                    here = [cell_ref[0, pl.ds(chan, SUB), spans[h]] for h in range(halves)]
                    south = southward(here, turned(rim_s, -side * g))
                    north = northward(here, turned(rim_n, LANES - side - side * g))
                    for h in range(halves):
                        at_w = h * group + g
                        west = jnp.where(first_col, turned(rim_w, -at_w), turned(here[h], 1))
                        east = jnp.where(last_col, turned(rim_e, side - 1 - at_w), turned(here[h], -1))
                        c, e, w, n, s = coef[h]
                        moved_ref[pl.ds(pl.multiple_of(SUB + chan, SUB), SUB), spans[h]] = (
                            c * here[h] + (e * east + w * west) + (n * north[h] + s * south[h])
                        )
            return carry

        lax.fori_loop(0, level_tiles, advect, 0)

        def reacting(lt, carry):
            at = pl.multiple_of(lt * SUB, SUB)
            depths = []
            for h in range(halves):
                mix_c, mix_d, mix_u = (coef_ref[n, pl.ds(at, SUB), spans[h]] for n in (5, 6, 7))
                mixed = []
                for t in range(tracer_count):
                    base = t * levels + lt * SUB
                    before = moved_ref[pl.ds(pl.multiple_of(base, SUB), SUB), spans[h]]
                    now = moved_ref[pl.ds(pl.multiple_of(base + SUB, SUB), SUB), spans[h]]
                    after = moved_ref[pl.ds(pl.multiple_of(base + 2 * SUB, SUB), SUB), spans[h]]
                    up = pltpu.roll(jnp.where(sub == SUB - 1, before, now), 1, 0)
                    down = pltpu.roll(jnp.where(sub == 0, after, now), SUB - 1, 0)
                    mixed.append(mix_c * now + mix_d * down + mix_u * up)
                absorb = 0.04 + 0.02 * (
                    positive(mixed[nano_chl_index]) + positive(mixed[diat_chl_index])
                )
                total = absorb
                for by in (1, 2, 4):
                    total = total + jnp.where(sub >= by, pltpu.roll(total, by, 0), 0.0)
                above = carry[h] + (total - absorb)
                depths.append(carry[h] + total[SUB - 1 : SUB, :])
                light = flag(LIGHT, h)
                wet = flag(WET, h)
                par_light = light * jnp.exp(-(above + 0.5 * absorb))
                warm = phys_ref[0, pl.ds(pl.multiple_of(2 * levels + lt * SUB, SUB), SUB), spans[h]]
                new = [value * wet for value in react(mixed, par_light, warm)]
                for t in range(tracer_count):
                    out_ref[0, pl.ds(pl.multiple_of(t * levels + lt * SUB, SUB), SUB), spans[h]] = new[t]
                if last:
                    chl_ref[0, pl.ds(at, SUB), spans[h]] = positive(new[nano_chl_index]) + positive(
                        new[diat_chl_index]
                    )
                else:
                    for i in range(rounds):
                        row = pl.multiple_of(i * levels + lt * SUB, SUB)
                        cells = new[i * group : (i + 1) * group]
                        west = None if h == 0 else west_ref[0, pl.ds(row, SUB), :]
                        east = None if h == 0 else east_ref[0, pl.ds(row, SUB), :]
                        west_ref[0, pl.ds(row, SUB), :] = pack_col(cells, group, side, 0, h * group, west)
                        east_ref[0, pl.ds(row, SUB), :] = pack_col(
                            cells, group, side, side - 1, h * group, east
                        )
                        if h == 0:
                            south_ref[0, pl.ds(row, SUB), :] = pack_row(cells, group, side, 0)
                        if h == halves - 1:
                            north_ref[0, pl.ds(row, SUB), :] = pack_row(cells, group, side, LANES - side)
            return tuple(depths)

        start = tuple(jnp.zeros((1, LANES), jnp.float32) for _ in range(halves))
        lax.fori_loop(0, level_tiles, reacting, start)


def step(table, cells, phys, rims, rim_w, rim_e, levels, side, last):
    slot_count, channels, cell_count = cells.shape
    lon_count = lax.axis_size("lon")
    rows = channels * side // LANES
    phys_rows = phys.shape[1]
    f32 = jnp.float32
    by_slot = pl.BlockSpec((1, channels, cell_count), lambda s, t: (s, 0, 0))
    shapes = [jax.ShapeDtypeStruct(cells.shape, f32)]
    specs = [by_slot]
    if last:
        shapes.append(jax.ShapeDtypeStruct((lon_count, levels, cell_count), f32))
        specs.append(pl.BlockSpec((1, levels, cell_count), lambda s, t: (t[SLOT_TILE, s], 0, 0)))
    else:
        more_shapes, more_specs = edge_shapes(slot_count, lon_count, rows)
        shapes += more_shapes
        specs += more_specs
    return pl.pallas_call(
        functools.partial(step_kernel, levels, side, last),
        out_shape=shapes,
        grid_spec=pltpu.PrefetchScalarGridSpec(
            num_scalar_prefetch=1,
            grid=(slot_count,),
            in_specs=[
                by_slot,
                pl.BlockSpec((1, phys_rows, cell_count), lambda s, t: (t[SLOT_TILE, s], 0, 0)),
                pl.BlockSpec((1, 2 * rows, LANES), lambda s, t: (t[SLOT_TILE, s], 0, 0)),
                pl.BlockSpec((1, rows, LANES), lambda s, t: (t[SLOT_WEST, s], 0, 0)),
                pl.BlockSpec((1, rows, LANES), lambda s, t: (t[SLOT_EAST, s], 0, 0)),
            ],
            out_specs=specs,
            scratch_shapes=[
                pltpu.VMEM((8, levels, cell_count), f32),
                pltpu.VMEM((channels + 2 * SUB, cell_count), f32),
            ],
        ),
        compiler_params=pltpu.CompilerParams(vmem_limit_bytes=VMEM_LIMIT),
        name="step",
    )(table, cells, phys, rims, rim_w, rim_e)


def coarsen_kernel(
    levels,
    side,
    factor,
    table_ref,
    fine_ref,
    mix_ref,
    light_ref,
    land_ref,
    south_ref,
    north_ref,
    west_ref,
    east_ref,
    pick_ref,
    out_ref,
    rows_ref,
):
    row = pl.program_id(0)
    row_count = pl.num_programs(0)
    tile_blocks = land_ref.shape[1] // side
    halves = side * side // LANES
    group = LANES // side
    fine_cols = light_ref.shape[1]
    f32 = jnp.float32
    picks = pick_ref[...]

    east_face = jnp.zeros((levels, LANES), f32)
    temp_mean = jnp.zeros((levels, LANES), f32)
    for r in range(factor):
        got = jnp.dot(fine_ref[r], picks, preferred_element_type=f32)
        east_face += got[0:levels, 0:LANES]
        temp_mean += got[2 * levels : 3 * levels, LANES : 2 * LANES]
        if r == factor - 1:
            north_face = got[levels : 2 * levels, LANES : 2 * LANES]
    rows_ref[row, 0:levels, :] = east_face * (1.0 / factor)
    rows_ref[row, levels : 2 * levels, :] = north_face * (1.0 / factor)
    rows_ref[row, 2 * levels : 3 * levels, :] = jnp.exp(0.0639 * (temp_mean * (1.0 / (factor * factor))))
    rows_ref[row, 3 * levels : 4 * levels, :] = mix_ref[0].astype(f32)

    @pl.when(row == row_count - 1)
    def _():
        lane = lane_ids()
        group_id = lane >> (side.bit_length() - 1)
        col_id = lane & (side - 1)
        flag_row = 4 * levels
        pack_at = flag_row + SUB
        wet = land_ref[...].astype(f32)
        sides = wet.shape
        lane2 = lax.broadcasted_iota(jnp.int32, sides, 1)
        sub2 = lax.broadcasted_iota(jnp.int32, sides, 0)
        diagonal = lane2 == sub2
        rim_w = jnp.sum(jnp.where(diagonal, west_ref[SUB : SUB + 1, :], 0.0), axis=1, keepdims=True)
        rim_e = jnp.sum(jnp.where(diagonal, east_ref[0:1, :], 0.0), axis=1, keepdims=True)
        wet_w = jnp.where(lane2 == 0, rim_w, pltpu.roll(wet, 1, 1))
        wet_e = jnp.where(lane2 == LANES - 1, rim_e, pltpu.roll(wet, LANES - 1, 1))
        wet_s = jnp.where(sub2 == 0, south_ref[levels : levels + 1, 0:LANES], pltpu.roll(wet, 1, 0))
        wet_n = jnp.where(sub2 == side - 1, north_ref[0:1, 0:LANES], pltpu.roll(wet, side - 1, 0))
        fold_r = lax.broadcasted_iota(jnp.int32, (side, side * factor), 0)
        fold_c = lax.broadcasted_iota(jnp.int32, (side, side * factor), 1)
        fold_d = fold_c - factor * fold_r
        fold = jnp.where((fold_d >= 0) & (fold_d < factor), 1.0, 0.0)
        narrow = picks[:, LANES : 2 * LANES].astype(f32)
        light_rows = jnp.dot(fold, light_ref[...], precision=lax.Precision.HIGHEST, preferred_element_type=f32)
        light_mean = jnp.dot(
            light_rows, narrow, precision=lax.Precision.HIGHEST, preferred_element_type=f32
        ) * (1.0 / (factor * factor))
        flags = [wet * wet_e, wet * wet_n, wet * wet_w, wet * wet_s, light_mean, wet]
        for r in range(side):
            for f, value in enumerate(flags):
                rows_ref[r, flag_row + f : flag_row + f + 1, :] = value[r : r + 1, :]
            rows_ref[r, flag_row + len(flags) : flag_row + SUB, :] = jnp.zeros((SUB - len(flags), LANES), f32)

        def place(q, carry):
            at = pl.multiple_of(q * SUB, SUB)
            for h in range(halves):
                values = [rows_ref[h * group + r, pl.ds(at, SUB), :] for r in range(group)]
                for b in range(tile_blocks):
                    block = None
                    for r in range(group):
                        piece = turned(values[r], side * (r - b))
                        block = piece if block is None else jnp.where(group_id == r, piece, block)
                    owner = table_ref[TILE_OWNER, b]
                    out_ref[owner, pl.ds(at, SUB), h * LANES : (h + 1) * LANES] = block
            return carry

        lax.fori_loop(0, pack_at // SUB, place, 0)

        fine_v = south_ref[0:levels, 0:fine_cols].astype(jnp.bfloat16)
        north_below = jnp.dot(fine_v, picks, preferred_element_type=f32)[:, LANES : 2 * LANES] * (1.0 / factor)
        for b in range(tile_blocks):
            owner = table_ref[TILE_OWNER, b]
            south_pack = jnp.zeros((SUB, LANES), f32)
            for lt in range(levels // SUB):
                piece = turned(north_below[lt * SUB : (lt + 1) * SUB, :], side * (lt - b))
                south_pack = jnp.where(group_id == lt, piece, south_pack)
            if b == 0:
                west_pack = west_ref[0:SUB, :]
            else:
                beside = table_ref[TILE_OWNER, b - 1]
                west_pack = jnp.zeros((SUB, LANES), f32)
                for h in range(halves):
                    for lt in range(levels // SUB):
                        face = out_ref[beside, lt * SUB : (lt + 1) * SUB, h * LANES : (h + 1) * LANES]
                        piece = turned(face, h * group + lt - (side - 1))
                        west_pack = jnp.where(col_id == h * group + lt, piece, west_pack)
            out_ref[owner, pack_at : pack_at + SUB, 0:LANES] = west_pack
            out_ref[owner, pack_at : pack_at + SUB, LANES : 2 * LANES] = south_pack


def coarsen(table, fine, mix, light, land, from_south, from_north, from_west, from_east, picks):
    lon_count = lax.axis_size("lon")
    side, tile_cols = land.shape
    levels = mix.shape[1]
    factor = fine.shape[0] // side
    fine_cols = fine.shape[2]
    phys_rows = 4 * levels + 2 * SUB
    f32 = jnp.float32

    def whole(x):
        return pl.BlockSpec(x.shape, lambda i, t: (0,) * x.ndim)

    return pl.pallas_call(
        functools.partial(coarsen_kernel, levels, side, factor),
        out_shape=jax.ShapeDtypeStruct((lon_count, phys_rows, side * side), f32),
        grid_spec=pltpu.PrefetchScalarGridSpec(
            num_scalar_prefetch=1,
            grid=(side,),
            in_specs=[
                pl.BlockSpec((factor, 3 * levels, fine_cols), lambda i, t: (i, 0, 0)),
                pl.BlockSpec((1, levels, tile_cols), lambda i, t: (i, 0, 0)),
                whole(light),
                whole(land),
                whole(from_south),
                whole(from_north),
                whole(from_west),
                whole(from_east),
                whole(picks),
            ],
            out_specs=pl.BlockSpec((lon_count, phys_rows, side * side), lambda i, t: (0, 0, 0)),
            scratch_shapes=[pltpu.VMEM((side, 4 * levels + SUB, LANES), f32)],
        ),
        compiler_params=pltpu.CompilerParams(vmem_limit_bytes=VMEM_LIMIT),
        name="coarsen",
    )(table, fine, mix, light, land, from_south, from_north, from_west, from_east, picks)


def owner_of(codes, block, slot_count, lon_count):
    return lax.rem(lax.div(jnp.maximum(codes[0, block], 0), slot_count), lon_count)


def hand_kernel(table_ref, below_ref, above_ref, south_ref, north_ref, out_ref):
    b = pl.program_id(0)
    rows = south_ref.shape[1]
    block = table_ref[TILE_BASE, 0] + b
    out_ref[0, 0:rows, :] = jnp.where(below_ref[0, block] >= 0, south_ref[0], 0.0)
    out_ref[0, rows : 2 * rows, :] = jnp.where(above_ref[0, block] >= 0, north_ref[0], 0.0)


def hand_on(table, codes_below, codes_above, from_south, from_north, slot_count, tile_blocks):
    lon_count, rows, width = from_south.shape

    def spot(t, b):
        return t[TILE_BASE, 0] + b

    return pl.pallas_call(
        hand_kernel,
        out_shape=jax.ShapeDtypeStruct((lon_count, 2 * rows, width), jnp.float32),
        grid_spec=pltpu.PrefetchScalarGridSpec(
            num_scalar_prefetch=3,
            grid=(tile_blocks,),
            in_specs=[
                pl.BlockSpec(
                    (1, rows, width),
                    lambda b, t, lo, hi: (owner_of(lo, spot(t, b), slot_count, lon_count), 0, 0),
                ),
                pl.BlockSpec(
                    (1, rows, width),
                    lambda b, t, lo, hi: (owner_of(hi, spot(t, b), slot_count, lon_count), 0, 0),
                ),
            ],
            out_specs=pl.BlockSpec((1, 2 * rows, width), lambda b, t, lo, hi: (t[TILE_OWNER, b], 0, 0)),
        ),
        compiler_params=pltpu.CompilerParams(vmem_limit_bytes=VMEM_LIMIT),
        name="hand_on",
    )(table, codes_below, codes_above, from_south, from_north)


def heat_kernel(levels, side, factor, table_ref, chl_ref, light_ref, land_ref, widen_ref, out_ref, rows_ref, wide_ref):
    tile_blocks = land_ref.shape[1] // side
    halves = side * side // LANES
    group = LANES // side
    fine_cols = light_ref.shape[1]
    fine_rows = light_ref.shape[0]
    f32 = jnp.float32
    group_id = lane_ids() >> (side.bit_length() - 1)

    def place(lt, carry):
        at = pl.multiple_of(lt * SUB, SUB)
        for h in range(halves):
            blocks = []
            for b in range(tile_blocks):
                owner = table_ref[TILE_OWNER, b]
                values = chl_ref[owner, pl.ds(at, SUB), h * LANES : (h + 1) * LANES]
                blocks.append(jnp.where(table_ref[TILE_WET, b] == 1, values, 0.0))
            for r in range(group):
                line = None
                for b in range(tile_blocks):
                    piece = turned(blocks[b], side * (b - r))
                    line = piece if line is None else jnp.where(group_id == b, piece, line)
                rows_ref[pl.ds(pl.multiple_of((h * group + r) * levels + lt * SUB, SUB), SUB), :] = line
        return carry

    lax.fori_loop(0, levels // SUB, place, 0)
    wet = land_ref[...].astype(f32)
    widen = widen_ref[...]
    above = jnp.zeros_like(wet)
    passing = jnp.ones_like(wet)
    for l in range(levels):
        chl = rows_ref[pl.ds(l, side, stride=levels), :]
        above = above + (0.04 + 0.02 * chl)
        through = jnp.exp(-above)
        kept = (passing - through) * wet
        passing = through
        high = kept.astype(jnp.bfloat16)
        low = (kept - high.astype(f32)).astype(jnp.bfloat16)
        wide_ref[l * side : (l + 1) * side, :] = jnp.dot(
            high, widen, preferred_element_type=f32
        ) + jnp.dot(low, widen, preferred_element_type=f32)

    sub = lax.broadcasted_iota(jnp.int32, (SUB, LANES), 0)
    sources = []
    for m in range(fine_rows // SUB):
        start = (m * SUB // factor) // SUB * SUB
        index = jnp.zeros_like(sub)
        for r in range(1, side):
            index = index + jnp.where(sub + m * SUB >= r * factor, 1, 0)
        sources.append((start, index - start))

    def spread(l, carry):
        for c in range(fine_cols // LANES):
            span = slice(c * LANES, (c + 1) * LANES)
            for m in range(0, fine_rows // SUB, 2):
                both = []
                for n in (m, m + 1):
                    start, index = sources[n]
                    lines = wide_ref[pl.ds(pl.multiple_of(l * side + start, SUB), SUB), span]
                    lines = jnp.take_along_axis(lines, index, axis=0)
                    both.append(lines * light_ref[n * SUB : (n + 1) * SUB, span])
                out_ref[l, m * SUB : (m + 2) * SUB, span] = jnp.concatenate(both, axis=0).astype(jnp.bfloat16)
        return carry

    lax.fori_loop(0, levels, spread, 0)


def heat(table, chl, light, land, levels, widen):
    side = land.shape[0]
    factor = light.shape[0] // side
    vmem = pl.BlockSpec(memory_space=pltpu.VMEM)
    return pl.pallas_call(
        functools.partial(heat_kernel, levels, side, factor),
        out_shape=jax.ShapeDtypeStruct((levels,) + light.shape, jnp.bfloat16),
        in_specs=[pl.BlockSpec(memory_space=pltpu.SMEM), vmem, vmem, vmem, vmem],
        out_specs=vmem,
        scratch_shapes=[
            pltpu.VMEM((side * levels, LANES), jnp.float32),
            pltpu.VMEM((side * levels, light.shape[1]), jnp.float32),
        ],
        compiler_params=pltpu.CompilerParams(vmem_limit_bytes=VMEM_LIMIT),
        name="heat",
    )(table, chl, light, land, widen)


def widened(x, rows, width):
    return jnp.pad(x, ((0, rows - x.shape[0]), (0, width - x.shape[1])))


def on_device(tracers, phys_fine, mix_coarse, surf_light, land_mask, owner_map):
    f32 = jnp.float32
    slot_count = tracers.shape[0]
    side = land_mask.shape[0]
    levels = mix_coarse.shape[2]
    tile_blocks = land_mask.shape[1] // side
    factor = phys_fine.shape[0] // side
    fine_cols = phys_fine.shape[1]
    block_count = owner_map.shape[1]
    group = LANES // side

    fine = jnp.transpose(phys_fine, (0, 2, 1))
    mix = jnp.transpose(mix_coarse, (0, 2, 1))
    wet = land_mask.astype(f32)
    codes = owner_map.astype(f32) + 1.0
    width = max(fine_cols, block_count)

    northward = jnp.concatenate(
        [
            widened(fine[-1, levels : 2 * levels, :].astype(f32), levels, width),
            widened(wet[-1:], 1, width),
            widened(codes, 1, width),
        ],
        axis=0,
    )
    southward = jnp.concatenate([widened(wet[:1], 1, width), widened(codes, 1, width)], axis=0)
    last_face = jnp.mean(
        fine[:, :levels, fine_cols - 1].astype(f32).reshape(side, factor, levels), axis=1
    )
    face_pack = jnp.pad(
        last_face.reshape(side // group, group, levels // SUB, SUB).transpose(3, 1, 0, 2),
        ((0, 0), (0, 0), (0, 0), (0, group - levels // SUB)),
    ).reshape(SUB, LANES)
    eastward = jnp.concatenate([face_pack, widened(wet[:, -1][None], 1, LANES)], axis=0)
    westward = widened(wet[:, 0][None], 1, LANES)

    from_south = lax.ppermute(northward, "lat", along("lat", 1, False))
    from_north = lax.ppermute(southward, "lat", along("lat", -1, False))
    from_west = lax.ppermute(eastward, "lon", along("lon", 1, True))
    from_east = lax.ppermute(westward, "lon", along("lon", -1, True))
    codes_below = from_south[levels + 1 :, :block_count].astype(jnp.int32) - 1
    codes_above = from_north[1:, :block_count].astype(jnp.int32) - 1

    fine_id = jnp.arange(fine_cols)[:, None]
    coarse_id = jnp.arange(land_mask.shape[1])[None, :]
    member = (fine_id // factor == coarse_id).astype(jnp.bfloat16)
    final = (fine_id == factor * coarse_id + factor - 1).astype(jnp.bfloat16)
    picks = jnp.concatenate([final, member], axis=1)

    table = routing(owner_map, slot_count, tile_blocks)
    south, north, west, east = first_edges(table, tracers, levels, side)
    phys = coarsen(
        table, fine, mix, surf_light, land_mask, from_south, from_north, from_west, from_east, picks
    )
    phys = lax.all_to_all(phys, "lon", 0, 0, tiled=True)

    current = tracers
    for step_index in range(ITERS):
        rim_w = lax.ppermute(east, "lon", along("lon", 1, True))
        rim_e = lax.ppermute(west, "lon", along("lon", -1, True))
        rim_s = lax.ppermute(north, "lat", along("lat", 1, False))
        rim_n = lax.ppermute(south, "lat", along("lat", -1, False))
        rim_s = lax.all_to_all(rim_s, "lon", 0, 0, tiled=True)
        rim_n = lax.all_to_all(rim_n, "lon", 0, 0, tiled=True)
        rims = hand_on(table, codes_below, codes_above, rim_s, rim_n, slot_count, tile_blocks)
        rims = lax.all_to_all(rims, "lon", 0, 0, tiled=True)
        last = step_index == ITERS - 1
        got = step(table, current, phys, rims, rim_w, rim_e, levels, side, last)
        if last:
            current, chl = got
        else:
            current, south, north, west, east = got
    chl = lax.all_to_all(chl, "lon", 0, 0, tiled=True)
    heating = heat(table, chl, surf_light, land_mask, levels, jnp.transpose(member))
    return current, heating


def solution(mesh):
    in_specs = (
        P(("lat", "lon"), None, None),
        P("lat", "lon", None),
        P("lat", "lon", None),
        P("lat", "lon"),
        P("lat", "lon"),
        P("lat", None),
    )
    out_specs = (P(("lat", "lon"), None, None), P(None, "lat", "lon"))
    return jax.shard_map(
        on_device, mesh=mesh, in_specs=in_specs, out_specs=out_specs, check_vma=False
    )
```

```python
import functools

import jax
import jax.numpy as jnp
from jax import lax
from jax.experimental import pallas as pl
from jax.experimental.pallas import tpu as pltpu
from jax.sharding import PartitionSpec as P

ITERS = 2
LANES = 128
SUB = 8

diffuse_rate = 0.08
nano_chl_index = 10
diat_chl_index = 11

SLOT_TILE, SLOT_FULL, SLOT_WEST, SLOT_EAST, TILE_OWNER, TILE_WET, TILE_BASE = range(7)
TABLE_ROWS = 8

OPEN_EAST, OPEN_NORTH, OPEN_WEST, OPEN_SOUTH, LIGHT, WET = range(6)

VMEM_LIMIT = 48 * 1024 * 1024


def positive(value):
    return jnp.maximum(value, 0.0)


def lane_ids(rows=SUB):
    return lax.broadcasted_iota(jnp.int32, (rows, LANES), 1)


def turned(value, by):
    by = by % LANES
    return value if by == 0 else pltpu.roll(value, by, 1)


def quotient(value, by):
    if by & (by - 1) == 0:
        return lax.shift_right_logical(value, jnp.int32(by.bit_length() - 1))
    return lax.div(value, jnp.int32(by))


def remainder(value, by):
    if by & (by - 1) == 0:
        return value & (by - 1)
    return lax.rem(value, jnp.int32(by))


def along(axis, by, closed):
    size = lax.axis_size(axis)
    pairs = [(i, (i + by) % size) for i in range(size)]
    return [p for p in pairs if closed or p[1] == p[0] + by]


def table_kernel(slot_count, tile_blocks, lon_count, row_ref, out_ref, used_ref):
    me = lax.axis_index("lon")
    block_count = row_ref.shape[1]
    width = out_ref.shape[1]

    def clear(i, carry):
        for r in range(TABLE_ROWS):
            out_ref[r, i] = 0
        return carry

    lax.fori_loop(0, width, clear, 0)

    def unuse(i, carry):
        used_ref[0, i] = 0
        used_ref[1, i] = 0
        return carry

    lax.fori_loop(0, lon_count, unuse, 0)
    out_ref[TILE_BASE, 0] = me * tile_blocks

    def visit(k, carry):
        code = row_ref[0, k]
        safe = jnp.maximum(code, 0)
        owner = remainder(quotient(safe, slot_count), lon_count)
        slot = remainder(safe, slot_count)
        tile = quotient(k, tile_blocks)

        @pl.when((code >= 0) & (owner == me))
        def _():
            west = row_ref[0, remainder(k + block_count - 1, block_count)]
            east = row_ref[0, remainder(k + 1, block_count)]
            out_ref[SLOT_TILE, slot] = tile
            out_ref[SLOT_FULL, slot] = 1
            out_ref[SLOT_WEST, slot] = remainder(jnp.maximum(west, 0), slot_count)
            out_ref[SLOT_EAST, slot] = remainder(jnp.maximum(east, 0), slot_count)
            used_ref[0, tile] = 1

        @pl.when((code >= 0) & (tile == me))
        def _():
            local = remainder(k, tile_blocks)
            out_ref[TILE_OWNER, local] = owner
            out_ref[TILE_WET, local] = 1
            used_ref[1, owner] = 1

        return carry

    lax.fori_loop(0, block_count, visit, 0, unroll=4)

    def give(target, filled, line, count):
        def one(i, carry):
            def look(j, done):
                take = (done == 0) & (used_ref[line, j] == 0)

                @pl.when(take)
                def _():
                    out_ref[target, i] = j
                    used_ref[line, j] = 1

                return jnp.where(take, 1, done)

            @pl.when(out_ref[filled, i] == 0)
            def _():
                lax.fori_loop(0, lon_count, look, 0)

            return carry

        lax.fori_loop(0, count, one, 0)

    give(SLOT_TILE, SLOT_FULL, 0, slot_count)
    give(TILE_OWNER, TILE_WET, 1, tile_blocks)


def routing(row, slot_count, tile_blocks):
    lon_count = lax.axis_size("lon")
    width = max(slot_count, tile_blocks, lon_count)
    return pl.pallas_call(
        functools.partial(table_kernel, slot_count, tile_blocks, lon_count),
        out_shape=jax.ShapeDtypeStruct((TABLE_ROWS, width), jnp.int32),
        in_specs=[pl.BlockSpec(memory_space=pltpu.SMEM)],
        out_specs=pl.BlockSpec(memory_space=pltpu.SMEM),
        scratch_shapes=[pltpu.SMEM((2, lon_count), jnp.int32)],
        name="routing",
    )(row)


def merged(pieces, ids):
    packed = pieces[0]
    for g in range(1, len(pieces)):
        packed = jnp.where(ids == g, pieces[g], packed)
    return packed


def pack_columns(first, second, side):
    lane = lane_ids()
    odd = (lane & 1) == 1
    here = (lane & (side - 1)) >> 1
    there = ((lane + 1) & (side - 1)) >> 1
    even_ends = merged([turned(v, 1 + 2 * g) for g, v in enumerate(first)], here)
    odd_ends = merged([turned(v, 2 * g) for g, v in enumerate(second)], there)
    return jnp.where(odd, even_ends, odd_ends), jnp.where(odd, odd_ends, even_ends)


def pack_rows(first, second, side):
    lane = lane_ids()
    low = lane < LANES // 2
    lead = (lane & side) == 0
    here = lane >> side.bit_length()
    there = ((lane + side) & (LANES - 1)) >> side.bit_length()
    count = LANES // (2 * side)
    both = [jnp.where(low, a, b) for a, b in zip(first, second)]
    early = merged([turned(both[g], side + 2 * side * g) for g in range(count)], here)
    late = merged([turned(both[count + g], 2 * side * g) for g in range(count)], there)
    return jnp.where(lead, late, early), jnp.where(lead, early, late)


def edges_kernel(levels, side, table_ref, cell_ref, *refs):
    rows_ref, west_ref, east_ref = refs[-3:]
    group = LANES // side
    rounds = cell_ref.shape[1] // levels // group
    level_tiles = levels // SUB
    rows = rounds * levels

    def body(lt, carry):
        for i in range(rounds):
            row = pl.multiple_of(i * levels + lt * SUB, SUB)
            first, second = [], []
            for g in range(group):
                at = pl.multiple_of((i * group + g) * levels + lt * SUB, SUB)
                first.append(cell_ref[0, pl.ds(at, SUB), 0:LANES])
                second.append(cell_ref[0, pl.ds(at, SUB), LANES : 2 * LANES])
            west, east = pack_columns(first, second, side)
            south, north = pack_rows(first, second, side)
            west_ref[0, pl.ds(row, SUB), :] = west
            east_ref[0, pl.ds(row, SUB), :] = east
            rows_ref[0, pl.ds(row, SUB), :] = south
            rows_ref[0, pl.ds(pl.multiple_of(rows + row, SUB), SUB), :] = north
        return carry

    lax.fori_loop(0, level_tiles, body, 0, unroll=True)


def edge_shapes(slot_count, lon_count, rows):
    f32 = jnp.float32
    shapes = [
        jax.ShapeDtypeStruct((lon_count, 2 * rows, LANES), f32),
        jax.ShapeDtypeStruct((slot_count, rows, LANES), f32),
        jax.ShapeDtypeStruct((slot_count, rows, LANES), f32),
    ]
    by_tile = pl.BlockSpec((1, 2 * rows, LANES), lambda s, t: (t[SLOT_TILE, s], 0, 0))
    by_slot = pl.BlockSpec((1, rows, LANES), lambda s, t: (s, 0, 0))
    return shapes, [by_tile, by_slot, by_slot]


def first_edges(table, tracers, levels, side, *after):
    slot_count, channels, cell_count = tracers.shape
    lon_count = lax.axis_size("lon")
    rows = channels * side // LANES
    shapes, specs = edge_shapes(slot_count, lon_count, rows)
    return pl.pallas_call(
        functools.partial(edges_kernel, levels, side),
        out_shape=shapes,
        grid_spec=pltpu.PrefetchScalarGridSpec(
            num_scalar_prefetch=1,
            grid=(slot_count,),
            in_specs=[pl.BlockSpec((1, channels, cell_count), lambda s, t: (s, 0, 0))]
            + [pl.BlockSpec(memory_space=pl.ANY)] * len(after),
            out_specs=specs,
        ),
        compiler_params=pltpu.CompilerParams(vmem_limit_bytes=VMEM_LIMIT),
        name="first_edges",
    )(table, tracers, *after)


def react(mixed, par_light, warm_factor):
    (
        carbon_dis,
        alkalinity,
        oxygen,
        nitrate,
        ammonium,
        phosphate,
        silicate,
        iron_free,
        nano_carbon,
        diat_carbon,
        nano_chl,
        diat_chl,
        nano_iron,
        diat_iron,
        diat_silica,
        micro_zoo,
        meso_zoo,
        dissolved_org,
        small_part,
        big_part,
        small_iron,
        big_iron,
        big_silica,
        calcite,
    ) = mixed
    nitrogen = positive(nitrate) + positive(ammonium)
    limit_nitro = nitrogen / (0.5 + nitrogen)
    limit_phos = positive(phosphate) / (0.3 + positive(phosphate))
    limit_iron = positive(iron_free) / (0.2 + positive(iron_free))
    limit_sil = positive(silicate) / (1.0 + positive(silicate))
    nutr_nano = jnp.minimum(jnp.minimum(limit_nitro, limit_phos), limit_iron)
    nutr_diat = jnp.minimum(nutr_nano, limit_sil)
    lit = warm_factor * par_light
    prod_nano = 0.1 * lit / (par_light + 0.5) * nutr_nano * nano_carbon
    prod_diat = 0.12 * lit / (par_light + 1.0) * nutr_diat * diat_carbon
    ammon_share = (positive(ammonium) + 0.01) / (nitrogen + 0.02)
    graze_nano = 0.08 * warm_factor * micro_zoo / (1.0 + positive(nano_carbon))
    graze_diat = 0.06 * warm_factor * meso_zoo / (1.0 + positive(diat_carbon))
    loss_nano = graze_nano + 0.02
    loss_diat = graze_diat + 0.02
    eaten_nano = graze_nano * nano_carbon
    eaten_diat = graze_diat * diat_carbon
    death_micro = 0.03 * micro_zoo * positive(micro_zoo)
    death_meso = 0.03 * meso_zoo * positive(meso_zoo)
    remin_doc = 0.03 * warm_factor * dissolved_org
    remin_poc = 0.02 * warm_factor * small_part
    remin_goc = 0.01 * warm_factor * big_part
    nitrify = 0.05 * ammonium
    melt_si = 0.02 * big_silica
    melt_cal = 0.01 * calcite
    melt_sfe = 0.02 * small_iron
    melt_bfe = 0.01 * big_iron
    uptake = prod_nano + prod_diat
    remin_total = remin_doc + remin_poc + remin_goc
    calcify = 0.02 * prod_nano
    gained = remin_total - uptake
    shell = melt_cal - calcify
    by_ammon = ammon_share * uptake
    by_nitrate = 0.16 * (uptake - by_ammon - nitrify)
    return [
        carbon_dis + gained + shell,
        alkalinity + 2.0 * shell + by_nitrate,
        oxygen - 1.3 * gained - 0.32 * nitrify,
        nitrate - by_nitrate,
        ammonium + 0.16 * (remin_total - by_ammon - nitrify),
        phosphate + 0.01 * gained,
        silicate + melt_si - 0.15 * prod_diat,
        iron_free + melt_sfe + melt_bfe - 0.005 * uptake,
        nano_carbon + prod_nano - loss_nano * nano_carbon,
        diat_carbon + prod_diat - loss_diat * diat_carbon,
        nano_chl + 0.03 * prod_nano - loss_nano * nano_chl,
        diat_chl + 0.03 * prod_diat - loss_diat * diat_chl,
        nano_iron + 0.005 * prod_nano - loss_nano * nano_iron,
        diat_iron + 0.005 * prod_diat - loss_diat * diat_iron,
        diat_silica + 0.15 * prod_diat - loss_diat * diat_silica,
        micro_zoo + 0.3 * eaten_nano - death_micro,
        meso_zoo + 0.3 * eaten_diat - death_meso,
        dissolved_org + 0.3 * eaten_nano + 0.02 * nano_carbon - remin_doc,
        small_part + 0.4 * eaten_nano + death_micro - remin_poc,
        big_part + 0.4 * eaten_diat + 0.02 * diat_carbon + death_meso - remin_goc,
        small_iron + loss_nano * nano_iron - melt_sfe,
        big_iron + loss_diat * diat_iron - melt_bfe,
        big_silica + loss_diat * diat_silica - melt_si,
        calcite + calcify - melt_cal,
    ]


def step_kernel(levels, side, last, table_ref, cell_ref, phys_ref, rim_ref, rim_w_ref, rim_e_ref, *refs):
    if last:
        out_ref, chl_ref, coef_ref, moved_ref, ends_ref = refs
        edge_refs = ()
    else:
        out_ref, rows_ref, west_ref, east_ref, coef_ref, moved_ref, ends_ref = refs
        edge_refs = (rows_ref, west_ref, east_ref)
    channels, cell_count = cell_ref.shape[1:]
    tracer_count = channels // levels
    group = LANES // side
    halves = cell_count // LANES
    rounds = tracer_count // group
    level_tiles = levels // SUB
    rows = rounds * levels
    slot = pl.program_id(0)
    full = table_ref[SLOT_FULL, slot] == 1
    spans = [slice(h * LANES, (h + 1) * LANES) for h in range(halves)]

    @pl.when(jnp.logical_not(full))
    def _():
        out_ref[...] = jnp.zeros_like(out_ref)
        for ref in edge_refs:
            ref[...] = jnp.zeros_like(ref)
        if last:
            chl_ref[...] = jnp.zeros_like(chl_ref)

    @pl.when(full)
    def _():
        lane = lane_ids()
        sub = lax.broadcasted_iota(jnp.int32, (SUB, LANES), 0)
        col = lane & (side - 1)
        first_col = col == 0
        last_col = col == side - 1
        first_row = lane < side
        last_row = lane >= LANES - side
        flag_row = 4 * levels
        pack_at = flag_row + SUB

        def flag(f, h):
            return phys_ref[0, flag_row + f : flag_row + f + 1, spans[h]]

        def southward(values, edge):
            out = []
            for h in range(halves):
                before = edge if h == 0 else turned(values[h - 1], side)
                out.append(jnp.where(first_row, before, turned(values[h], side)))
            return out

        def northward(values, edge):
            out = []
            for h in range(halves):
                after = edge if h == halves - 1 else turned(values[h + 1], -side)
                out.append(jnp.where(last_row, after, turned(values[h], -side)))
            return out

        above_mix = [jnp.zeros((SUB, LANES), jnp.float32)] * halves
        west_pack = phys_ref[0, pack_at : pack_at + SUB, spans[0]]
        south_pack = phys_ref[0, pack_at : pack_at + SUB, spans[1]]
        for lt in range(level_tiles):
            at = slice(lt * SUB, (lt + 1) * SUB)
            east_face = [phys_ref[0, lt * SUB : (lt + 1) * SUB, spans[h]] for h in range(halves)]
            north_face = [
                phys_ref[0, levels + lt * SUB : levels + (lt + 1) * SUB, spans[h]] for h in range(halves)
            ]
            south_face = southward(north_face, turned(south_pack, -side * lt))
            for h in range(halves):
                open_e, open_n, open_w, open_s = (flag(f, h) for f in range(4))
                west_face = jnp.where(
                    first_col, turned(west_pack, -(h * group + lt)), turned(east_face[h], 1)
                )
                flow_e = east_face[h] * open_e
                flow_n = north_face[h] * open_n
                flow_w = west_face * open_w
                flow_s = south_face[h] * open_s
                out_e, in_e = jnp.maximum(flow_e, 0.0), jnp.minimum(flow_e, 0.0)
                out_n, in_n = jnp.maximum(flow_n, 0.0), jnp.minimum(flow_n, 0.0)
                in_w, out_w = jnp.maximum(flow_w, 0.0), jnp.minimum(flow_w, 0.0)
                in_s, out_s = jnp.maximum(flow_s, 0.0), jnp.minimum(flow_s, 0.0)
                drift = diffuse_rate * (open_w + open_e + open_s + open_n)
                coef_ref[0, at, spans[h]] = 1.0 - (out_e - out_w) - (out_n - out_s) - drift
                coef_ref[1, at, spans[h]] = diffuse_rate * open_e - in_e
                coef_ref[2, at, spans[h]] = diffuse_rate * open_w + in_w
                coef_ref[3, at, spans[h]] = diffuse_rate * open_n - in_n
                coef_ref[4, at, spans[h]] = diffuse_rate * open_s + in_s
                mix = phys_ref[0, 3 * levels + lt * SUB : 3 * levels + (lt + 1) * SUB, spans[h]]
                mix_up = pltpu.roll(jnp.where(sub == SUB - 1, above_mix[h], mix), 1, 0)
                above_mix[h] = mix
                if lt == level_tiles - 1:
                    mix = jnp.where(sub == SUB - 1, 0.0, mix)
                coef_ref[5, at, spans[h]] = 1.0 - mix - mix_up
                coef_ref[6, at, spans[h]] = mix
                coef_ref[7, at, spans[h]] = mix_up

        odd = (lane & 1) == 1
        for at in range(0, rows, SUB):
            ends_ref[at : at + SUB, :] = turned(rim_w_ref[0, at : at + SUB, :], 2 - 2 * side)

        blank = jnp.zeros((SUB, cell_count), jnp.float32)
        moved_ref[0:SUB, :] = blank
        moved_ref[SUB + channels : 2 * SUB + channels, :] = blank

        def advect(lt, carry):
            at = pl.multiple_of(lt * SUB, SUB)
            coef = [[coef_ref[n, pl.ds(at, SUB), spans[h]] for n in range(5)] for h in range(halves)]
            for i in range(rounds):
                row = pl.multiple_of(i * levels + lt * SUB, SUB)
                rims = [
                    rim_ref[0, pl.ds(row, SUB), :],
                    rim_ref[0, pl.ds(pl.multiple_of(rows + row, SUB), SUB), :],
                ]
                ends_w = ends_ref[pl.ds(row, SUB), :]
                ends_e = rim_e_ref[0, pl.ds(row, SUB), :]
                sides = [jnp.where(odd, ends_e, ends_w), jnp.where(odd, ends_w, ends_e)]
                for g in range(group):
                    chan = pl.multiple_of((i * group + g) * levels + lt * SUB, SUB)
                    here = [cell_ref[0, pl.ds(chan, SUB), spans[h]] for h in range(halves)]
                    rim = turned(rims[2 * g // group], -side - 2 * side * (g % (group // 2)))
                    south = southward(here, rim)
                    north = northward(here, rim)
                    for h in range(halves):
                        ends = turned(sides[h], side - 2 + h - 2 * g)
                        west = jnp.where(first_col, ends, turned(here[h], 1))
                        east = jnp.where(last_col, ends, turned(here[h], -1))
                        c, e, w, n, s = coef[h]
                        moved_ref[pl.ds(pl.multiple_of(SUB + chan, SUB), SUB), spans[h]] = (
                            c * here[h] + (e * east + w * west) + (n * north[h] + s * south[h])
                        )
            return carry

        lax.fori_loop(0, level_tiles, advect, 0, unroll=True)

        def reacting(lt, carry):
            at = pl.multiple_of(lt * SUB, SUB)
            depths = []
            halves_new = []
            for h in range(halves):
                mix_c, mix_d, mix_u = (coef_ref[n, pl.ds(at, SUB), spans[h]] for n in (5, 6, 7))
                mixed = []
                for t in range(tracer_count):
                    base = t * levels + lt * SUB
                    before = moved_ref[pl.ds(pl.multiple_of(base, SUB), SUB), spans[h]]
                    now = moved_ref[pl.ds(pl.multiple_of(base + SUB, SUB), SUB), spans[h]]
                    after = moved_ref[pl.ds(pl.multiple_of(base + 2 * SUB, SUB), SUB), spans[h]]
                    up = pltpu.roll(jnp.where(sub == SUB - 1, before, now), 1, 0)
                    down = pltpu.roll(jnp.where(sub == 0, after, now), SUB - 1, 0)
                    mixed.append(mix_c * now + mix_d * down + mix_u * up)
                absorb = 0.04 + 0.02 * (
                    positive(mixed[nano_chl_index]) + positive(mixed[diat_chl_index])
                )
                total = absorb
                for by in (1, 2, 4):
                    total = total + jnp.where(sub >= by, pltpu.roll(total, by, 0), 0.0)
                above = carry[h] + (total - absorb)
                depths.append(carry[h] + total[SUB - 1 : SUB, :])
                light = flag(LIGHT, h)
                wet = flag(WET, h)
                par_light = light * jnp.exp(-(above + 0.5 * absorb))
                warm = phys_ref[0, pl.ds(pl.multiple_of(2 * levels + lt * SUB, SUB), SUB), spans[h]]
                new = [value * wet for value in react(mixed, par_light, warm)]
                for t in range(tracer_count):
                    out_ref[0, pl.ds(pl.multiple_of(t * levels + lt * SUB, SUB), SUB), spans[h]] = new[t]
                if last:
                    chl_ref[0, pl.ds(at, SUB), spans[h]] = positive(new[nano_chl_index]) + positive(
                        new[diat_chl_index]
                    )
                halves_new.append(new)
            if not last:
                for i in range(rounds):
                    row = pl.multiple_of(i * levels + lt * SUB, SUB)
                    first, second = (new[i * group : (i + 1) * group] for new in halves_new)
                    west, east = pack_columns(first, second, side)
                    south, north = pack_rows(first, second, side)
                    west_ref[0, pl.ds(row, SUB), :] = west
                    east_ref[0, pl.ds(row, SUB), :] = east
                    rows_ref[0, pl.ds(row, SUB), :] = south
                    rows_ref[0, pl.ds(pl.multiple_of(rows + row, SUB), SUB), :] = north
            return tuple(depths)

        start = tuple(jnp.zeros((1, LANES), jnp.float32) for _ in range(halves))
        lax.fori_loop(0, level_tiles, reacting, start, unroll=True)


def step(table, cells, phys, rims, rim_w, rim_e, levels, side, last):
    slot_count, channels, cell_count = cells.shape
    lon_count = lax.axis_size("lon")
    rows = channels * side // LANES
    phys_rows = phys.shape[1]
    f32 = jnp.float32
    by_slot = pl.BlockSpec((1, channels, cell_count), lambda s, t: (s, 0, 0))
    shapes = [jax.ShapeDtypeStruct(cells.shape, f32)]
    specs = [by_slot]
    if last:
        shapes.append(jax.ShapeDtypeStruct((lon_count, levels, cell_count), f32))
        specs.append(pl.BlockSpec((1, levels, cell_count), lambda s, t: (t[SLOT_TILE, s], 0, 0)))
    else:
        more_shapes, more_specs = edge_shapes(slot_count, lon_count, rows)
        shapes += more_shapes
        specs += more_specs
    return pl.pallas_call(
        functools.partial(step_kernel, levels, side, last),
        out_shape=shapes,
        grid_spec=pltpu.PrefetchScalarGridSpec(
            num_scalar_prefetch=1,
            grid=(slot_count,),
            in_specs=[
                by_slot,
                pl.BlockSpec((1, phys_rows, cell_count), lambda s, t: (t[SLOT_TILE, s], 0, 0)),
                pl.BlockSpec((1, 2 * rows, LANES), lambda s, t: (t[SLOT_TILE, s], 0, 0)),
                pl.BlockSpec((1, rows, LANES), lambda s, t: (t[SLOT_WEST, s], 0, 0)),
                pl.BlockSpec((1, rows, LANES), lambda s, t: (t[SLOT_EAST, s], 0, 0)),
            ],
            out_specs=specs,
            scratch_shapes=[
                pltpu.VMEM((8, levels, cell_count), f32),
                pltpu.VMEM((channels + 2 * SUB, cell_count), f32),
                pltpu.VMEM((rows, LANES), f32),
            ],
        ),
        compiler_params=pltpu.CompilerParams(vmem_limit_bytes=VMEM_LIMIT),
        name="step",
    )(table, cells, phys, rims, rim_w, rim_e)


def coarsen_kernel(
    levels,
    side,
    factor,
    table_ref,
    fine_ref,
    mix_ref,
    light_ref,
    land_ref,
    south_ref,
    north_ref,
    west_ref,
    east_ref,
    pick_ref,
    out_ref,
    rows_ref,
):
    row = pl.program_id(0)
    row_count = pl.num_programs(0)
    tile_blocks = land_ref.shape[1] // side
    halves = side * side // LANES
    group = LANES // side
    fine_cols = light_ref.shape[1]
    f32 = jnp.float32
    picks = pick_ref[...]

    east_face = jnp.zeros((levels, LANES), f32)
    temp_mean = jnp.zeros((levels, LANES), f32)
    for r in range(factor):
        got = jnp.dot(fine_ref[r], picks, preferred_element_type=f32)
        east_face += got[0:levels, 0:LANES]
        temp_mean += got[2 * levels : 3 * levels, LANES : 2 * LANES]
        if r == factor - 1:
            north_face = got[levels : 2 * levels, LANES : 2 * LANES]
    rows_ref[row, 0:levels, :] = east_face * (1.0 / factor)
    rows_ref[row, levels : 2 * levels, :] = north_face * (1.0 / factor)
    rows_ref[row, 2 * levels : 3 * levels, :] = jnp.exp(0.0639 * (temp_mean * (1.0 / (factor * factor))))
    rows_ref[row, 3 * levels : 4 * levels, :] = mix_ref[0].astype(f32)

    @pl.when(row == row_count - 1)
    def _():
        lane = lane_ids()
        group_id = lane >> (side.bit_length() - 1)
        col_id = lane & (side - 1)
        flag_row = 4 * levels
        pack_at = flag_row + SUB
        wet = land_ref[...].astype(f32)
        sides = wet.shape
        lane2 = lax.broadcasted_iota(jnp.int32, sides, 1)
        sub2 = lax.broadcasted_iota(jnp.int32, sides, 0)
        diagonal = lane2 == sub2
        rim_w = jnp.sum(jnp.where(diagonal, west_ref[SUB : SUB + 1, :], 0.0), axis=1, keepdims=True)
        rim_e = jnp.sum(jnp.where(diagonal, east_ref[0:1, :], 0.0), axis=1, keepdims=True)
        wet_w = jnp.where(lane2 == 0, rim_w, pltpu.roll(wet, 1, 1))
        wet_e = jnp.where(lane2 == LANES - 1, rim_e, pltpu.roll(wet, LANES - 1, 1))
        wet_s = jnp.where(sub2 == 0, south_ref[levels : levels + 1, 0:LANES], pltpu.roll(wet, 1, 0))
        wet_n = jnp.where(sub2 == side - 1, north_ref[0:1, 0:LANES], pltpu.roll(wet, side - 1, 0))
        fold_r = lax.broadcasted_iota(jnp.int32, (side, side * factor), 0)
        fold_c = lax.broadcasted_iota(jnp.int32, (side, side * factor), 1)
        fold_d = fold_c - factor * fold_r
        fold = jnp.where((fold_d >= 0) & (fold_d < factor), 1.0, 0.0)
        narrow = picks[:, LANES : 2 * LANES].astype(f32)
        light_rows = jnp.dot(fold, light_ref[...], precision=lax.Precision.HIGHEST, preferred_element_type=f32)
        light_mean = jnp.dot(
            light_rows, narrow, precision=lax.Precision.HIGHEST, preferred_element_type=f32
        ) * (1.0 / (factor * factor))
        flags = [wet * wet_e, wet * wet_n, wet * wet_w, wet * wet_s, light_mean, wet]
        for r in range(side):
            for f, value in enumerate(flags):
                rows_ref[r, flag_row + f : flag_row + f + 1, :] = value[r : r + 1, :]
            rows_ref[r, flag_row + len(flags) : flag_row + SUB, :] = jnp.zeros((SUB - len(flags), LANES), f32)

        def place(q, carry):
            at = pl.multiple_of(q * SUB, SUB)
            for h in range(halves):
                values = [rows_ref[h * group + r, pl.ds(at, SUB), :] for r in range(group)]
                for b in range(tile_blocks):
                    block = None
                    for r in range(group):
                        piece = turned(values[r], side * (r - b))
                        block = piece if block is None else jnp.where(group_id == r, piece, block)
                    owner = table_ref[TILE_OWNER, b]
                    out_ref[owner, pl.ds(at, SUB), h * LANES : (h + 1) * LANES] = block
            return carry

        lax.fori_loop(0, pack_at // SUB, place, 0)

        fine_v = south_ref[0:levels, 0:fine_cols].astype(jnp.bfloat16)
        north_below = jnp.dot(fine_v, picks, preferred_element_type=f32)[:, LANES : 2 * LANES] * (1.0 / factor)
        for b in range(tile_blocks):
            owner = table_ref[TILE_OWNER, b]
            south_pack = jnp.zeros((SUB, LANES), f32)
            for lt in range(levels // SUB):
                piece = turned(north_below[lt * SUB : (lt + 1) * SUB, :], side * (lt - b))
                south_pack = jnp.where(group_id == lt, piece, south_pack)
            if b == 0:
                west_pack = west_ref[0:SUB, :]
            else:
                beside = table_ref[TILE_OWNER, b - 1]
                west_pack = jnp.zeros((SUB, LANES), f32)
                for h in range(halves):
                    for lt in range(levels // SUB):
                        face = out_ref[beside, lt * SUB : (lt + 1) * SUB, h * LANES : (h + 1) * LANES]
                        piece = turned(face, h * group + lt - (side - 1))
                        west_pack = jnp.where(col_id == h * group + lt, piece, west_pack)
            out_ref[owner, pack_at : pack_at + SUB, 0:LANES] = west_pack
            out_ref[owner, pack_at : pack_at + SUB, LANES : 2 * LANES] = south_pack


def coarsen(table, fine, mix, light, land, from_south, from_north, from_west, from_east, picks):
    lon_count = lax.axis_size("lon")
    side, tile_cols = land.shape
    levels = mix.shape[1]
    factor = fine.shape[0] // side
    fine_cols = fine.shape[2]
    phys_rows = 4 * levels + 2 * SUB
    f32 = jnp.float32

    def whole(x):
        return pl.BlockSpec(x.shape, lambda i, t: (0,) * x.ndim)

    return pl.pallas_call(
        functools.partial(coarsen_kernel, levels, side, factor),
        out_shape=jax.ShapeDtypeStruct((lon_count, phys_rows, side * side), f32),
        grid_spec=pltpu.PrefetchScalarGridSpec(
            num_scalar_prefetch=1,
            grid=(side,),
            in_specs=[
                pl.BlockSpec((factor, 3 * levels, fine_cols), lambda i, t: (i, 0, 0)),
                pl.BlockSpec((1, levels, tile_cols), lambda i, t: (i, 0, 0)),
                whole(light),
                whole(land),
                whole(from_south),
                whole(from_north),
                whole(from_west),
                whole(from_east),
                whole(picks),
            ],
            out_specs=pl.BlockSpec((lon_count, phys_rows, side * side), lambda i, t: (0, 0, 0)),
            scratch_shapes=[pltpu.VMEM((side, 4 * levels + SUB, LANES), f32)],
        ),
        compiler_params=pltpu.CompilerParams(vmem_limit_bytes=VMEM_LIMIT),
        name="coarsen",
    )(table, fine, mix, light, land, from_south, from_north, from_west, from_east, picks)


def owner_of(codes, block, slot_count, lon_count):
    return remainder(quotient(jnp.maximum(codes[0, block], 0), slot_count), lon_count)


def hand_kernel(side, table_ref, below_ref, above_ref, south_ref, north_ref, *refs):
    out_ref = refs[-1]
    b = pl.program_id(0)
    rows = south_ref.shape[1]
    block = table_ref[TILE_BASE, 0] + b
    lead = (lane_ids(rows) & side) == 0
    south = jnp.where(below_ref[0, block] >= 0, south_ref[0], 0.0)
    north = jnp.where(above_ref[0, block] >= 0, north_ref[0], 0.0)
    out_ref[0, 0:rows, :] = jnp.where(lead, turned(north, -side), turned(south, side))
    out_ref[0, rows : 2 * rows, :] = jnp.where(lead, north, turned(south, 2 * side))


def hand_on(
    table, codes_below, codes_above, from_south, from_north, joined, side, slot_count, tile_blocks, *after
):
    lon_count, rows, width = from_south.shape
    if joined:
        rows = rows // 2

    def spot(t, b):
        return t[TILE_BASE, 0] + b

    return pl.pallas_call(
        functools.partial(hand_kernel, side),
        out_shape=jax.ShapeDtypeStruct((lon_count, 2 * rows, width), jnp.float32),
        grid_spec=pltpu.PrefetchScalarGridSpec(
            num_scalar_prefetch=3,
            grid=(tile_blocks,),
            in_specs=[
                pl.BlockSpec(
                    (1, rows, width),
                    lambda b, t, lo, hi: (owner_of(lo, spot(t, b), slot_count, lon_count), 0, 0),
                ),
                pl.BlockSpec(
                    (1, rows, width),
                    lambda b, t, lo, hi: (owner_of(hi, spot(t, b), slot_count, lon_count), int(joined), 0),
                ),
            ]
            + [pl.BlockSpec(memory_space=pl.ANY)] * len(after),
            out_specs=pl.BlockSpec((1, 2 * rows, width), lambda b, t, lo, hi: (t[TILE_OWNER, b], 0, 0)),
        ),
        compiler_params=pltpu.CompilerParams(vmem_limit_bytes=VMEM_LIMIT),
        name="hand_on",
    )(table, codes_below, codes_above, from_south, from_north, *after)


def gate_kernel(*refs):
    pass


def gate(x, *others):
    anywhere = pl.BlockSpec(memory_space=pl.ANY)
    return pl.pallas_call(
        gate_kernel,
        out_shape=jax.ShapeDtypeStruct(x.shape, x.dtype),
        in_specs=[anywhere] * (1 + len(others)),
        out_specs=anywhere,
        input_output_aliases={0: 0},
        name="gate",
    )(x, *others)


def heat_kernel(levels, side, factor, table_ref, chl_ref, light_ref, land_ref, widen_ref, out_ref, rows_ref, wide_ref):
    tile_blocks = land_ref.shape[1] // side
    halves = side * side // LANES
    group = LANES // side
    fine_cols = light_ref.shape[1]
    fine_rows = light_ref.shape[0]
    f32 = jnp.float32
    group_id = lane_ids() >> (side.bit_length() - 1)

    def place(lt, carry):
        at = pl.multiple_of(lt * SUB, SUB)
        for h in range(halves):
            blocks = []
            for b in range(tile_blocks):
                owner = table_ref[TILE_OWNER, b]
                values = chl_ref[owner, pl.ds(at, SUB), h * LANES : (h + 1) * LANES]
                blocks.append(jnp.where(table_ref[TILE_WET, b] == 1, values, 0.0))
            for r in range(group):
                line = None
                for b in range(tile_blocks):
                    piece = turned(blocks[b], side * (b - r))
                    line = piece if line is None else jnp.where(group_id == b, piece, line)
                rows_ref[pl.ds(pl.multiple_of((h * group + r) * levels + lt * SUB, SUB), SUB), :] = line
        return carry

    lax.fori_loop(0, levels // SUB, place, 0)
    wet = land_ref[...].astype(f32)
    widen = widen_ref[...]
    above = jnp.zeros_like(wet)
    passing = jnp.ones_like(wet)
    for l in range(levels):
        chl = rows_ref[pl.ds(l, side, stride=levels), :]
        above = above + (0.04 + 0.02 * chl)
        through = jnp.exp(-above)
        kept = (passing - through) * wet
        passing = through
        high = kept.astype(jnp.bfloat16)
        low = (kept - high.astype(f32)).astype(jnp.bfloat16)
        wide_ref[l * side : (l + 1) * side, :] = jnp.dot(
            high, widen, preferred_element_type=f32
        ) + jnp.dot(low, widen, preferred_element_type=f32)

    sub = lax.broadcasted_iota(jnp.int32, (SUB, LANES), 0)
    sources = []
    for m in range(fine_rows // SUB):
        start = (m * SUB // factor) // SUB * SUB
        index = jnp.zeros_like(sub)
        for r in range(1, side):
            index = index + jnp.where(sub + m * SUB >= r * factor, 1, 0)
        sources.append((start, index - start))

    def spread(l, carry):
        for c in range(fine_cols // LANES):
            span = slice(c * LANES, (c + 1) * LANES)
            for m in range(0, fine_rows // SUB, 2):
                both = []
                for n in (m, m + 1):
                    start, index = sources[n]
                    lines = wide_ref[pl.ds(pl.multiple_of(l * side + start, SUB), SUB), span]
                    lines = jnp.take_along_axis(lines, index, axis=0)
                    both.append(lines * light_ref[n * SUB : (n + 1) * SUB, span])
                out_ref[l, m * SUB : (m + 2) * SUB, span] = jnp.concatenate(both, axis=0).astype(jnp.bfloat16)
        return carry

    lax.fori_loop(0, levels, spread, 0)


def heat(table, chl, light, land, levels, widen):
    side = land.shape[0]
    factor = light.shape[0] // side
    vmem = pl.BlockSpec(memory_space=pltpu.VMEM)
    return pl.pallas_call(
        functools.partial(heat_kernel, levels, side, factor),
        out_shape=jax.ShapeDtypeStruct((levels,) + light.shape, jnp.bfloat16),
        in_specs=[pl.BlockSpec(memory_space=pltpu.SMEM), vmem, vmem, vmem, vmem],
        out_specs=vmem,
        scratch_shapes=[
            pltpu.VMEM((side * levels, LANES), jnp.float32),
            pltpu.VMEM((side * levels, light.shape[1]), jnp.float32),
        ],
        compiler_params=pltpu.CompilerParams(vmem_limit_bytes=VMEM_LIMIT),
        name="heat",
    )(table, chl, light, land, widen)


def part_kernel(rows, both_ref, *refs):
    south_ref, north_ref = refs[-2:]
    south_ref[...] = both_ref[:, 0:rows, :]
    north_ref[...] = both_ref[:, rows : 2 * rows, :]


def part(both, *after):
    count, rows, width = both.shape
    rows = rows // 2
    half = jax.ShapeDtypeStruct((count, rows, width), both.dtype)
    spec = pl.BlockSpec((1, rows, width), lambda i: (i, 0, 0))
    return pl.pallas_call(
        functools.partial(part_kernel, rows),
        out_shape=[half, half],
        grid=(count,),
        in_specs=[pl.BlockSpec((1, 2 * rows, width), lambda i: (i, 0, 0))]
        + [pl.BlockSpec(memory_space=pl.ANY)] * len(after),
        out_specs=[spec, spec],
        compiler_params=pltpu.CompilerParams(vmem_limit_bytes=VMEM_LIMIT),
        name="part",
    )(both, *after)


def widened(x, rows, width):
    return jnp.pad(x, ((0, rows - x.shape[0]), (0, width - x.shape[1])))


def on_device(tracers, phys_fine, mix_coarse, surf_light, land_mask, owner_map):
    f32 = jnp.float32
    slot_count = tracers.shape[0]
    side = land_mask.shape[0]
    levels = mix_coarse.shape[2]
    tile_blocks = land_mask.shape[1] // side
    factor = phys_fine.shape[0] // side
    fine_cols = phys_fine.shape[1]
    block_count = owner_map.shape[1]
    group = LANES // side

    fine = jnp.transpose(phys_fine, (0, 2, 1))
    mix = jnp.transpose(mix_coarse, (0, 2, 1))
    wet = land_mask.astype(f32)
    codes = owner_map.astype(f32) + 1.0
    width = max(fine_cols, block_count)

    northward = jnp.concatenate(
        [
            widened(fine[-1, levels : 2 * levels, :].astype(f32), levels, width),
            widened(wet[-1:], 1, width),
            widened(codes, 1, width),
        ],
        axis=0,
    )
    southward = jnp.concatenate([widened(wet[:1], 1, width), widened(codes, 1, width)], axis=0)
    last_face = jnp.mean(
        fine[:, :levels, fine_cols - 1].astype(f32).reshape(side, factor, levels), axis=1
    )
    face_pack = jnp.pad(
        last_face.reshape(side // group, group, levels // SUB, SUB).transpose(3, 1, 0, 2),
        ((0, 0), (0, 0), (0, 0), (0, group - levels // SUB)),
    ).reshape(SUB, LANES)
    eastward = jnp.concatenate([face_pack, widened(wet[:, -1][None], 1, LANES)], axis=0)
    westward = widened(wet[:, 0][None], 1, LANES)

    from_south = lax.ppermute(northward, "lat", along("lat", 1, False))
    from_north = lax.ppermute(southward, "lat", along("lat", -1, False))
    from_west = lax.ppermute(eastward, "lon", along("lon", 1, True))
    from_east = lax.ppermute(westward, "lon", along("lon", -1, True))
    codes_below = from_south[levels + 1 :, :block_count].astype(jnp.int32) - 1
    codes_above = from_north[1:, :block_count].astype(jnp.int32) - 1

    fine_id = jnp.arange(fine_cols)[:, None]
    coarse_id = jnp.arange(land_mask.shape[1])[None, :]
    member = (fine_id // factor == coarse_id).astype(jnp.bfloat16)
    final = (fine_id == factor * coarse_id + factor - 1).astype(jnp.bfloat16)
    picks = jnp.concatenate([final, member], axis=1)

    table = routing(owner_map, slot_count, tile_blocks)
    edge_rows, west, east = first_edges(
        table, tracers, levels, side, from_south, from_north, from_west, from_east
    )
    phys = coarsen(
        table, fine, mix, surf_light, land_mask, from_south, from_north, from_west, from_east, picks
    )
    rows = edge_rows.shape[1] // 2

    def hand(from_south, from_north, joined, *after):
        handed = hand_on(
            table,
            codes_below,
            codes_above,
            from_south,
            from_north,
            joined,
            side,
            slot_count,
            tile_blocks,
            *after,
        )
        return lax.all_to_all(handed, "lon", 0, 0, tiled=True)

    def to_north(x):
        return lax.ppermute(x, "lat", along("lat", 1, False))

    def to_south(x):
        return lax.ppermute(x, "lat", along("lat", -1, False))

    def beside(west, east):
        return (
            lax.ppermute(east, "lon", along("lon", 1, True)),
            lax.ppermute(west, "lon", along("lon", -1, True)),
        )

    rim_w, rim_e = beside(west, east)
    tile_rows = lax.all_to_all(edge_rows, "lon", 0, 0, tiled=True)
    phys = gate(phys, rim_w, rim_e, tile_rows)
    south, north = part(tile_rows, phys)
    phys = lax.all_to_all(phys, "lon", 0, 0, tiled=True)
    rims = hand(to_north(north), to_south(south), False)

    current = tracers
    for step_index in range(ITERS):
        last = step_index == ITERS - 1
        got = step(table, current, phys, rims, rim_w, rim_e, levels, side, last)
        if last:
            current, chl = got
            break
        current, edge_rows, west, east = got
        rim_w, rim_e = beside(west, east)
        moved_rows = jnp.concatenate([to_north(edge_rows[:, rows:]), to_south(edge_rows[:, :rows])], axis=1)
        tile_rows = lax.all_to_all(moved_rows, "lon", 0, 0, tiled=True)
        rims = hand(tile_rows, tile_rows, True, rim_w, rim_e)
    chl = lax.all_to_all(chl, "lon", 0, 0, tiled=True)
    heating = heat(table, chl, surf_light, land_mask, levels, jnp.transpose(member))
    return current, heating


def solution(mesh):
    in_specs = (
        P(("lat", "lon"), None, None),
        P("lat", "lon", None),
        P("lat", "lon", None),
        P("lat", "lon"),
        P("lat", "lon"),
        P("lat", None),
    )
    out_specs = (P(("lat", "lon"), None, None), P(None, "lat", "lon"))
    return jax.shard_map(
        on_device, mesh=mesh, in_specs=in_specs, out_specs=out_specs, check_vma=False
    )
```

```python
import functools

import jax
import jax.numpy as jnp
from jax import lax
from jax.experimental import pallas as pl
from jax.experimental.pallas import tpu as pltpu
from jax.sharding import PartitionSpec as P

LANES = 128
SUB = 8

diffuse_rate = 0.08
nano_chl_index = 10
diat_chl_index = 11

SLOT_TILE, SLOT_FULL, SLOT_WEST, SLOT_EAST, TILE_OWNER, TILE_WET, TILE_BASE = range(7)
TABLE_ROWS = 8

OPEN_EAST, OPEN_NORTH, OPEN_WEST, OPEN_SOUTH, LIGHT, WET = range(6)

VMEM_LIMIT = 48 * 1024 * 1024


def positive(value):
    return jnp.maximum(value, 0.0)


def lane_ids(rows=SUB):
    return lax.broadcasted_iota(jnp.int32, (rows, LANES), 1)


def turned(value, by):
    by = by % LANES
    return value if by == 0 else pltpu.roll(value, by, 1)


def quotient(value, by):
    if by & (by - 1) == 0:
        return lax.shift_right_logical(value, jnp.int32(by.bit_length() - 1))
    return lax.div(value, jnp.int32(by))


def remainder(value, by):
    if by & (by - 1) == 0:
        return value & (by - 1)
    return lax.rem(value, jnp.int32(by))


def along(axis, by, closed):
    size = lax.axis_size(axis)
    pairs = [(i, (i + by) % size) for i in range(size)]
    return [p for p in pairs if closed or p[1] == p[0] + by]


def table_kernel(slot_count, tile_blocks, lon_count, row_ref, out_ref, used_ref):
    me = lax.axis_index("lon")
    block_count = row_ref.shape[1]
    width = out_ref.shape[1]

    def clear(i, carry):
        for r in range(TABLE_ROWS):
            out_ref[r, i] = 0
        return carry

    lax.fori_loop(0, width, clear, 0)

    def unuse(i, carry):
        used_ref[0, i] = 0
        used_ref[1, i] = 0
        return carry

    lax.fori_loop(0, lon_count, unuse, 0)
    out_ref[TILE_BASE, 0] = me * tile_blocks

    def visit(k, carry):
        code = row_ref[0, k]
        safe = jnp.maximum(code, 0)
        owner = remainder(quotient(safe, slot_count), lon_count)
        slot = remainder(safe, slot_count)
        tile = quotient(k, tile_blocks)

        @pl.when((code >= 0) & (owner == me))
        def _():
            west = row_ref[0, remainder(k + block_count - 1, block_count)]
            east = row_ref[0, remainder(k + 1, block_count)]
            out_ref[SLOT_TILE, slot] = tile
            out_ref[SLOT_FULL, slot] = 1
            out_ref[SLOT_WEST, slot] = remainder(jnp.maximum(west, 0), slot_count)
            out_ref[SLOT_EAST, slot] = remainder(jnp.maximum(east, 0), slot_count)
            used_ref[0, tile] = 1

        @pl.when((code >= 0) & (tile == me))
        def _():
            local = remainder(k, tile_blocks)
            out_ref[TILE_OWNER, local] = owner
            out_ref[TILE_WET, local] = 1
            used_ref[1, owner] = 1

        return carry

    lax.fori_loop(0, block_count, visit, 0, unroll=4)

    def give(target, filled, line, count):
        def one(i, carry):
            def look(j, done):
                take = (done == 0) & (used_ref[line, j] == 0)

                @pl.when(take)
                def _():
                    out_ref[target, i] = j
                    used_ref[line, j] = 1

                return jnp.where(take, 1, done)

            @pl.when(out_ref[filled, i] == 0)
            def _():
                lax.fori_loop(0, lon_count, look, 0)

            return carry

        lax.fori_loop(0, count, one, 0)

    give(SLOT_TILE, SLOT_FULL, 0, slot_count)
    give(TILE_OWNER, TILE_WET, 1, tile_blocks)


def routing(row, slot_count, tile_blocks):
    lon_count = lax.axis_size("lon")
    width = max(slot_count, tile_blocks, lon_count)
    return pl.pallas_call(
        functools.partial(table_kernel, slot_count, tile_blocks, lon_count),
        out_shape=jax.ShapeDtypeStruct((TABLE_ROWS, width), jnp.int32),
        in_specs=[pl.BlockSpec(memory_space=pltpu.SMEM)],
        out_specs=pl.BlockSpec(memory_space=pltpu.SMEM),
        scratch_shapes=[pltpu.SMEM((2, lon_count), jnp.int32)],
        name="routing",
    )(row)


def merged(pieces, ids):
    packed = pieces[0]
    for g in range(1, len(pieces)):
        packed = jnp.where(ids == g, pieces[g], packed)
    return packed


def pack_columns(first, second, side):
    lane = lane_ids()
    odd = (lane & 1) == 1
    here = (lane & (side - 1)) >> 1
    there = ((lane + 1) & (side - 1)) >> 1
    even_ends = merged([turned(v, 1 + 2 * g) for g, v in enumerate(first)], here)
    odd_ends = merged([turned(v, 2 * g) for g, v in enumerate(second)], there)
    return jnp.where(odd, even_ends, odd_ends), jnp.where(odd, odd_ends, even_ends)


def pack_quads(first, second, side):
    low = lane_ids() < LANES // 2
    both = [jnp.where(low, a, b) for a, b in zip(first, second)]
    turns = [turned(v, 2 * side + (g % 2) * (LANES // 2)) for g, v in enumerate(both)]
    return [jnp.where(low, turns[g], turns[g + 1]) for g in range(0, len(turns), 2)]


def regroup(values, side):
    values = list(values)
    ids = lane_ids() >> (side.bit_length() - 1)
    bit = 1
    while bit < len(values):
        keep = (ids & bit) == 0
        for n in range(len(values)):
            if n & bit == 0:
                a, b = values[n], values[n + bit]
                values[n] = jnp.where(keep, a, turned(b, side * bit))
                values[n + bit] = jnp.where(keep, turned(a, -side * bit), b)
        bit *= 2
    return values


def edges_kernel(levels, side, table_ref, cell_ref, rows_ref, west_ref, east_ref):
    group = LANES // side
    rounds = cell_ref.shape[1] // levels // group
    level_tiles = levels // SUB

    def body(lt, carry):
        for i in range(rounds):
            row = pl.multiple_of(i * levels + lt * SUB, SUB)
            first, second = [], []
            for g in range(group):
                at = pl.multiple_of((i * group + g) * levels + lt * SUB, SUB)
                first.append(cell_ref[0, pl.ds(at, SUB), 0:LANES])
                second.append(cell_ref[0, pl.ds(at, SUB), LANES : 2 * LANES])
            west, east = pack_columns(first, second, side)
            west_ref[0, pl.ds(row, SUB), :] = west
            east_ref[0, pl.ds(row, SUB), :] = east
            for n, quad in enumerate(pack_quads(first, second, side)):
                at = pl.multiple_of((i * (group // 2) + n) * levels + lt * SUB, SUB)
                rows_ref[0, pl.ds(at, SUB), :] = quad
        return carry

    lax.fori_loop(0, level_tiles, body, 0, unroll=True)


def first_edges(table, tracers, levels, side):
    slot_count, channels, cell_count = tracers.shape
    lon_count = lax.axis_size("lon")
    rows = channels * side // LANES
    f32 = jnp.float32
    by_slot = pl.BlockSpec((1, rows, LANES), lambda s, t: (s, 0, 0))
    return pl.pallas_call(
        functools.partial(edges_kernel, levels, side),
        out_shape=[
            jax.ShapeDtypeStruct((lon_count, 4 * rows, LANES), f32),
            jax.ShapeDtypeStruct((slot_count, rows, LANES), f32),
            jax.ShapeDtypeStruct((slot_count, rows, LANES), f32),
        ],
        grid_spec=pltpu.PrefetchScalarGridSpec(
            num_scalar_prefetch=1,
            grid=(slot_count,),
            in_specs=[pl.BlockSpec((1, channels, cell_count), lambda s, t: (s, 0, 0))],
            out_specs=[
                pl.BlockSpec((1, 4 * rows, LANES), lambda s, t: (t[SLOT_TILE, s], 0, 0)),
                by_slot,
                by_slot,
            ],
        ),
        compiler_params=pltpu.CompilerParams(vmem_limit_bytes=VMEM_LIMIT),
        name="first_edges",
    )(table, tracers)


def react(mixed, par_light, warm_factor):
    (
        carbon_dis,
        alkalinity,
        oxygen,
        nitrate,
        ammonium,
        phosphate,
        silicate,
        iron_free,
        nano_carbon,
        diat_carbon,
        nano_chl,
        diat_chl,
        nano_iron,
        diat_iron,
        diat_silica,
        micro_zoo,
        meso_zoo,
        dissolved_org,
        small_part,
        big_part,
        small_iron,
        big_iron,
        big_silica,
        calcite,
    ) = mixed
    nitrogen = positive(nitrate) + positive(ammonium)
    limit_nitro = nitrogen / (0.5 + nitrogen)
    limit_phos = positive(phosphate) / (0.3 + positive(phosphate))
    limit_iron = positive(iron_free) / (0.2 + positive(iron_free))
    limit_sil = positive(silicate) / (1.0 + positive(silicate))
    nutr_nano = jnp.minimum(jnp.minimum(limit_nitro, limit_phos), limit_iron)
    nutr_diat = jnp.minimum(nutr_nano, limit_sil)
    lit = warm_factor * par_light
    prod_nano = 0.1 * lit / (par_light + 0.5) * nutr_nano * nano_carbon
    prod_diat = 0.12 * lit / (par_light + 1.0) * nutr_diat * diat_carbon
    ammon_share = (positive(ammonium) + 0.01) / (nitrogen + 0.02)
    graze_nano = 0.08 * warm_factor * micro_zoo / (1.0 + positive(nano_carbon))
    graze_diat = 0.06 * warm_factor * meso_zoo / (1.0 + positive(diat_carbon))
    loss_nano = graze_nano + 0.02
    loss_diat = graze_diat + 0.02
    eaten_nano = graze_nano * nano_carbon
    eaten_diat = graze_diat * diat_carbon
    death_micro = 0.03 * micro_zoo * positive(micro_zoo)
    death_meso = 0.03 * meso_zoo * positive(meso_zoo)
    remin_doc = 0.03 * warm_factor * dissolved_org
    remin_poc = 0.02 * warm_factor * small_part
    remin_goc = 0.01 * warm_factor * big_part
    nitrify = 0.05 * ammonium
    melt_si = 0.02 * big_silica
    melt_cal = 0.01 * calcite
    melt_sfe = 0.02 * small_iron
    melt_bfe = 0.01 * big_iron
    uptake = prod_nano + prod_diat
    remin_total = remin_doc + remin_poc + remin_goc
    calcify = 0.02 * prod_nano
    gained = remin_total - uptake
    shell = melt_cal - calcify
    by_ammon = ammon_share * uptake
    by_nitrate = 0.16 * (uptake - by_ammon - nitrify)
    return [
        carbon_dis + gained + shell,
        alkalinity + 2.0 * shell + by_nitrate,
        oxygen - 1.3 * gained - 0.32 * nitrify,
        nitrate - by_nitrate,
        ammonium + 0.16 * (remin_total - by_ammon - nitrify),
        phosphate + 0.01 * gained,
        silicate + melt_si - 0.15 * prod_diat,
        iron_free + melt_sfe + melt_bfe - 0.005 * uptake,
        nano_carbon + prod_nano - loss_nano * nano_carbon,
        diat_carbon + prod_diat - loss_diat * diat_carbon,
        nano_chl + 0.03 * prod_nano - loss_nano * nano_chl,
        diat_chl + 0.03 * prod_diat - loss_diat * diat_chl,
        nano_iron + 0.005 * prod_nano - loss_nano * nano_iron,
        diat_iron + 0.005 * prod_diat - loss_diat * diat_iron,
        diat_silica + 0.15 * prod_diat - loss_diat * diat_silica,
        micro_zoo + 0.3 * eaten_nano - death_micro,
        meso_zoo + 0.3 * eaten_diat - death_meso,
        dissolved_org + 0.3 * eaten_nano + 0.02 * nano_carbon - remin_doc,
        small_part + 0.4 * eaten_nano + death_micro - remin_poc,
        big_part + 0.4 * eaten_diat + 0.02 * diat_carbon + death_meso - remin_goc,
        small_iron + loss_nano * nano_iron - melt_sfe,
        big_iron + loss_diat * diat_iron - melt_bfe,
        big_silica + loss_diat * diat_silica - melt_si,
        calcite + calcify - melt_cal,
    ]


def set_transport(coef_ref, at, span, faces, opens):
    flow_e, flow_n, flow_w, flow_s = (face * is_open for face, is_open in zip(faces, opens))
    open_e, open_n, open_w, open_s = opens
    out_e, in_e = jnp.maximum(flow_e, 0.0), jnp.minimum(flow_e, 0.0)
    out_n, in_n = jnp.maximum(flow_n, 0.0), jnp.minimum(flow_n, 0.0)
    in_w, out_w = jnp.maximum(flow_w, 0.0), jnp.minimum(flow_w, 0.0)
    in_s, out_s = jnp.maximum(flow_s, 0.0), jnp.minimum(flow_s, 0.0)
    drift = diffuse_rate * (open_w + open_e + open_s + open_n)
    coef_ref[0, at, span] = 1.0 - (out_e - out_w) - (out_n - out_s) - drift
    coef_ref[1, at, span] = diffuse_rate * open_e - in_e
    coef_ref[2, at, span] = diffuse_rate * open_w + in_w
    coef_ref[3, at, span] = diffuse_rate * open_n - in_n
    coef_ref[4, at, span] = diffuse_rate * open_s + in_s


def set_mixing(coef_ref, at, span, mix, above, bottom):
    sub = lax.broadcasted_iota(jnp.int32, (SUB, LANES), 0)
    mix_up = pltpu.roll(jnp.where(sub == SUB - 1, above, mix), 1, 0)
    if bottom:
        mix = jnp.where(sub == SUB - 1, 0.0, mix)
    coef_ref[5, at, span] = 1.0 - mix - mix_up
    coef_ref[6, at, span] = mix
    coef_ref[7, at, span] = mix_up


def set_blank(moved_ref, channels):
    blank = jnp.zeros((SUB, moved_ref.shape[1]), jnp.float32)
    moved_ref[0:SUB, :] = blank
    moved_ref[SUB + channels : 2 * SUB + channels, :] = blank


def mix_and_react(levels, tracer_count, spans, moved_ref, coef_ref, light, wet, warm_at, store):
    sub = lax.broadcasted_iota(jnp.int32, (SUB, LANES), 0)

    def reacting(lt, carry):
        at = pl.multiple_of(lt * SUB, SUB)
        depths = []
        halves_new = []
        for h, span in enumerate(spans):
            mix_c, mix_d, mix_u = (coef_ref[n, pl.ds(at, SUB), span] for n in (5, 6, 7))
            mixed = []
            for t in range(tracer_count):
                base = t * levels + lt * SUB
                before = moved_ref[pl.ds(pl.multiple_of(base, SUB), SUB), span]
                now = moved_ref[pl.ds(pl.multiple_of(base + SUB, SUB), SUB), span]
                after = moved_ref[pl.ds(pl.multiple_of(base + 2 * SUB, SUB), SUB), span]
                up = pltpu.roll(jnp.where(sub == SUB - 1, before, now), 1, 0)
                down = pltpu.roll(jnp.where(sub == 0, after, now), SUB - 1, 0)
                mixed.append(mix_c * now + mix_d * down + mix_u * up)
            absorb = 0.04 + 0.02 * (positive(mixed[nano_chl_index]) + positive(mixed[diat_chl_index]))
            total = absorb
            for by in (1, 2, 4):
                total = total + jnp.where(sub >= by, pltpu.roll(total, by, 0), 0.0)
            above = carry[h] + (total - absorb)
            depths.append(carry[h] + total[SUB - 1 : SUB, :])
            par_light = light[h] * jnp.exp(-(above + 0.5 * absorb))
            halves_new.append([value * wet[h] for value in react(mixed, par_light, warm_at(lt, h))])
            for t in range(tracer_count):
                store(t, pl.multiple_of(t * levels + lt * SUB, SUB), h, halves_new[h][t])
        store(None, lt, None, halves_new)
        return tuple(depths)

    start = tuple(jnp.zeros((1, LANES), jnp.float32) for _ in spans)
    lax.fori_loop(0, levels // SUB, reacting, start, unroll=True)


def step_kernel(levels, side, last, table_ref, cell_ref, phys_ref, rim_ref, rim_w_ref, rim_e_ref, *refs):
    if last:
        out_ref, chl_ref, coef_ref, moved_ref, ends_ref = refs
        edge_refs = (chl_ref,)
    else:
        out_ref, west_ref, east_ref, coef_ref, moved_ref, ends_ref = refs
        edge_refs = (west_ref, east_ref)
    channels, cell_count = cell_ref.shape[1:]
    tracer_count = channels // levels
    group = LANES // side
    halves = cell_count // LANES
    rounds = tracer_count // group
    level_tiles = levels // SUB
    rows = rounds * levels
    slot = pl.program_id(0)
    full = table_ref[SLOT_FULL, slot] == 1
    spans = [slice(h * LANES, (h + 1) * LANES) for h in range(halves)]

    @pl.when(jnp.logical_not(full))
    def _():
        out_ref[...] = jnp.zeros_like(out_ref)
        for ref in edge_refs:
            ref[...] = jnp.zeros_like(ref)

    @pl.when(full)
    def _():
        lane = lane_ids()
        col = lane & (side - 1)
        first_col = col == 0
        last_col = col == side - 1
        first_row = lane < side
        last_row = lane >= LANES - side
        odd = (lane & 1) == 1
        flag_row = 4 * levels
        pack_at = flag_row + SUB

        def flag(f, h):
            return phys_ref[0, flag_row + f : flag_row + f + 1, spans[h]]

        def southward(values, edge):
            out = []
            for h in range(halves):
                before = edge if h == 0 else turned(values[h - 1], side)
                out.append(jnp.where(first_row, before, turned(values[h], side)))
            return out

        def northward(values, edge):
            out = []
            for h in range(halves):
                after = edge if h == halves - 1 else turned(values[h + 1], -side)
                out.append(jnp.where(last_row, after, turned(values[h], -side)))
            return out

        above_mix = [jnp.zeros((SUB, LANES), jnp.float32)] * halves
        west_pack = phys_ref[0, pack_at : pack_at + SUB, spans[0]]
        south_pack = phys_ref[0, pack_at : pack_at + SUB, spans[1]]
        for lt in range(level_tiles):
            at = slice(lt * SUB, (lt + 1) * SUB)
            east_face = [phys_ref[0, lt * SUB : (lt + 1) * SUB, spans[h]] for h in range(halves)]
            north_face = [
                phys_ref[0, levels + lt * SUB : levels + (lt + 1) * SUB, spans[h]] for h in range(halves)
            ]
            south_face = southward(north_face, turned(south_pack, -side * lt))
            for h in range(halves):
                west_face = jnp.where(
                    first_col, turned(west_pack, -(h * group + lt)), turned(east_face[h], 1)
                )
                faces = (east_face[h], north_face[h], west_face, south_face[h])
                set_transport(coef_ref, at, spans[h], faces, [flag(f, h) for f in range(4)])
                mix = phys_ref[0, 3 * levels + lt * SUB : 3 * levels + (lt + 1) * SUB, spans[h]]
                set_mixing(coef_ref, at, spans[h], mix, above_mix[h], lt == level_tiles - 1)
                above_mix[h] = mix

        for at in range(0, rows, SUB):
            ends_ref[at : at + SUB, :] = turned(rim_w_ref[0, at : at + SUB, :], 2 - 2 * side)
        set_blank(moved_ref, channels)

        def advect(lt, carry):
            at = pl.multiple_of(lt * SUB, SUB)
            coef = [[coef_ref[n, pl.ds(at, SUB), spans[h]] for n in range(5)] for h in range(halves)]
            for i in range(rounds):
                row = pl.multiple_of(i * levels + lt * SUB, SUB)
                rims = [
                    rim_ref[0, pl.ds(row, SUB), :],
                    rim_ref[0, pl.ds(pl.multiple_of(rows + row, SUB), SUB), :],
                ]
                ends_w = ends_ref[pl.ds(row, SUB), :]
                ends_e = rim_e_ref[0, pl.ds(row, SUB), :]
                sides = [jnp.where(odd, ends_e, ends_w), jnp.where(odd, ends_w, ends_e)]
                for g in range(group):
                    chan = pl.multiple_of((i * group + g) * levels + lt * SUB, SUB)
                    here = [cell_ref[0, pl.ds(chan, SUB), spans[h]] for h in range(halves)]
                    rim = turned(rims[2 * g // group], -side - 2 * side * (g % (group // 2)))
                    south = southward(here, rim)
                    north = northward(here, rim)
                    for h in range(halves):
                        ends = turned(sides[h], side - 2 + h - 2 * g)
                        west = jnp.where(first_col, ends, turned(here[h], 1))
                        east = jnp.where(last_col, ends, turned(here[h], -1))
                        c, e, w, n, s = coef[h]
                        moved_ref[pl.ds(pl.multiple_of(SUB + chan, SUB), SUB), spans[h]] = (
                            c * here[h] + (e * east + w * west) + (n * north[h] + s * south[h])
                        )
            return carry

        lax.fori_loop(0, level_tiles, advect, 0, unroll=True)

        def store(t, at, h, value):
            if t is not None:
                out_ref[0, pl.ds(at, SUB), spans[h]] = value
            elif last:
                for k, new in enumerate(value):
                    chl_ref[0, pl.ds(pl.multiple_of(at * SUB, SUB), SUB), spans[k]] = positive(
                        new[nano_chl_index]
                    ) + positive(new[diat_chl_index])
            else:
                for i in range(rounds):
                    row = pl.multiple_of(i * levels + at * SUB, SUB)
                    first, second = (new[i * group : (i + 1) * group] for new in value)
                    west, east = pack_columns(first, second, side)
                    west_ref[0, pl.ds(row, SUB), :] = west
                    east_ref[0, pl.ds(row, SUB), :] = east

        def warm_at(lt, h):
            return phys_ref[0, pl.ds(pl.multiple_of(2 * levels + lt * SUB, SUB), SUB), spans[h]]

        light = [flag(LIGHT, h) for h in range(halves)]
        wet = [flag(WET, h) for h in range(halves)]
        mix_and_react(levels, tracer_count, spans, moved_ref, coef_ref, light, wet, warm_at, store)


def step(table, cells, phys, rims, rim_w, rim_e, levels, side, last):
    slot_count, channels, cell_count = cells.shape
    lon_count = lax.axis_size("lon")
    rows = channels * side // LANES
    phys_rows = phys.shape[1]
    f32 = jnp.float32
    by_slot = pl.BlockSpec((1, channels, cell_count), lambda s, t: (s, 0, 0))
    shapes = [jax.ShapeDtypeStruct(cells.shape, f32)]
    specs = [by_slot]
    if last:
        shapes.append(jax.ShapeDtypeStruct((lon_count, levels, cell_count), f32))
        specs.append(pl.BlockSpec((1, levels, cell_count), lambda s, t: (t[SLOT_TILE, s], 0, 0)))
    else:
        beside = jax.ShapeDtypeStruct((slot_count, rows, LANES), f32)
        shapes += [beside, beside]
        specs += [pl.BlockSpec((1, rows, LANES), lambda s, t: (s, 0, 0))] * 2
    return pl.pallas_call(
        functools.partial(step_kernel, levels, side, last),
        out_shape=shapes,
        grid_spec=pltpu.PrefetchScalarGridSpec(
            num_scalar_prefetch=1,
            grid=(slot_count,),
            in_specs=[
                by_slot,
                pl.BlockSpec((1, phys_rows, cell_count), lambda s, t: (t[SLOT_TILE, s], 0, 0)),
                pl.BlockSpec((1, 2 * rows, LANES), lambda s, t: (t[SLOT_TILE, s], 0, 0)),
                pl.BlockSpec((1, rows, LANES), lambda s, t: (t[SLOT_WEST, s], 0, 0)),
                pl.BlockSpec((1, rows, LANES), lambda s, t: (t[SLOT_EAST, s], 0, 0)),
            ],
            out_specs=specs,
            scratch_shapes=[
                pltpu.VMEM((8, levels, cell_count), f32),
                pltpu.VMEM((channels + 2 * SUB, cell_count), f32),
                pltpu.VMEM((rows, LANES), f32),
            ],
        ),
        compiler_params=pltpu.CompilerParams(vmem_limit_bytes=VMEM_LIMIT),
        name="step",
    )(table, cells, phys, rims, rim_w, rim_e)


def rows_kernel(levels, factor, fine_ref, mix_ref, pick_ref, rows_ref):
    f32 = jnp.float32
    picks = pick_ref[...]
    east_face = jnp.zeros((levels, LANES), f32)
    temp_mean = jnp.zeros((levels, LANES), f32)
    for r in range(factor):
        got = jnp.dot(fine_ref[r], picks, preferred_element_type=f32)
        east_face += got[0:levels, 0:LANES]
        temp_mean += got[2 * levels : 3 * levels, LANES : 2 * LANES]
        if r == factor - 1:
            north_face = got[levels : 2 * levels, LANES : 2 * LANES]
    rows_ref[0, 0:levels, :] = east_face * (1.0 / factor)
    rows_ref[0, levels : 2 * levels, :] = north_face * (1.0 / factor)
    rows_ref[0, 2 * levels : 3 * levels, :] = jnp.exp(0.0639 * (temp_mean * (1.0 / (factor * factor))))
    rows_ref[0, 3 * levels : 4 * levels, :] = mix_ref[0].astype(f32)


def coarse_rows(fine, mix, picks):
    side, levels, tile_cols = mix.shape
    factor = fine.shape[0] // side
    fine_cols = fine.shape[2]
    return pl.pallas_call(
        functools.partial(rows_kernel, levels, factor),
        out_shape=jax.ShapeDtypeStruct((side, 4 * levels, tile_cols), jnp.float32),
        grid=(side,),
        in_specs=[
            pl.BlockSpec((factor, 3 * levels, fine_cols), lambda i: (i, 0, 0)),
            pl.BlockSpec((1, levels, tile_cols), lambda i: (i, 0, 0)),
            pl.BlockSpec(picks.shape, lambda i: (0, 0)),
        ],
        out_specs=pl.BlockSpec((1, 4 * levels, tile_cols), lambda i: (i, 0, 0)),
        compiler_params=pltpu.CompilerParams(vmem_limit_bytes=VMEM_LIMIT),
        name="coarse_rows",
    )(fine, mix, picks)


def place_kernel(
    levels,
    side,
    factor,
    table_ref,
    rows_ref,
    light_ref,
    land_ref,
    south_ref,
    north_ref,
    west_ref,
    east_ref,
    pick_ref,
    out_ref,
    line_ref,
    flags_ref,
):
    tile_blocks = land_ref.shape[1] // side
    halves = side * side // LANES
    group = LANES // side
    fine_cols = light_ref.shape[1]
    f32 = jnp.float32
    picks = pick_ref[...]
    lane = lane_ids()
    group_id = lane >> (side.bit_length() - 1)
    col_id = lane & (side - 1)
    flag_row = 4 * levels
    pack_at = flag_row + SUB
    wet = land_ref[...].astype(f32)
    sides = wet.shape
    lane2 = lax.broadcasted_iota(jnp.int32, sides, 1)
    sub2 = lax.broadcasted_iota(jnp.int32, sides, 0)
    diagonal = lane2 == sub2
    rim_w = jnp.sum(jnp.where(diagonal, west_ref[SUB : SUB + 1, :], 0.0), axis=1, keepdims=True)
    rim_e = jnp.sum(jnp.where(diagonal, east_ref[0:1, :], 0.0), axis=1, keepdims=True)
    wet_w = jnp.where(lane2 == 0, rim_w, pltpu.roll(wet, 1, 1))
    wet_e = jnp.where(lane2 == LANES - 1, rim_e, pltpu.roll(wet, LANES - 1, 1))
    wet_s = jnp.where(sub2 == 0, south_ref[levels : levels + 1, 0:LANES], pltpu.roll(wet, 1, 0))
    wet_n = jnp.where(sub2 == side - 1, north_ref[0:1, 0:LANES], pltpu.roll(wet, side - 1, 0))
    fold_r = lax.broadcasted_iota(jnp.int32, (side, side * factor), 0)
    fold_c = lax.broadcasted_iota(jnp.int32, (side, side * factor), 1)
    fold_d = fold_c - factor * fold_r
    fold = jnp.where((fold_d >= 0) & (fold_d < factor), 1.0, 0.0)
    narrow = picks[:, LANES : 2 * LANES].astype(f32)
    light_rows = jnp.dot(fold, light_ref[...], precision=lax.Precision.HIGHEST, preferred_element_type=f32)
    light_mean = jnp.dot(
        light_rows, narrow, precision=lax.Precision.HIGHEST, preferred_element_type=f32
    ) * (1.0 / (factor * factor))
    flags = [wet * wet_e, wet * wet_n, wet * wet_w, wet * wet_s, light_mean, wet]
    for r in range(side):
        for f, value in enumerate(flags):
            flags_ref[r, f : f + 1, :] = value[r : r + 1, :]
        flags_ref[r, len(flags) : SUB, :] = jnp.zeros((SUB - len(flags), LANES), f32)

    def place(ref, frm, to):
        for h in range(halves):
            values = [ref[h * group + r, pl.ds(frm, SUB), :] for r in range(group)]
            for b, block in enumerate(regroup(values, side)):
                owner = table_ref[TILE_OWNER, b]
                out_ref[owner, pl.ds(to, SUB), h * LANES : (h + 1) * LANES] = block

    def place_four(q, carry):
        for n in range(4):
            at = pl.multiple_of(n * levels + q * SUB, SUB)
            place(rows_ref, at, at)
        return carry

    lax.fori_loop(0, levels // SUB, place_four, 0)
    place(flags_ref, 0, flag_row)

    fine_v = south_ref[0:levels, 0:fine_cols].astype(jnp.bfloat16)
    north_below = jnp.dot(fine_v, picks, preferred_element_type=f32)[:, LANES : 2 * LANES] * (1.0 / factor)
    for h, r in enumerate((0, side - 1)):
        span = slice(h * LANES, (h + 1) * LANES)
        line_ref[0 : 4 * levels, span] = rows_ref[r, 0 : 4 * levels, :]
        line_ref[6 * levels : 6 * levels + SUB, span] = flags_ref[r]
        line_ref[5 * levels : 6 * levels, span] = (
            north_below if h == 0 else rows_ref[r - 1, levels : 2 * levels, :]
        )
        from_lane = side * (r % group) + group * (r // group)
        for lt in range(levels // SUB):
            face = rows_ref[r, lt * SUB : (lt + 1) * SUB, :]
            line_ref[4 * levels + lt * SUB : 4 * levels + (lt + 1) * SUB, span] = jnp.where(
                lane == 0, turned(west_ref[0:SUB, :], -(from_lane + lt)), turned(face, 1)
            )
    for b in range(tile_blocks):
        owner = table_ref[TILE_OWNER, b]
        south_pack = jnp.zeros((SUB, LANES), f32)
        for lt in range(levels // SUB):
            piece = turned(north_below[lt * SUB : (lt + 1) * SUB, :], side * (lt - b))
            south_pack = jnp.where(group_id == lt, piece, south_pack)
        if b == 0:
            west_pack = west_ref[0:SUB, :]
        else:
            beside = table_ref[TILE_OWNER, b - 1]
            west_pack = jnp.zeros((SUB, LANES), f32)
            for h in range(halves):
                for lt in range(levels // SUB):
                    face = out_ref[beside, lt * SUB : (lt + 1) * SUB, h * LANES : (h + 1) * LANES]
                    piece = turned(face, h * group + lt - (side - 1))
                    west_pack = jnp.where(col_id == h * group + lt, piece, west_pack)
        out_ref[owner, pack_at : pack_at + SUB, 0:LANES] = west_pack
        out_ref[owner, pack_at : pack_at + SUB, LANES : 2 * LANES] = south_pack


def coarsen(table, rows, light, land, from_south, from_north, from_west, from_east, picks):
    lon_count = lax.axis_size("lon")
    side, tile_cols = land.shape
    levels = rows.shape[1] // 4
    factor = light.shape[0] // side
    phys_rows = 4 * levels + 2 * SUB
    f32 = jnp.float32
    vmem = pl.BlockSpec(memory_space=pltpu.VMEM)
    return pl.pallas_call(
        functools.partial(place_kernel, levels, side, factor),
        out_shape=[
            jax.ShapeDtypeStruct((lon_count, phys_rows, side * side), f32),
            jax.ShapeDtypeStruct((6 * levels + SUB, 2 * LANES), f32),
        ],
        in_specs=[pl.BlockSpec(memory_space=pltpu.SMEM)] + [vmem] * 8,
        out_specs=[vmem, vmem],
        scratch_shapes=[pltpu.VMEM((side, SUB, LANES), f32)],
        compiler_params=pltpu.CompilerParams(vmem_limit_bytes=VMEM_LIMIT),
        name="coarsen",
    )(table, rows, light, land, from_south, from_north, from_west, from_east, picks)


def lines_kernel(levels, side, table_ref, quad_ref, low_ref, high_ref, low_in_ref, high_in_ref, ends_ref):
    tile_blocks = LANES // side
    pairs = quad_ref.shape[1] // levels
    lane = lane_ids()
    spot = lane >> 1

    def body(lt, carry):
        packed = jnp.zeros((SUB, LANES), jnp.float32)
        for m in range(pairs):
            at = pl.multiple_of(m * levels + lt * SUB, SUB)
            blocks = []
            for b in range(tile_blocks):
                value = quad_ref[table_ref[TILE_OWNER, b], pl.ds(at, SUB), :]
                blocks.append(jnp.where(table_ref[TILE_WET, b] == 1, value, 0.0))
            parts = regroup(blocks, side)
            for p in range(2):
                t = 2 * m + p
                chan = pl.ds(pl.multiple_of(t * levels + lt * SUB, SUB), SUB)
                high_in, high, low, low_in = parts[4 * p : 4 * p + 4]
                low_ref[chan, :] = low
                high_ref[chan, :] = high
                low_in_ref[chan, :] = low_in
                high_in_ref[chan, :] = high_in
                for k, line in ((2 * t, low), (2 * t + 1, high)):
                    packed = jnp.where(spot == k, turned(line, 1 + 2 * k), packed)
        ends_ref[pl.ds(pl.multiple_of(lt * SUB, SUB), SUB), :] = packed
        return carry

    lax.fori_loop(0, levels // SUB, body, 0)


def tile_lines(table, quads, levels, side):
    channels = quads.shape[1] // levels * 2 * levels
    vmem = pl.BlockSpec(memory_space=pltpu.VMEM)
    line = jax.ShapeDtypeStruct((channels, LANES), jnp.float32)
    return pl.pallas_call(
        functools.partial(lines_kernel, levels, side),
        out_shape=[line] * 4 + [jax.ShapeDtypeStruct((levels, LANES), jnp.float32)],
        in_specs=[pl.BlockSpec(memory_space=pltpu.SMEM), vmem],
        out_specs=[vmem] * 5,
        compiler_params=pltpu.CompilerParams(vmem_limit_bytes=VMEM_LIMIT),
        name="tile_lines",
    )(table, quads)


def line_kernel(
    levels,
    low_ref,
    high_ref,
    low_in_ref,
    high_in_ref,
    below_ref,
    above_ref,
    west_ref,
    east_ref,
    phys_ref,
    low_out_ref,
    high_out_ref,
    coef_ref,
    moved_ref,
    ends_ref,
):
    channels = low_ref.shape[0]
    tracer_count = channels // levels
    level_tiles = levels // SUB
    lane = lane_ids()
    odd = (lane & 1) == 1
    spans = [slice(0, LANES), slice(LANES, 2 * LANES)]
    flag_row = 6 * levels
    lines = (
        (low_ref, low_in_ref, below_ref, low_out_ref),
        (high_ref, above_ref, high_in_ref, high_out_ref),
    )

    def flag(f, h):
        return phys_ref[flag_row + f : flag_row + f + 1, spans[h]]

    above_mix = [jnp.zeros((SUB, LANES), jnp.float32)] * 2
    for lt in range(level_tiles):
        at = slice(lt * SUB, (lt + 1) * SUB)
        from_west = west_ref[lt * SUB : (lt + 1) * SUB, :]
        from_east = east_ref[lt * SUB : (lt + 1) * SUB, :]
        ends_ref[at, :] = jnp.where(odd, turned(from_east, -2), from_west)
        for h in range(2):
            faces = [
                phys_ref[n * levels + lt * SUB : n * levels + (lt + 1) * SUB, spans[h]] for n in (0, 1, 4, 5)
            ]
            set_transport(coef_ref, at, spans[h], faces, [flag(f, h) for f in range(4)])
            mix = phys_ref[3 * levels + lt * SUB : 3 * levels + (lt + 1) * SUB, spans[h]]
            set_mixing(coef_ref, at, spans[h], mix, above_mix[h], lt == level_tiles - 1)
            above_mix[h] = mix
    set_blank(moved_ref, channels)

    def advect(lt, carry):
        at = pl.multiple_of(lt * SUB, SUB)
        ends = ends_ref[pl.ds(at, SUB), :]
        for h in range(2):
            here_ref, north_ref, south_ref, _ = lines[h]
            c, e, w, n, s = (coef_ref[k, pl.ds(at, SUB), spans[h]] for k in range(5))
            for t in range(tracer_count):
                chan = pl.multiple_of(t * levels + lt * SUB, SUB)
                here = here_ref[pl.ds(chan, SUB), :]
                end = turned(ends, -2 * (2 * t + h))
                west = jnp.where(lane == 0, end, turned(here, 1))
                east = jnp.where(lane == LANES - 1, end, turned(here, -1))
                moved_ref[pl.ds(pl.multiple_of(SUB + chan, SUB), SUB), spans[h]] = (
                    c * here
                    + (e * east + w * west)
                    + (n * north_ref[pl.ds(chan, SUB), :] + s * south_ref[pl.ds(chan, SUB), :])
                )
        return carry

    lax.fori_loop(0, level_tiles, advect, 0, unroll=True)

    def store(t, at, h, value):
        if t is not None:
            lines[h][3][pl.ds(at, SUB), :] = value

    def warm_at(lt, h):
        return phys_ref[pl.ds(pl.multiple_of(2 * levels + lt * SUB, SUB), SUB), spans[h]]

    light = [flag(LIGHT, h) for h in range(2)]
    wet = [flag(WET, h) for h in range(2)]
    mix_and_react(levels, tracer_count, spans, moved_ref, coef_ref, light, wet, warm_at, store)


def line_step(low, high, low_in, high_in, below, above, from_west, from_east, phys, levels):
    channels = low.shape[0]
    vmem = pl.BlockSpec(memory_space=pltpu.VMEM)
    f32 = jnp.float32
    line = jax.ShapeDtypeStruct((channels, LANES), f32)
    return pl.pallas_call(
        functools.partial(line_kernel, levels),
        out_shape=[line, line],
        in_specs=[vmem] * 9,
        out_specs=[vmem, vmem],
        scratch_shapes=[
            pltpu.VMEM((8, levels, 2 * LANES), f32),
            pltpu.VMEM((channels + 2 * SUB, 2 * LANES), f32),
            pltpu.VMEM((levels, LANES), f32),
        ],
        compiler_params=pltpu.CompilerParams(vmem_limit_bytes=VMEM_LIMIT),
        name="line_step",
    )(low, high, low_in, high_in, below, above, from_west, from_east, phys)


def hand_kernel(levels, side, table_ref, below_ref, above_ref, *refs):
    out_ref = refs[-1]
    group = LANES // side
    rounds = below_ref.shape[0] // levels // group
    half = group // 2

    def body(lt, carry):
        for i in range(rounds):
            for part in range(2):
                lines = []
                for g in range(half):
                    t = i * group + part * half + g
                    chan = pl.ds(pl.multiple_of(t * levels + lt * SUB, SUB), SUB)
                    lines += [above_ref[chan, :], below_ref[chan, :]]
                row = pl.multiple_of((part * rounds + i) * levels + lt * SUB, SUB)
                for b, value in enumerate(regroup(lines, side)):
                    out_ref[table_ref[TILE_OWNER, b], pl.ds(row, SUB), :] = value
        return carry

    lax.fori_loop(0, levels // SUB, body, 0)


def hand_on(table, below, above, levels, side, *after):
    lon_count = lax.axis_size("lon")
    rows = 2 * below.shape[0] * side // LANES
    vmem = pl.BlockSpec(memory_space=pltpu.VMEM)
    return pl.pallas_call(
        functools.partial(hand_kernel, levels, side),
        out_shape=jax.ShapeDtypeStruct((lon_count, rows, LANES), jnp.float32),
        in_specs=[pl.BlockSpec(memory_space=pltpu.SMEM), vmem, vmem]
        + [pl.BlockSpec(memory_space=pl.ANY)] * len(after),
        out_specs=vmem,
        compiler_params=pltpu.CompilerParams(vmem_limit_bytes=VMEM_LIMIT),
        name="hand_on",
    )(table, below, above, *after)


def gate_kernel(*refs):
    pass


def gate(values, *others):
    anywhere = pl.BlockSpec(memory_space=pl.ANY)
    count = len(values)
    return pl.pallas_call(
        gate_kernel,
        out_shape=[jax.ShapeDtypeStruct(x.shape, x.dtype) for x in values],
        in_specs=[anywhere] * (count + len(others)),
        out_specs=[anywhere] * count,
        input_output_aliases={i: i for i in range(count)},
        name="gate",
    )(*values, *others)


def heat_kernel(levels, side, factor, table_ref, chl_ref, light_ref, land_ref, widen_ref, out_ref, rows_ref, wide_ref):
    tile_blocks = land_ref.shape[1] // side
    halves = side * side // LANES
    group = LANES // side
    fine_cols = light_ref.shape[1]
    fine_rows = light_ref.shape[0]
    f32 = jnp.float32
    group_id = lane_ids() >> (side.bit_length() - 1)

    def place(lt, carry):
        at = pl.multiple_of(lt * SUB, SUB)
        for h in range(halves):
            blocks = []
            for b in range(tile_blocks):
                owner = table_ref[TILE_OWNER, b]
                values = chl_ref[owner, pl.ds(at, SUB), h * LANES : (h + 1) * LANES]
                blocks.append(jnp.where(table_ref[TILE_WET, b] == 1, values, 0.0))
            for r in range(group):
                line = None
                for b in range(tile_blocks):
                    piece = turned(blocks[b], side * (b - r))
                    line = piece if line is None else jnp.where(group_id == b, piece, line)
                rows_ref[pl.ds(pl.multiple_of((h * group + r) * levels + lt * SUB, SUB), SUB), :] = line
        return carry

    lax.fori_loop(0, levels // SUB, place, 0)
    wet = land_ref[...].astype(f32)
    widen = widen_ref[...]
    above = jnp.zeros_like(wet)
    passing = jnp.ones_like(wet)
    for l in range(levels):
        chl = rows_ref[pl.ds(l, side, stride=levels), :]
        above = above + (0.04 + 0.02 * chl)
        through = jnp.exp(-above)
        kept = (passing - through) * wet
        passing = through
        high = kept.astype(jnp.bfloat16)
        low = (kept - high.astype(f32)).astype(jnp.bfloat16)
        wide_ref[l * side : (l + 1) * side, :] = jnp.dot(
            high, widen, preferred_element_type=f32
        ) + jnp.dot(low, widen, preferred_element_type=f32)

    sub = lax.broadcasted_iota(jnp.int32, (SUB, LANES), 0)
    sources = []
    for m in range(fine_rows // SUB):
        start = (m * SUB // factor) // SUB * SUB
        index = jnp.zeros_like(sub)
        for r in range(1, side):
            index = index + jnp.where(sub + m * SUB >= r * factor, 1, 0)
        sources.append((start, index - start))

    def spread(l, carry):
        for c in range(fine_cols // LANES):
            span = slice(c * LANES, (c + 1) * LANES)
            for m in range(0, fine_rows // SUB, 2):
                both = []
                for n in (m, m + 1):
                    start, index = sources[n]
                    lines = wide_ref[pl.ds(pl.multiple_of(l * side + start, SUB), SUB), span]
                    lines = jnp.take_along_axis(lines, index, axis=0)
                    both.append(lines * light_ref[n * SUB : (n + 1) * SUB, span])
                out_ref[l, m * SUB : (m + 2) * SUB, span] = jnp.concatenate(both, axis=0).astype(jnp.bfloat16)
        return carry

    lax.fori_loop(0, levels, spread, 0)


def heat(table, chl, light, land, levels, widen):
    side = land.shape[0]
    factor = light.shape[0] // side
    vmem = pl.BlockSpec(memory_space=pltpu.VMEM)
    return pl.pallas_call(
        functools.partial(heat_kernel, levels, side, factor),
        out_shape=jax.ShapeDtypeStruct((levels,) + light.shape, jnp.bfloat16),
        in_specs=[pl.BlockSpec(memory_space=pltpu.SMEM), vmem, vmem, vmem, vmem],
        out_specs=vmem,
        scratch_shapes=[
            pltpu.VMEM((side * levels, LANES), jnp.float32),
            pltpu.VMEM((side * levels, light.shape[1]), jnp.float32),
        ],
        compiler_params=pltpu.CompilerParams(vmem_limit_bytes=VMEM_LIMIT),
        name="heat",
    )(table, chl, light, land, widen)


def widened(x, rows, width):
    return jnp.pad(x, ((0, rows - x.shape[0]), (0, width - x.shape[1])))


def on_device(tracers, phys_fine, mix_coarse, surf_light, land_mask, owner_map):
    f32 = jnp.float32
    slot_count = tracers.shape[0]
    side = land_mask.shape[0]
    levels = mix_coarse.shape[2]
    tile_blocks = land_mask.shape[1] // side
    factor = phys_fine.shape[0] // side
    fine_cols = phys_fine.shape[1]
    group = LANES // side

    fine = jnp.transpose(phys_fine, (0, 2, 1))
    mix = jnp.transpose(mix_coarse, (0, 2, 1))
    wet = land_mask.astype(f32)
    width = fine_cols

    northward = jnp.concatenate(
        [
            widened(fine[-1, levels : 2 * levels, :].astype(f32), levels, width),
            widened(wet[-1:], 1, width),
        ],
        axis=0,
    )
    southward = widened(wet[:1], 1, width)
    last_face = jnp.mean(
        fine[:, :levels, fine_cols - 1].astype(f32).reshape(side, factor, levels), axis=1
    )
    face_pack = jnp.pad(
        last_face.reshape(side // group, group, levels // SUB, SUB).transpose(3, 1, 0, 2),
        ((0, 0), (0, 0), (0, 0), (0, group - levels // SUB)),
    ).reshape(SUB, LANES)
    eastward = jnp.concatenate([face_pack, widened(wet[:, -1][None], 1, LANES)], axis=0)
    westward = widened(wet[:, 0][None], 1, LANES)

    from_south = lax.ppermute(northward, "lat", along("lat", 1, False))
    from_north = lax.ppermute(southward, "lat", along("lat", -1, False))
    from_west = lax.ppermute(eastward, "lon", along("lon", 1, True))
    from_east = lax.ppermute(westward, "lon", along("lon", -1, True))

    fine_id = jnp.arange(fine_cols)[:, None]
    coarse_id = jnp.arange(land_mask.shape[1])[None, :]
    member = (fine_id // factor == coarse_id).astype(jnp.bfloat16)
    final = (fine_id == factor * coarse_id + factor - 1).astype(jnp.bfloat16)
    picks = jnp.concatenate([final, member], axis=1)

    table = routing(owner_map, slot_count, tile_blocks)
    def to_north(x):
        return lax.ppermute(x, "lat", along("lat", 1, False))

    def to_south(x):
        return lax.ppermute(x, "lat", along("lat", -1, False))

    def to_east(x):
        return lax.ppermute(x, "lon", along("lon", 1, True))

    def to_west(x):
        return lax.ppermute(x, "lon", along("lon", -1, True))

    def across(x):
        return lax.all_to_all(x, "lon", 0, 0, tiled=True)

    quads, west, east = first_edges(table, tracers, levels, side)
    quads = across(quads)
    rows = coarse_rows(fine, mix, picks)
    phys, line_phys = coarsen(
        table, rows, surf_light, land_mask, from_south, from_north, from_west, from_east, picks
    )
    phys = across(phys)
    low, high, low_in, high_in, ends = tile_lines(table, quads, levels, side)
    below, above = to_north(high), to_south(low)
    west, east = gate((west, east), phys)
    rim_w, rim_e = to_east(east), to_west(west)
    ends_w, ends_e = to_east(ends), to_west(ends)
    rims = across(hand_on(table, below, above, levels, side, phys, ends_w, ends_e))
    new_low, new_high = line_step(
        low, high, low_in, high_in, below, above, ends_w, ends_e, line_phys, levels
    )
    below, above = to_north(new_high), to_south(new_low)
    new_rims = across(hand_on(table, below, above, levels, side, rims, rim_w, rim_e))
    current, west, east = step(table, tracers, phys, rims, rim_w, rim_e, levels, side, False)
    current, chl = step(table, current, phys, new_rims, to_east(east), to_west(west), levels, side, True)
    chl = lax.all_to_all(chl, "lon", 0, 0, tiled=True)
    heating = heat(table, chl, surf_light, land_mask, levels, jnp.transpose(member))
    return current, heating


def solution(mesh):
    in_specs = (
        P(("lat", "lon"), None, None),
        P("lat", "lon", None),
        P("lat", "lon", None),
        P("lat", "lon"),
        P("lat", "lon"),
        P("lat", None),
    )
    out_specs = (P(("lat", "lon"), None, None), P(None, "lat", "lon"))
    return jax.shard_map(
        on_device, mesh=mesh, in_specs=in_specs, out_specs=out_specs, check_vma=False
    )
```

```python
import functools

import jax
import jax.numpy as jnp
from jax import lax
from jax.experimental import pallas as pl
from jax.experimental.pallas import tpu as pltpu
from jax.sharding import PartitionSpec as P

LANES = 128
SUB = 8

diffuse_rate = 0.08
nano_chl_index = 10
diat_chl_index = 11

SLOT_TILE, SLOT_FULL, SLOT_WEST, SLOT_EAST, TILE_OWNER, TILE_WET, TILE_BASE = range(7)
TABLE_ROWS = 8

OPEN_EAST, OPEN_NORTH, OPEN_WEST, OPEN_SOUTH, LIGHT, WET = range(6)

VMEM_LIMIT = 48 * 1024 * 1024


def positive(value):
    return jnp.maximum(value, 0.0)


def lane_ids(rows=SUB):
    return lax.broadcasted_iota(jnp.int32, (rows, LANES), 1)


def turned(value, by):
    by = by % LANES
    return value if by == 0 else pltpu.roll(value, by, 1)


def quotient(value, by):
    if by & (by - 1) == 0:
        return lax.shift_right_logical(value, jnp.int32(by.bit_length() - 1))
    return lax.div(value, jnp.int32(by))


def remainder(value, by):
    if by & (by - 1) == 0:
        return value & (by - 1)
    return lax.rem(value, jnp.int32(by))


def along(axis, by, closed):
    size = lax.axis_size(axis)
    pairs = [(i, (i + by) % size) for i in range(size)]
    return [p for p in pairs if closed or p[1] == p[0] + by]


def table_kernel(slot_count, tile_blocks, lon_count, row_ref, out_ref, used_ref):
    me = lax.axis_index("lon")
    block_count = row_ref.shape[1]
    width = out_ref.shape[1]

    def clear(i, carry):
        for r in range(TABLE_ROWS):
            out_ref[r, i] = 0
        return carry

    lax.fori_loop(0, width, clear, 0)

    def unuse(i, carry):
        used_ref[0, i] = 0
        used_ref[1, i] = 0
        return carry

    lax.fori_loop(0, lon_count, unuse, 0)
    out_ref[TILE_BASE, 0] = me * tile_blocks

    def visit(k, carry):
        code = row_ref[0, k]
        safe = jnp.maximum(code, 0)
        owner = remainder(quotient(safe, slot_count), lon_count)
        slot = remainder(safe, slot_count)
        tile = quotient(k, tile_blocks)

        @pl.when((code >= 0) & (owner == me))
        def _():
            west = row_ref[0, remainder(k + block_count - 1, block_count)]
            east = row_ref[0, remainder(k + 1, block_count)]
            out_ref[SLOT_TILE, slot] = tile
            out_ref[SLOT_FULL, slot] = 1
            out_ref[SLOT_WEST, slot] = remainder(jnp.maximum(west, 0), slot_count)
            out_ref[SLOT_EAST, slot] = remainder(jnp.maximum(east, 0), slot_count)
            used_ref[0, tile] = 1

        @pl.when((code >= 0) & (tile == me))
        def _():
            local = remainder(k, tile_blocks)
            out_ref[TILE_OWNER, local] = owner
            out_ref[TILE_WET, local] = 1
            used_ref[1, owner] = 1

        return carry

    lax.fori_loop(0, block_count, visit, 0, unroll=4)

    def give(target, filled, line, count):
        def one(i, carry):
            def look(j, done):
                take = (done == 0) & (used_ref[line, j] == 0)

                @pl.when(take)
                def _():
                    out_ref[target, i] = j
                    used_ref[line, j] = 1

                return jnp.where(take, 1, done)

            @pl.when(out_ref[filled, i] == 0)
            def _():
                lax.fori_loop(0, lon_count, look, 0)

            return carry

        lax.fori_loop(0, count, one, 0)

    give(SLOT_TILE, SLOT_FULL, 0, slot_count)
    give(TILE_OWNER, TILE_WET, 1, tile_blocks)


def routing(row, slot_count, tile_blocks):
    lon_count = lax.axis_size("lon")
    width = max(slot_count, tile_blocks, lon_count)
    return pl.pallas_call(
        functools.partial(table_kernel, slot_count, tile_blocks, lon_count),
        out_shape=jax.ShapeDtypeStruct((TABLE_ROWS, width), jnp.int32),
        in_specs=[pl.BlockSpec(memory_space=pltpu.SMEM)],
        out_specs=pl.BlockSpec(memory_space=pltpu.SMEM),
        scratch_shapes=[pltpu.SMEM((2, lon_count), jnp.int32)],
        name="routing",
    )(row)


def merged(pieces, ids):
    packed = pieces[0]
    for g in range(1, len(pieces)):
        packed = jnp.where(ids == g, pieces[g], packed)
    return packed


def pack_columns(first, second, side):
    lane = lane_ids()
    odd = (lane & 1) == 1
    here = (lane & (side - 1)) >> 1
    there = ((lane + 1) & (side - 1)) >> 1
    even_ends = merged([turned(v, 1 + 2 * g) for g, v in enumerate(first)], here)
    odd_ends = merged([turned(v, 2 * g) for g, v in enumerate(second)], there)
    return jnp.where(odd, even_ends, odd_ends), jnp.where(odd, odd_ends, even_ends)


def pack_quads(first, second, side):
    low = lane_ids() < LANES // 2
    both = [jnp.where(low, a, b) for a, b in zip(first, second)]
    turns = [turned(v, 2 * side + (g % 2) * (LANES // 2)) for g, v in enumerate(both)]
    return [jnp.where(low, turns[g], turns[g + 1]) for g in range(0, len(turns), 2)]


def regroup(values, side):
    values = list(values)
    ids = lane_ids() >> (side.bit_length() - 1)
    bit = 1
    while bit < len(values):
        keep = (ids & bit) == 0
        for n in range(len(values)):
            if n & bit == 0:
                a, b = values[n], values[n + bit]
                values[n] = jnp.where(keep, a, turned(b, side * bit))
                values[n + bit] = jnp.where(keep, turned(a, -side * bit), b)
        bit *= 2
    return values


def edges_kernel(levels, side, table_ref, cell_ref, rows_ref, west_ref, east_ref):
    group = LANES // side
    rounds = cell_ref.shape[1] // levels // group
    level_tiles = levels // SUB

    def body(lt, carry):
        for i in range(rounds):
            row = pl.multiple_of(i * levels + lt * SUB, SUB)
            first, second = [], []
            for g in range(group):
                at = pl.multiple_of((i * group + g) * levels + lt * SUB, SUB)
                first.append(cell_ref[0, pl.ds(at, SUB), 0:LANES])
                second.append(cell_ref[0, pl.ds(at, SUB), LANES : 2 * LANES])
            west, east = pack_columns(first, second, side)
            west_ref[0, pl.ds(row, SUB), :] = west
            east_ref[0, pl.ds(row, SUB), :] = east
            for n, quad in enumerate(pack_quads(first, second, side)):
                at = pl.multiple_of((i * (group // 2) + n) * levels + lt * SUB, SUB)
                rows_ref[0, pl.ds(at, SUB), :] = quad
        return carry

    lax.fori_loop(0, level_tiles, body, 0, unroll=True)


def first_edges(table, tracers, levels, side):
    slot_count, channels, cell_count = tracers.shape
    lon_count = lax.axis_size("lon")
    rows = channels * side // LANES
    f32 = jnp.float32
    by_slot = pl.BlockSpec((1, rows, LANES), lambda s, t: (s, 0, 0))
    return pl.pallas_call(
        functools.partial(edges_kernel, levels, side),
        out_shape=[
            jax.ShapeDtypeStruct((lon_count, 4 * rows, LANES), f32),
            jax.ShapeDtypeStruct((slot_count, rows, LANES), f32),
            jax.ShapeDtypeStruct((slot_count, rows, LANES), f32),
        ],
        grid_spec=pltpu.PrefetchScalarGridSpec(
            num_scalar_prefetch=1,
            grid=(slot_count,),
            in_specs=[pl.BlockSpec((1, channels, cell_count), lambda s, t: (s, 0, 0))],
            out_specs=[
                pl.BlockSpec((1, 4 * rows, LANES), lambda s, t: (t[SLOT_TILE, s], 0, 0)),
                by_slot,
                by_slot,
            ],
        ),
        compiler_params=pltpu.CompilerParams(vmem_limit_bytes=VMEM_LIMIT),
        name="first_edges",
    )(table, tracers)


def react(mixed, par_light, warm_factor):
    (
        carbon_dis,
        alkalinity,
        oxygen,
        nitrate,
        ammonium,
        phosphate,
        silicate,
        iron_free,
        nano_carbon,
        diat_carbon,
        nano_chl,
        diat_chl,
        nano_iron,
        diat_iron,
        diat_silica,
        micro_zoo,
        meso_zoo,
        dissolved_org,
        small_part,
        big_part,
        small_iron,
        big_iron,
        big_silica,
        calcite,
    ) = mixed
    nitrogen = positive(nitrate) + positive(ammonium)
    limit_nitro = nitrogen / (0.5 + nitrogen)
    limit_phos = positive(phosphate) / (0.3 + positive(phosphate))
    limit_iron = positive(iron_free) / (0.2 + positive(iron_free))
    limit_sil = positive(silicate) / (1.0 + positive(silicate))
    nutr_nano = jnp.minimum(jnp.minimum(limit_nitro, limit_phos), limit_iron)
    nutr_diat = jnp.minimum(nutr_nano, limit_sil)
    lit = warm_factor * par_light
    prod_nano = 0.1 * lit / (par_light + 0.5) * nutr_nano * nano_carbon
    prod_diat = 0.12 * lit / (par_light + 1.0) * nutr_diat * diat_carbon
    ammon_share = (positive(ammonium) + 0.01) / (nitrogen + 0.02)
    graze_nano = 0.08 * warm_factor * micro_zoo / (1.0 + positive(nano_carbon))
    graze_diat = 0.06 * warm_factor * meso_zoo / (1.0 + positive(diat_carbon))
    loss_nano = graze_nano + 0.02
    loss_diat = graze_diat + 0.02
    eaten_nano = graze_nano * nano_carbon
    eaten_diat = graze_diat * diat_carbon
    death_micro = 0.03 * micro_zoo * positive(micro_zoo)
    death_meso = 0.03 * meso_zoo * positive(meso_zoo)
    remin_doc = 0.03 * warm_factor * dissolved_org
    remin_poc = 0.02 * warm_factor * small_part
    remin_goc = 0.01 * warm_factor * big_part
    nitrify = 0.05 * ammonium
    melt_si = 0.02 * big_silica
    melt_cal = 0.01 * calcite
    melt_sfe = 0.02 * small_iron
    melt_bfe = 0.01 * big_iron
    uptake = prod_nano + prod_diat
    remin_total = remin_doc + remin_poc + remin_goc
    calcify = 0.02 * prod_nano
    gained = remin_total - uptake
    shell = melt_cal - calcify
    by_ammon = ammon_share * uptake
    by_nitrate = 0.16 * (uptake - by_ammon - nitrify)
    return [
        carbon_dis + gained + shell,
        alkalinity + 2.0 * shell + by_nitrate,
        oxygen - 1.3 * gained - 0.32 * nitrify,
        nitrate - by_nitrate,
        ammonium + 0.16 * (remin_total - by_ammon - nitrify),
        phosphate + 0.01 * gained,
        silicate + melt_si - 0.15 * prod_diat,
        iron_free + melt_sfe + melt_bfe - 0.005 * uptake,
        nano_carbon + prod_nano - loss_nano * nano_carbon,
        diat_carbon + prod_diat - loss_diat * diat_carbon,
        nano_chl + 0.03 * prod_nano - loss_nano * nano_chl,
        diat_chl + 0.03 * prod_diat - loss_diat * diat_chl,
        nano_iron + 0.005 * prod_nano - loss_nano * nano_iron,
        diat_iron + 0.005 * prod_diat - loss_diat * diat_iron,
        diat_silica + 0.15 * prod_diat - loss_diat * diat_silica,
        micro_zoo + 0.3 * eaten_nano - death_micro,
        meso_zoo + 0.3 * eaten_diat - death_meso,
        dissolved_org + 0.3 * eaten_nano + 0.02 * nano_carbon - remin_doc,
        small_part + 0.4 * eaten_nano + death_micro - remin_poc,
        big_part + 0.4 * eaten_diat + 0.02 * diat_carbon + death_meso - remin_goc,
        small_iron + loss_nano * nano_iron - melt_sfe,
        big_iron + loss_diat * diat_iron - melt_bfe,
        big_silica + loss_diat * diat_silica - melt_si,
        calcite + calcify - melt_cal,
    ]


def transport(faces, opens):
    flow_e, flow_n, flow_w, flow_s = (face * is_open for face, is_open in zip(faces, opens))
    open_e, open_n, open_w, open_s = opens
    out_e, in_e = jnp.maximum(flow_e, 0.0), jnp.minimum(flow_e, 0.0)
    out_n, in_n = jnp.maximum(flow_n, 0.0), jnp.minimum(flow_n, 0.0)
    in_w, out_w = jnp.maximum(flow_w, 0.0), jnp.minimum(flow_w, 0.0)
    in_s, out_s = jnp.maximum(flow_s, 0.0), jnp.minimum(flow_s, 0.0)
    drift = diffuse_rate * (open_w + open_e + open_s + open_n)
    return (
        1.0 - (out_e - out_w) - (out_n - out_s) - drift,
        diffuse_rate * open_e - in_e,
        diffuse_rate * open_w + in_w,
        diffuse_rate * open_n - in_n,
        diffuse_rate * open_s + in_s,
    )


def set_mixing(coef_ref, at, span, mix, above, bottom):
    sub = lax.broadcasted_iota(jnp.int32, (SUB, LANES), 0)
    mix_up = pltpu.roll(jnp.where(sub == SUB - 1, above, mix), 1, 0)
    if bottom:
        mix = jnp.where(sub == SUB - 1, 0.0, mix)
    coef_ref[5, at, span] = 1.0 - mix - mix_up
    coef_ref[6, at, span] = mix
    coef_ref[7, at, span] = mix_up


def set_blank(moved_ref, channels):
    blank = jnp.zeros((SUB, moved_ref.shape[1]), jnp.float32)
    moved_ref[0:SUB, :] = blank
    moved_ref[SUB + channels : 2 * SUB + channels, :] = blank


def mix_and_react(levels, tracer_count, spans, moved_ref, coef_ref, light, wet, warm_at, store):
    sub = lax.broadcasted_iota(jnp.int32, (SUB, LANES), 0)

    def reacting(lt, carry):
        at = pl.multiple_of(lt * SUB, SUB)
        depths = []
        halves_new = []
        for h, span in enumerate(spans):
            mix_c, mix_d, mix_u = (coef_ref[n, pl.ds(at, SUB), span] for n in (5, 6, 7))
            mixed = []
            for t in range(tracer_count):
                base = t * levels + lt * SUB
                before = moved_ref[pl.ds(pl.multiple_of(base, SUB), SUB), span]
                now = moved_ref[pl.ds(pl.multiple_of(base + SUB, SUB), SUB), span]
                after = moved_ref[pl.ds(pl.multiple_of(base + 2 * SUB, SUB), SUB), span]
                up = pltpu.roll(jnp.where(sub == SUB - 1, before, now), 1, 0)
                down = pltpu.roll(jnp.where(sub == 0, after, now), SUB - 1, 0)
                mixed.append(mix_c * now + mix_d * down + mix_u * up)
            absorb = 0.04 + 0.02 * (positive(mixed[nano_chl_index]) + positive(mixed[diat_chl_index]))
            total = absorb
            for by in (1, 2, 4):
                total = total + jnp.where(sub >= by, pltpu.roll(total, by, 0), 0.0)
            above = carry[h] + (total - absorb)
            depths.append(carry[h] + total[SUB - 1 : SUB, :])
            par_light = light[h] * jnp.exp(-(above + 0.5 * absorb))
            halves_new.append([value * wet[h] for value in react(mixed, par_light, warm_at(lt, h))])
            for t in range(tracer_count):
                store(t, pl.multiple_of(t * levels + lt * SUB, SUB), h, halves_new[h][t])
        store(None, lt, None, halves_new)
        return tuple(depths)

    start = tuple(jnp.zeros((1, LANES), jnp.float32) for _ in spans)
    lax.fori_loop(0, levels // SUB, reacting, start, unroll=True)


def block_faces(phys_ref, spans, levels, side, lt):
    group = LANES // side
    pack_at = 4 * levels + SUB
    lane = lane_ids()
    first_col = (lane & (side - 1)) == 0
    first_row = lane < side
    west_pack = phys_ref[0, pack_at : pack_at + SUB, spans[0]]
    south_pack = phys_ref[0, pack_at : pack_at + SUB, spans[1]]
    east = [phys_ref[0, lt * SUB : (lt + 1) * SUB, span] for span in spans]
    north = [phys_ref[0, levels + lt * SUB : levels + (lt + 1) * SUB, span] for span in spans]
    faces = []
    for h in range(len(spans)):
        west = jnp.where(first_col, turned(west_pack, -(h * group + lt)), turned(east[h], 1))
        before = turned(south_pack, -side * lt) if h == 0 else turned(north[h - 1], side)
        south = jnp.where(first_row, before, turned(north[h], side))
        faces.append((east[h], north[h], west, south))
    return faces


def inner_kernel(levels, side, table_ref, cell_ref, phys_ref, out_ref, coef_ref):
    channels, cell_count = cell_ref.shape[1:]
    tracer_count = channels // levels
    halves = cell_count // LANES
    level_tiles = levels // SUB
    spans = [slice(h * LANES, (h + 1) * LANES) for h in range(halves)]
    full = table_ref[SLOT_FULL, pl.program_id(0)] == 1

    @pl.when(jnp.logical_not(full))
    def _():
        out_ref[...] = jnp.zeros_like(out_ref)

    @pl.when(full)
    def _():
        lane = lane_ids()
        col = lane & (side - 1)
        first_row = lane < side
        last_row = lane >= LANES - side
        flag_row = 4 * levels

        def flag(f, h):
            return phys_ref[0, flag_row + f : flag_row + f + 1, spans[h]]

        for lt in range(level_tiles):
            at = slice(lt * SUB, (lt + 1) * SUB)
            for h, faces in enumerate(block_faces(phys_ref, spans, levels, side, lt)):
                c, e, w, n, s = transport(faces, [flag(f, h) for f in range(4)])
                e = jnp.where(col == side - 1, 0.0, e)
                w = jnp.where(col == 0, 0.0, w)
                if h == halves - 1:
                    n = jnp.where(last_row, 0.0, n)
                if h == 0:
                    s = jnp.where(first_row, 0.0, s)
                for k, value in enumerate((c, e, w, n, s)):
                    coef_ref[k, at, spans[h]] = value

        def advect(lt, carry):
            at = pl.multiple_of(lt * SUB, SUB)
            coef = [[coef_ref[n, pl.ds(at, SUB), span] for n in range(5)] for span in spans]
            for t in range(tracer_count):
                chan = pl.multiple_of(t * levels + lt * SUB, SUB)
                here = [cell_ref[0, pl.ds(chan, SUB), span] for span in spans]
                up = [turned(value, side) for value in here]
                down = [turned(value, -side) for value in here]
                for h in range(halves):
                    south = up[h] if h == 0 else jnp.where(first_row, up[h - 1], up[h])
                    north = down[h] if h == halves - 1 else jnp.where(last_row, down[h + 1], down[h])
                    c, e, w, n, s = coef[h]
                    out_ref[0, pl.ds(chan, SUB), spans[h]] = (
                        c * here[h]
                        + (e * turned(here[h], -1) + w * turned(here[h], 1))
                        + (n * north + s * south)
                    )
            return carry

        lax.fori_loop(0, level_tiles, advect, 0, unroll=True)


def inner(table, cells, phys, levels, side):
    slot_count, channels, cell_count = cells.shape
    phys_rows = phys.shape[1]
    by_slot = pl.BlockSpec((1, channels, cell_count), lambda s, t: (s, 0, 0))
    return pl.pallas_call(
        functools.partial(inner_kernel, levels, side),
        out_shape=jax.ShapeDtypeStruct(cells.shape, jnp.float32),
        grid_spec=pltpu.PrefetchScalarGridSpec(
            num_scalar_prefetch=1,
            grid=(slot_count,),
            in_specs=[
                by_slot,
                pl.BlockSpec((1, phys_rows, cell_count), lambda s, t: (t[SLOT_TILE, s], 0, 0)),
            ],
            out_specs=by_slot,
            scratch_shapes=[pltpu.VMEM((5, levels, cell_count), jnp.float32)],
        ),
        compiler_params=pltpu.CompilerParams(vmem_limit_bytes=VMEM_LIMIT),
        name="inner",
    )(table, cells, phys)


def step_kernel(levels, side, last, table_ref, part_ref, phys_ref, rim_ref, rim_w_ref, rim_e_ref, *refs):
    if last:
        out_ref, chl_ref, coef_ref, moved_ref, ends_ref = refs
        edge_refs = (chl_ref,)
    else:
        out_ref, west_ref, east_ref, coef_ref, moved_ref, ends_ref = refs
        edge_refs = (west_ref, east_ref)
    channels, cell_count = part_ref.shape[1:]
    tracer_count = channels // levels
    group = LANES // side
    halves = cell_count // LANES
    rounds = tracer_count // group
    level_tiles = levels // SUB
    rows = rounds * levels
    slot = pl.program_id(0)
    full = table_ref[SLOT_FULL, slot] == 1
    spans = [slice(h * LANES, (h + 1) * LANES) for h in range(halves)]

    @pl.when(jnp.logical_not(full))
    def _():
        out_ref[...] = jnp.zeros_like(out_ref)
        for ref in edge_refs:
            ref[...] = jnp.zeros_like(ref)

    @pl.when(full)
    def _():
        lane = lane_ids()
        col = lane & (side - 1)
        first_row = lane < side
        last_row = lane >= LANES - side
        odd = (lane & 1) == 1
        flag_row = 4 * levels

        def flag(f, h):
            return phys_ref[0, flag_row + f : flag_row + f + 1, spans[h]]

        above_mix = [jnp.zeros((SUB, LANES), jnp.float32)] * halves
        for lt in range(level_tiles):
            at = slice(lt * SUB, (lt + 1) * SUB)
            for h, faces in enumerate(block_faces(phys_ref, spans, levels, side, lt)):
                _, e, w, n, s = transport(faces, [flag(f, h) for f in range(4)])
                coef_ref[0, at, spans[h]] = jnp.where(col == 0, w, jnp.where(col == side - 1, e, 0.0))
                if h == 0:
                    coef_ref[1, at, spans[h]] = jnp.where(first_row, s, 0.0)
                if h == halves - 1:
                    coef_ref[1, at, spans[h]] = jnp.where(last_row, n, 0.0)
                mix = phys_ref[0, 3 * levels + lt * SUB : 3 * levels + (lt + 1) * SUB, spans[h]]
                set_mixing(coef_ref, at, spans[h], mix, above_mix[h], lt == level_tiles - 1)
                above_mix[h] = mix

        for at in range(0, rows, SUB):
            ends_ref[at : at + SUB, :] = turned(rim_w_ref[0, at : at + SUB, :], 2 - 2 * side)
        set_blank(moved_ref, channels)

        def gather(lt, carry):
            at = pl.multiple_of(lt * SUB, SUB)
            for i in range(rounds):
                row = pl.multiple_of(i * levels + lt * SUB, SUB)
                rims = [
                    rim_ref[0, pl.ds(row, SUB), :],
                    rim_ref[0, pl.ds(pl.multiple_of(rows + row, SUB), SUB), :],
                ]
                ends_w = ends_ref[pl.ds(row, SUB), :]
                ends_e = rim_e_ref[0, pl.ds(row, SUB), :]
                sides = [jnp.where(odd, ends_e, ends_w), jnp.where(odd, ends_w, ends_e)]
                for g in range(group):
                    chan = pl.multiple_of((i * group + g) * levels + lt * SUB, SUB)
                    rim = turned(rims[2 * g // group], -side - 2 * side * (g % (group // 2)))
                    for h in range(halves):
                        ends = turned(sides[h], side - 2 + h - 2 * g)
                        moved = part_ref[0, pl.ds(chan, SUB), spans[h]]
                        moved = moved + coef_ref[0, pl.ds(at, SUB), spans[h]] * ends
                        if h in (0, halves - 1):
                            moved = moved + coef_ref[1, pl.ds(at, SUB), spans[h]] * rim
                        moved_ref[pl.ds(pl.multiple_of(SUB + chan, SUB), SUB), spans[h]] = moved
            return carry

        lax.fori_loop(0, level_tiles, gather, 0, unroll=True)

        def store(t, at, h, value):
            if t is not None:
                out_ref[0, pl.ds(at, SUB), spans[h]] = value
            elif last:
                for k, new in enumerate(value):
                    chl_ref[0, pl.ds(pl.multiple_of(at * SUB, SUB), SUB), spans[k]] = positive(
                        new[nano_chl_index]
                    ) + positive(new[diat_chl_index])
            else:
                for i in range(rounds):
                    row = pl.multiple_of(i * levels + at * SUB, SUB)
                    first, second = (new[i * group : (i + 1) * group] for new in value)
                    west, east = pack_columns(first, second, side)
                    west_ref[0, pl.ds(row, SUB), :] = west
                    east_ref[0, pl.ds(row, SUB), :] = east

        def warm_at(lt, h):
            return phys_ref[0, pl.ds(pl.multiple_of(2 * levels + lt * SUB, SUB), SUB), spans[h]]

        light = [flag(LIGHT, h) for h in range(halves)]
        wet = [flag(WET, h) for h in range(halves)]
        mix_and_react(levels, tracer_count, spans, moved_ref, coef_ref, light, wet, warm_at, store)


def step(table, cells, phys, rims, rim_w, rim_e, levels, side, last):
    slot_count, channels, cell_count = cells.shape
    lon_count = lax.axis_size("lon")
    rows = channels * side // LANES
    phys_rows = phys.shape[1]
    f32 = jnp.float32
    by_slot = pl.BlockSpec((1, channels, cell_count), lambda s, t: (s, 0, 0))
    shapes = [jax.ShapeDtypeStruct(cells.shape, f32)]
    specs = [by_slot]
    if last:
        shapes.append(jax.ShapeDtypeStruct((lon_count, levels, cell_count), f32))
        specs.append(pl.BlockSpec((1, levels, cell_count), lambda s, t: (t[SLOT_TILE, s], 0, 0)))
    else:
        beside = jax.ShapeDtypeStruct((slot_count, rows, LANES), f32)
        shapes += [beside, beside]
        specs += [pl.BlockSpec((1, rows, LANES), lambda s, t: (s, 0, 0))] * 2
    return pl.pallas_call(
        functools.partial(step_kernel, levels, side, last),
        out_shape=shapes,
        grid_spec=pltpu.PrefetchScalarGridSpec(
            num_scalar_prefetch=1,
            grid=(slot_count,),
            in_specs=[
                by_slot,
                pl.BlockSpec((1, phys_rows, cell_count), lambda s, t: (t[SLOT_TILE, s], 0, 0)),
                pl.BlockSpec((1, 2 * rows, LANES), lambda s, t: (t[SLOT_TILE, s], 0, 0)),
                pl.BlockSpec((1, rows, LANES), lambda s, t: (t[SLOT_WEST, s], 0, 0)),
                pl.BlockSpec((1, rows, LANES), lambda s, t: (t[SLOT_EAST, s], 0, 0)),
            ],
            out_specs=specs,
            scratch_shapes=[
                pltpu.VMEM((8, levels, cell_count), f32),
                pltpu.VMEM((channels + 2 * SUB, cell_count), f32),
                pltpu.VMEM((rows, LANES), f32),
            ],
        ),
        compiler_params=pltpu.CompilerParams(vmem_limit_bytes=VMEM_LIMIT),
        name="step",
    )(table, cells, phys, rims, rim_w, rim_e)


def rows_kernel(levels, factor, fine_ref, mix_ref, pick_ref, rows_ref):
    f32 = jnp.float32
    picks = pick_ref[...]
    east_face = jnp.zeros((levels, LANES), f32)
    temp_mean = jnp.zeros((levels, LANES), f32)
    for r in range(factor):
        got = jnp.dot(fine_ref[r], picks, preferred_element_type=f32)
        east_face += got[0:levels, 0:LANES]
        temp_mean += got[2 * levels : 3 * levels, LANES : 2 * LANES]
        if r == factor - 1:
            north_face = got[levels : 2 * levels, LANES : 2 * LANES]
    rows_ref[0, 0:levels, :] = east_face * (1.0 / factor)
    rows_ref[0, levels : 2 * levels, :] = north_face * (1.0 / factor)
    rows_ref[0, 2 * levels : 3 * levels, :] = jnp.exp(0.0639 * (temp_mean * (1.0 / (factor * factor))))
    rows_ref[0, 3 * levels : 4 * levels, :] = mix_ref[0].astype(f32)


def coarse_rows(fine, mix, picks):
    side, levels, tile_cols = mix.shape
    factor = fine.shape[0] // side
    fine_cols = fine.shape[2]
    return pl.pallas_call(
        functools.partial(rows_kernel, levels, factor),
        out_shape=jax.ShapeDtypeStruct((side, 4 * levels, tile_cols), jnp.float32),
        grid=(side,),
        in_specs=[
            pl.BlockSpec((factor, 3 * levels, fine_cols), lambda i: (i, 0, 0)),
            pl.BlockSpec((1, levels, tile_cols), lambda i: (i, 0, 0)),
            pl.BlockSpec(picks.shape, lambda i: (0, 0)),
        ],
        out_specs=pl.BlockSpec((1, 4 * levels, tile_cols), lambda i: (i, 0, 0)),
        compiler_params=pltpu.CompilerParams(vmem_limit_bytes=VMEM_LIMIT),
        name="coarse_rows",
    )(fine, mix, picks)


def place_kernel(
    levels,
    side,
    factor,
    table_ref,
    rows_ref,
    light_ref,
    land_ref,
    south_ref,
    north_ref,
    west_ref,
    east_ref,
    pick_ref,
    out_ref,
    line_ref,
    flags_ref,
):
    tile_blocks = land_ref.shape[1] // side
    halves = side * side // LANES
    group = LANES // side
    fine_cols = light_ref.shape[1]
    f32 = jnp.float32
    picks = pick_ref[...]
    lane = lane_ids()
    group_id = lane >> (side.bit_length() - 1)
    col_id = lane & (side - 1)
    flag_row = 4 * levels
    pack_at = flag_row + SUB
    wet = land_ref[...].astype(f32)
    sides = wet.shape
    lane2 = lax.broadcasted_iota(jnp.int32, sides, 1)
    sub2 = lax.broadcasted_iota(jnp.int32, sides, 0)
    diagonal = lane2 == sub2
    rim_w = jnp.sum(jnp.where(diagonal, west_ref[SUB : SUB + 1, :], 0.0), axis=1, keepdims=True)
    rim_e = jnp.sum(jnp.where(diagonal, east_ref[0:1, :], 0.0), axis=1, keepdims=True)
    wet_w = jnp.where(lane2 == 0, rim_w, pltpu.roll(wet, 1, 1))
    wet_e = jnp.where(lane2 == LANES - 1, rim_e, pltpu.roll(wet, LANES - 1, 1))
    wet_s = jnp.where(sub2 == 0, south_ref[levels : levels + 1, 0:LANES], pltpu.roll(wet, 1, 0))
    wet_n = jnp.where(sub2 == side - 1, north_ref[0:1, 0:LANES], pltpu.roll(wet, side - 1, 0))
    fold_r = lax.broadcasted_iota(jnp.int32, (side, side * factor), 0)
    fold_c = lax.broadcasted_iota(jnp.int32, (side, side * factor), 1)
    fold_d = fold_c - factor * fold_r
    fold = jnp.where((fold_d >= 0) & (fold_d < factor), 1.0, 0.0)
    narrow = picks[:, LANES : 2 * LANES].astype(f32)
    light_rows = jnp.dot(fold, light_ref[...], precision=lax.Precision.HIGHEST, preferred_element_type=f32)
    light_mean = jnp.dot(
        light_rows, narrow, precision=lax.Precision.HIGHEST, preferred_element_type=f32
    ) * (1.0 / (factor * factor))
    flags = [wet * wet_e, wet * wet_n, wet * wet_w, wet * wet_s, light_mean, wet]
    for r in range(side):
        for f, value in enumerate(flags):
            flags_ref[r, f : f + 1, :] = value[r : r + 1, :]
        flags_ref[r, len(flags) : SUB, :] = jnp.zeros((SUB - len(flags), LANES), f32)

    def place(ref, frm, to):
        for h in range(halves):
            values = [ref[h * group + r, pl.ds(frm, SUB), :] for r in range(group)]
            for b, block in enumerate(regroup(values, side)):
                owner = table_ref[TILE_OWNER, b]
                out_ref[owner, pl.ds(to, SUB), h * LANES : (h + 1) * LANES] = block

    def place_four(q, carry):
        for n in range(4):
            at = pl.multiple_of(n * levels + q * SUB, SUB)
            place(rows_ref, at, at)
        return carry

    lax.fori_loop(0, levels // SUB, place_four, 0)
    place(flags_ref, 0, flag_row)

    fine_v = south_ref[0:levels, 0:fine_cols].astype(jnp.bfloat16)
    north_below = jnp.dot(fine_v, picks, preferred_element_type=f32)[:, LANES : 2 * LANES] * (1.0 / factor)
    for h, r in enumerate((0, side - 1)):
        span = slice(h * LANES, (h + 1) * LANES)
        line_ref[0 : 4 * levels, span] = rows_ref[r, 0 : 4 * levels, :]
        line_ref[6 * levels : 6 * levels + SUB, span] = flags_ref[r]
        line_ref[5 * levels : 6 * levels, span] = (
            north_below if h == 0 else rows_ref[r - 1, levels : 2 * levels, :]
        )
        from_lane = side * (r % group) + group * (r // group)
        for lt in range(levels // SUB):
            face = rows_ref[r, lt * SUB : (lt + 1) * SUB, :]
            line_ref[4 * levels + lt * SUB : 4 * levels + (lt + 1) * SUB, span] = jnp.where(
                lane == 0, turned(west_ref[0:SUB, :], -(from_lane + lt)), turned(face, 1)
            )
    for b in range(tile_blocks):
        owner = table_ref[TILE_OWNER, b]
        south_pack = jnp.zeros((SUB, LANES), f32)
        for lt in range(levels // SUB):
            piece = turned(north_below[lt * SUB : (lt + 1) * SUB, :], side * (lt - b))
            south_pack = jnp.where(group_id == lt, piece, south_pack)
        if b == 0:
            west_pack = west_ref[0:SUB, :]
        else:
            beside = table_ref[TILE_OWNER, b - 1]
            west_pack = jnp.zeros((SUB, LANES), f32)
            for h in range(halves):
                for lt in range(levels // SUB):
                    face = out_ref[beside, lt * SUB : (lt + 1) * SUB, h * LANES : (h + 1) * LANES]
                    piece = turned(face, h * group + lt - (side - 1))
                    west_pack = jnp.where(col_id == h * group + lt, piece, west_pack)
        out_ref[owner, pack_at : pack_at + SUB, 0:LANES] = west_pack
        out_ref[owner, pack_at : pack_at + SUB, LANES : 2 * LANES] = south_pack


def coarsen(table, rows, light, land, from_south, from_north, from_west, from_east, picks):
    lon_count = lax.axis_size("lon")
    side, tile_cols = land.shape
    levels = rows.shape[1] // 4
    factor = light.shape[0] // side
    phys_rows = 4 * levels + 2 * SUB
    f32 = jnp.float32
    vmem = pl.BlockSpec(memory_space=pltpu.VMEM)
    return pl.pallas_call(
        functools.partial(place_kernel, levels, side, factor),
        out_shape=[
            jax.ShapeDtypeStruct((lon_count, phys_rows, side * side), f32),
            jax.ShapeDtypeStruct((6 * levels + SUB, 2 * LANES), f32),
        ],
        in_specs=[pl.BlockSpec(memory_space=pltpu.SMEM)] + [vmem] * 8,
        out_specs=[vmem, vmem],
        scratch_shapes=[pltpu.VMEM((side, SUB, LANES), f32)],
        compiler_params=pltpu.CompilerParams(vmem_limit_bytes=VMEM_LIMIT),
        name="coarsen",
    )(table, rows, light, land, from_south, from_north, from_west, from_east, picks)


def lines_kernel(levels, side, table_ref, quad_ref, low_ref, high_ref, low_in_ref, high_in_ref, ends_ref):
    tile_blocks = LANES // side
    pairs = quad_ref.shape[1] // levels
    lane = lane_ids()
    spot = lane >> 1

    def body(lt, carry):
        packed = jnp.zeros((SUB, LANES), jnp.float32)
        for m in range(pairs):
            at = pl.multiple_of(m * levels + lt * SUB, SUB)
            blocks = []
            for b in range(tile_blocks):
                value = quad_ref[table_ref[TILE_OWNER, b], pl.ds(at, SUB), :]
                blocks.append(jnp.where(table_ref[TILE_WET, b] == 1, value, 0.0))
            parts = regroup(blocks, side)
            for p in range(2):
                t = 2 * m + p
                chan = pl.ds(pl.multiple_of(t * levels + lt * SUB, SUB), SUB)
                high_in, high, low, low_in = parts[4 * p : 4 * p + 4]
                low_ref[chan, :] = low
                high_ref[chan, :] = high
                low_in_ref[chan, :] = low_in
                high_in_ref[chan, :] = high_in
                for k, line in ((2 * t, low), (2 * t + 1, high)):
                    packed = jnp.where(spot == k, turned(line, 1 + 2 * k), packed)
        ends_ref[pl.ds(pl.multiple_of(lt * SUB, SUB), SUB), :] = packed
        return carry

    lax.fori_loop(0, levels // SUB, body, 0)


def tile_lines(table, quads, levels, side):
    channels = quads.shape[1] // levels * 2 * levels
    vmem = pl.BlockSpec(memory_space=pltpu.VMEM)
    line = jax.ShapeDtypeStruct((channels, LANES), jnp.float32)
    return pl.pallas_call(
        functools.partial(lines_kernel, levels, side),
        out_shape=[line] * 4 + [jax.ShapeDtypeStruct((levels, LANES), jnp.float32)],
        in_specs=[pl.BlockSpec(memory_space=pltpu.SMEM), vmem],
        out_specs=[vmem] * 5,
        compiler_params=pltpu.CompilerParams(vmem_limit_bytes=VMEM_LIMIT),
        name="tile_lines",
    )(table, quads)


def line_kernel(
    levels,
    low_ref,
    high_ref,
    low_in_ref,
    high_in_ref,
    below_ref,
    above_ref,
    west_ref,
    east_ref,
    phys_ref,
    low_out_ref,
    high_out_ref,
    coef_ref,
    moved_ref,
    ends_ref,
):
    channels = low_ref.shape[0]
    tracer_count = channels // levels
    level_tiles = levels // SUB
    lane = lane_ids()
    odd = (lane & 1) == 1
    spans = [slice(0, LANES), slice(LANES, 2 * LANES)]
    flag_row = 6 * levels
    lines = (
        (low_ref, low_in_ref, below_ref, low_out_ref),
        (high_ref, above_ref, high_in_ref, high_out_ref),
    )

    def flag(f, h):
        return phys_ref[flag_row + f : flag_row + f + 1, spans[h]]

    above_mix = [jnp.zeros((SUB, LANES), jnp.float32)] * 2
    for lt in range(level_tiles):
        at = slice(lt * SUB, (lt + 1) * SUB)
        from_west = west_ref[lt * SUB : (lt + 1) * SUB, :]
        from_east = east_ref[lt * SUB : (lt + 1) * SUB, :]
        ends_ref[at, :] = jnp.where(odd, turned(from_east, -2), from_west)
        for h in range(2):
            faces = [
                phys_ref[n * levels + lt * SUB : n * levels + (lt + 1) * SUB, spans[h]] for n in (0, 1, 4, 5)
            ]
            for n, value in enumerate(transport(faces, [flag(f, h) for f in range(4)])):
                coef_ref[n, at, spans[h]] = value
            mix = phys_ref[3 * levels + lt * SUB : 3 * levels + (lt + 1) * SUB, spans[h]]
            set_mixing(coef_ref, at, spans[h], mix, above_mix[h], lt == level_tiles - 1)
            above_mix[h] = mix
    set_blank(moved_ref, channels)

    def advect(lt, carry):
        at = pl.multiple_of(lt * SUB, SUB)
        ends = ends_ref[pl.ds(at, SUB), :]
        for h in range(2):
            here_ref, north_ref, south_ref, _ = lines[h]
            c, e, w, n, s = (coef_ref[k, pl.ds(at, SUB), spans[h]] for k in range(5))
            for t in range(tracer_count):
                chan = pl.multiple_of(t * levels + lt * SUB, SUB)
                here = here_ref[pl.ds(chan, SUB), :]
                end = turned(ends, -2 * (2 * t + h))
                west = jnp.where(lane == 0, end, turned(here, 1))
                east = jnp.where(lane == LANES - 1, end, turned(here, -1))
                moved_ref[pl.ds(pl.multiple_of(SUB + chan, SUB), SUB), spans[h]] = (
                    c * here
                    + (e * east + w * west)
                    + (n * north_ref[pl.ds(chan, SUB), :] + s * south_ref[pl.ds(chan, SUB), :])
                )
        return carry

    lax.fori_loop(0, level_tiles, advect, 0, unroll=True)

    def store(t, at, h, value):
        if t is not None:
            lines[h][3][pl.ds(at, SUB), :] = value

    def warm_at(lt, h):
        return phys_ref[pl.ds(pl.multiple_of(2 * levels + lt * SUB, SUB), SUB), spans[h]]

    light = [flag(LIGHT, h) for h in range(2)]
    wet = [flag(WET, h) for h in range(2)]
    mix_and_react(levels, tracer_count, spans, moved_ref, coef_ref, light, wet, warm_at, store)


def line_step(low, high, low_in, high_in, below, above, from_west, from_east, phys, levels):
    channels = low.shape[0]
    vmem = pl.BlockSpec(memory_space=pltpu.VMEM)
    f32 = jnp.float32
    line = jax.ShapeDtypeStruct((channels, LANES), f32)
    return pl.pallas_call(
        functools.partial(line_kernel, levels),
        out_shape=[line, line],
        in_specs=[vmem] * 9,
        out_specs=[vmem, vmem],
        scratch_shapes=[
            pltpu.VMEM((8, levels, 2 * LANES), f32),
            pltpu.VMEM((channels + 2 * SUB, 2 * LANES), f32),
            pltpu.VMEM((levels, LANES), f32),
        ],
        compiler_params=pltpu.CompilerParams(vmem_limit_bytes=VMEM_LIMIT),
        name="line_step",
    )(low, high, low_in, high_in, below, above, from_west, from_east, phys)


def hand_kernel(levels, side, table_ref, below_ref, above_ref, *refs):
    out_ref = refs[-1]
    group = LANES // side
    rounds = below_ref.shape[0] // levels // group
    half = group // 2

    def body(lt, carry):
        for i in range(rounds):
            for part in range(2):
                lines = []
                for g in range(half):
                    t = i * group + part * half + g
                    chan = pl.ds(pl.multiple_of(t * levels + lt * SUB, SUB), SUB)
                    lines += [above_ref[chan, :], below_ref[chan, :]]
                row = pl.multiple_of((part * rounds + i) * levels + lt * SUB, SUB)
                for b, value in enumerate(regroup(lines, side)):
                    out_ref[table_ref[TILE_OWNER, b], pl.ds(row, SUB), :] = value
        return carry

    lax.fori_loop(0, levels // SUB, body, 0)


def hand_on(table, below, above, levels, side, *after):
    lon_count = lax.axis_size("lon")
    rows = 2 * below.shape[0] * side // LANES
    vmem = pl.BlockSpec(memory_space=pltpu.VMEM)
    return pl.pallas_call(
        functools.partial(hand_kernel, levels, side),
        out_shape=jax.ShapeDtypeStruct((lon_count, rows, LANES), jnp.float32),
        in_specs=[pl.BlockSpec(memory_space=pltpu.SMEM), vmem, vmem]
        + [pl.BlockSpec(memory_space=pl.ANY)] * len(after),
        out_specs=vmem,
        compiler_params=pltpu.CompilerParams(vmem_limit_bytes=VMEM_LIMIT),
        name="hand_on",
    )(table, below, above, *after)


def gate_kernel(*refs):
    pass


def gate(values, *others):
    anywhere = pl.BlockSpec(memory_space=pl.ANY)
    count = len(values)
    return pl.pallas_call(
        gate_kernel,
        out_shape=[jax.ShapeDtypeStruct(x.shape, x.dtype) for x in values],
        in_specs=[anywhere] * (count + len(others)),
        out_specs=[anywhere] * count,
        input_output_aliases={i: i for i in range(count)},
        name="gate",
    )(*values, *others)


def heat_kernel(levels, side, factor, table_ref, chl_ref, light_ref, land_ref, widen_ref, out_ref, rows_ref, wide_ref):
    tile_blocks = land_ref.shape[1] // side
    halves = side * side // LANES
    group = LANES // side
    fine_cols = light_ref.shape[1]
    fine_rows = light_ref.shape[0]
    f32 = jnp.float32
    group_id = lane_ids() >> (side.bit_length() - 1)

    def place(lt, carry):
        at = pl.multiple_of(lt * SUB, SUB)
        for h in range(halves):
            blocks = []
            for b in range(tile_blocks):
                owner = table_ref[TILE_OWNER, b]
                values = chl_ref[owner, pl.ds(at, SUB), h * LANES : (h + 1) * LANES]
                blocks.append(jnp.where(table_ref[TILE_WET, b] == 1, values, 0.0))
            for r in range(group):
                line = None
                for b in range(tile_blocks):
                    piece = turned(blocks[b], side * (b - r))
                    line = piece if line is None else jnp.where(group_id == b, piece, line)
                rows_ref[pl.ds(pl.multiple_of((h * group + r) * levels + lt * SUB, SUB), SUB), :] = line
        return carry

    lax.fori_loop(0, levels // SUB, place, 0)
    wet = land_ref[...].astype(f32)
    widen = widen_ref[...]
    above = jnp.zeros_like(wet)
    passing = jnp.ones_like(wet)
    for l in range(levels):
        chl = rows_ref[pl.ds(l, side, stride=levels), :]
        above = above + (0.04 + 0.02 * chl)
        through = jnp.exp(-above)
        kept = (passing - through) * wet
        passing = through
        high = kept.astype(jnp.bfloat16)
        low = (kept - high.astype(f32)).astype(jnp.bfloat16)
        wide_ref[l * side : (l + 1) * side, :] = jnp.dot(
            high, widen, preferred_element_type=f32
        ) + jnp.dot(low, widen, preferred_element_type=f32)

    sub = lax.broadcasted_iota(jnp.int32, (SUB, LANES), 0)
    sources = []
    for m in range(fine_rows // SUB):
        start = (m * SUB // factor) // SUB * SUB
        index = jnp.zeros_like(sub)
        for r in range(1, side):
            index = index + jnp.where(sub + m * SUB >= r * factor, 1, 0)
        sources.append((start, index - start))

    def spread(l, carry):
        for c in range(fine_cols // LANES):
            span = slice(c * LANES, (c + 1) * LANES)
            for m in range(0, fine_rows // SUB, 2):
                both = []
                for n in (m, m + 1):
                    start, index = sources[n]
                    lines = wide_ref[pl.ds(pl.multiple_of(l * side + start, SUB), SUB), span]
                    lines = jnp.take_along_axis(lines, index, axis=0)
                    both.append(lines * light_ref[n * SUB : (n + 1) * SUB, span])
                out_ref[l, m * SUB : (m + 2) * SUB, span] = jnp.concatenate(both, axis=0).astype(jnp.bfloat16)
        return carry

    lax.fori_loop(0, levels, spread, 0)


def heat(table, chl, light, land, levels, widen):
    side = land.shape[0]
    factor = light.shape[0] // side
    vmem = pl.BlockSpec(memory_space=pltpu.VMEM)
    return pl.pallas_call(
        functools.partial(heat_kernel, levels, side, factor),
        out_shape=jax.ShapeDtypeStruct((levels,) + light.shape, jnp.bfloat16),
        in_specs=[pl.BlockSpec(memory_space=pltpu.SMEM), vmem, vmem, vmem, vmem],
        out_specs=vmem,
        scratch_shapes=[
            pltpu.VMEM((side * levels, LANES), jnp.float32),
            pltpu.VMEM((side * levels, light.shape[1]), jnp.float32),
        ],
        compiler_params=pltpu.CompilerParams(vmem_limit_bytes=VMEM_LIMIT),
        name="heat",
    )(table, chl, light, land, widen)


def widened(x, rows, width):
    return jnp.pad(x, ((0, rows - x.shape[0]), (0, width - x.shape[1])))


def on_device(tracers, phys_fine, mix_coarse, surf_light, land_mask, owner_map):
    f32 = jnp.float32
    slot_count = tracers.shape[0]
    side = land_mask.shape[0]
    levels = mix_coarse.shape[2]
    tile_blocks = land_mask.shape[1] // side
    factor = phys_fine.shape[0] // side
    fine_cols = phys_fine.shape[1]
    group = LANES // side

    fine = jnp.transpose(phys_fine, (0, 2, 1))
    mix = jnp.transpose(mix_coarse, (0, 2, 1))
    wet = land_mask.astype(f32)
    width = fine_cols

    northward = jnp.concatenate(
        [
            widened(fine[-1, levels : 2 * levels, :].astype(f32), levels, width),
            widened(wet[-1:], 1, width),
        ],
        axis=0,
    )
    southward = widened(wet[:1], 1, width)
    last_face = jnp.mean(
        fine[:, :levels, fine_cols - 1].astype(f32).reshape(side, factor, levels), axis=1
    )
    face_pack = jnp.pad(
        last_face.reshape(side // group, group, levels // SUB, SUB).transpose(3, 1, 0, 2),
        ((0, 0), (0, 0), (0, 0), (0, group - levels // SUB)),
    ).reshape(SUB, LANES)
    eastward = jnp.concatenate([face_pack, widened(wet[:, -1][None], 1, LANES)], axis=0)
    westward = widened(wet[:, 0][None], 1, LANES)

    from_south = lax.ppermute(northward, "lat", along("lat", 1, False))
    from_north = lax.ppermute(southward, "lat", along("lat", -1, False))
    from_west = lax.ppermute(eastward, "lon", along("lon", 1, True))
    from_east = lax.ppermute(westward, "lon", along("lon", -1, True))

    fine_id = jnp.arange(fine_cols)[:, None]
    coarse_id = jnp.arange(land_mask.shape[1])[None, :]
    member = (fine_id // factor == coarse_id).astype(jnp.bfloat16)
    final = (fine_id == factor * coarse_id + factor - 1).astype(jnp.bfloat16)
    picks = jnp.concatenate([final, member], axis=1)

    table = routing(owner_map, slot_count, tile_blocks)
    def to_north(x):
        return lax.ppermute(x, "lat", along("lat", 1, False))

    def to_south(x):
        return lax.ppermute(x, "lat", along("lat", -1, False))

    def to_east(x):
        return lax.ppermute(x, "lon", along("lon", 1, True))

    def to_west(x):
        return lax.ppermute(x, "lon", along("lon", -1, True))

    def across(x):
        return lax.all_to_all(x, "lon", 0, 0, tiled=True)

    quads, west, east = first_edges(table, tracers, levels, side)
    quads = across(quads)
    rows = coarse_rows(fine, mix, picks)
    phys, line_phys = coarsen(
        table, rows, surf_light, land_mask, from_south, from_north, from_west, from_east, picks
    )
    phys = across(phys)
    low, high, low_in, high_in, ends = tile_lines(table, quads, levels, side)
    below, above = to_north(high), to_south(low)
    west, east = gate((west, east), phys)
    rim_w, rim_e = to_east(east), to_west(west)
    ends_w, ends_e = to_east(ends), to_west(ends)
    rims = across(hand_on(table, below, above, levels, side, phys, ends_w, ends_e))
    new_low, new_high = line_step(
        low, high, low_in, high_in, below, above, ends_w, ends_e, line_phys, levels
    )
    below, above = to_north(new_high), to_south(new_low)
    partial = inner(table, tracers, phys, levels, side)
    (handed,) = gate((hand_on(table, below, above, levels, side),), rims, rim_w, rim_e, partial)
    new_rims = across(handed)
    current, west, east = step(table, partial, phys, rims, rim_w, rim_e, levels, side, False)
    rim_w, rim_e = to_east(east), to_west(west)
    partial = inner(table, current, phys, levels, side)
    current, chl = step(table, partial, phys, new_rims, rim_w, rim_e, levels, side, True)
    chl = lax.all_to_all(chl, "lon", 0, 0, tiled=True)
    heating = heat(table, chl, surf_light, land_mask, levels, jnp.transpose(member))
    return current, heating


def solution(mesh):
    in_specs = (
        P(("lat", "lon"), None, None),
        P("lat", "lon", None),
        P("lat", "lon", None),
        P("lat", "lon"),
        P("lat", "lon"),
        P("lat", None),
    )
    out_specs = (P(("lat", "lon"), None, None), P(None, "lat", "lon"))
    return jax.shard_map(
        on_device, mesh=mesh, in_specs=in_specs, out_specs=out_specs, check_vma=False
    )
```

```python
import functools

import jax
import jax.numpy as jnp
from jax import lax
from jax.experimental import pallas as pl
from jax.experimental.pallas import tpu as pltpu
from jax.sharding import PartitionSpec as P

LANES = 128
SUB = 8

diffuse_rate = 0.08
nano_chl_index = 10
diat_chl_index = 11

SLOT_TILE, SLOT_FULL, SLOT_WEST, SLOT_EAST, TILE_OWNER, TILE_WET, TILE_BASE = range(7)
TABLE_ROWS = 8

OPEN_EAST, OPEN_NORTH, OPEN_WEST, OPEN_SOUTH, LIGHT, WET = range(6)

VMEM_LIMIT = 48 * 1024 * 1024


def positive(value):
    return jnp.maximum(value, 0.0)


def lane_ids(rows=SUB):
    return lax.broadcasted_iota(jnp.int32, (rows, LANES), 1)


def turned(value, by):
    by = by % LANES
    return value if by == 0 else pltpu.roll(value, by, 1)


def quotient(value, by):
    if by & (by - 1) == 0:
        return lax.shift_right_logical(value, jnp.int32(by.bit_length() - 1))
    return lax.div(value, jnp.int32(by))


def remainder(value, by):
    if by & (by - 1) == 0:
        return value & (by - 1)
    return lax.rem(value, jnp.int32(by))


def along(axis, by, closed):
    size = lax.axis_size(axis)
    pairs = [(i, (i + by) % size) for i in range(size)]
    return [p for p in pairs if closed or p[1] == p[0] + by]


def table_kernel(slot_count, tile_blocks, lon_count, row_ref, out_ref, used_ref):
    me = lax.axis_index("lon")
    block_count = row_ref.shape[1]
    width = out_ref.shape[1]

    def clear(i, carry):
        for r in range(TABLE_ROWS):
            out_ref[r, i] = 0
        return carry

    lax.fori_loop(0, width, clear, 0)

    def unuse(i, carry):
        used_ref[0, i] = 0
        used_ref[1, i] = 0
        return carry

    lax.fori_loop(0, lon_count, unuse, 0)
    out_ref[TILE_BASE, 0] = me * tile_blocks

    def visit(k, carry):
        code = row_ref[0, k]
        safe = jnp.maximum(code, 0)
        owner = remainder(quotient(safe, slot_count), lon_count)
        slot = remainder(safe, slot_count)
        tile = quotient(k, tile_blocks)

        @pl.when((code >= 0) & (owner == me))
        def _():
            west = row_ref[0, remainder(k + block_count - 1, block_count)]
            east = row_ref[0, remainder(k + 1, block_count)]
            out_ref[SLOT_TILE, slot] = tile
            out_ref[SLOT_FULL, slot] = 1
            out_ref[SLOT_WEST, slot] = remainder(jnp.maximum(west, 0), slot_count)
            out_ref[SLOT_EAST, slot] = remainder(jnp.maximum(east, 0), slot_count)
            used_ref[0, tile] = 1

        @pl.when((code >= 0) & (tile == me))
        def _():
            local = remainder(k, tile_blocks)
            out_ref[TILE_OWNER, local] = owner
            out_ref[TILE_WET, local] = 1
            used_ref[1, owner] = 1

        return carry

    lax.fori_loop(0, block_count, visit, 0, unroll=4)

    def give(target, filled, line, count):
        def one(i, carry):
            def look(j, done):
                take = (done == 0) & (used_ref[line, j] == 0)

                @pl.when(take)
                def _():
                    out_ref[target, i] = j
                    used_ref[line, j] = 1

                return jnp.where(take, 1, done)

            @pl.when(out_ref[filled, i] == 0)
            def _():
                lax.fori_loop(0, lon_count, look, 0)

            return carry

        lax.fori_loop(0, count, one, 0)

    give(SLOT_TILE, SLOT_FULL, 0, slot_count)
    give(TILE_OWNER, TILE_WET, 1, tile_blocks)


def routing(row, slot_count, tile_blocks):
    lon_count = lax.axis_size("lon")
    width = max(slot_count, tile_blocks, lon_count)
    return pl.pallas_call(
        functools.partial(table_kernel, slot_count, tile_blocks, lon_count),
        out_shape=jax.ShapeDtypeStruct((TABLE_ROWS, width), jnp.int32),
        in_specs=[pl.BlockSpec(memory_space=pltpu.SMEM)],
        out_specs=pl.BlockSpec(memory_space=pltpu.SMEM),
        scratch_shapes=[pltpu.SMEM((2, lon_count), jnp.int32)],
        name="routing",
    )(row)


def merged(pieces, ids):
    packed = pieces[0]
    for g in range(1, len(pieces)):
        packed = jnp.where(ids == g, pieces[g], packed)
    return packed


def pack_columns(first, second, side):
    lane = lane_ids()
    odd = (lane & 1) == 1
    here = (lane & (side - 1)) >> 1
    there = ((lane + 1) & (side - 1)) >> 1
    even_ends = merged([turned(v, 1 + 2 * g) for g, v in enumerate(first)], here)
    odd_ends = merged([turned(v, 2 * g) for g, v in enumerate(second)], there)
    return jnp.where(odd, even_ends, odd_ends), jnp.where(odd, odd_ends, even_ends)


def pack_quads(first, second, side):
    low = lane_ids() < LANES // 2
    both = [jnp.where(low, a, b) for a, b in zip(first, second)]
    turns = [turned(v, 2 * side + (g % 2) * (LANES // 2)) for g, v in enumerate(both)]
    return [jnp.where(low, turns[g], turns[g + 1]) for g in range(0, len(turns), 2)]


def regroup(values, side):
    values = list(values)
    ids = lane_ids() >> (side.bit_length() - 1)
    bit = 1
    while bit < len(values):
        keep = (ids & bit) == 0
        for n in range(len(values)):
            if n & bit == 0:
                a, b = values[n], values[n + bit]
                values[n] = jnp.where(keep, a, turned(b, side * bit))
                values[n + bit] = jnp.where(keep, turned(a, -side * bit), b)
        bit *= 2
    return values


def edges_kernel(levels, side, table_ref, cell_ref, rows_ref, west_ref, east_ref):
    group = LANES // side
    rounds = cell_ref.shape[1] // levels // group
    level_tiles = levels // SUB

    def body(lt, carry):
        for i in range(rounds):
            row = pl.multiple_of(i * levels + lt * SUB, SUB)
            first, second = [], []
            for g in range(group):
                at = pl.multiple_of((i * group + g) * levels + lt * SUB, SUB)
                first.append(cell_ref[0, pl.ds(at, SUB), 0:LANES])
                second.append(cell_ref[0, pl.ds(at, SUB), LANES : 2 * LANES])
            west, east = pack_columns(first, second, side)
            west_ref[0, pl.ds(row, SUB), :] = west
            east_ref[0, pl.ds(row, SUB), :] = east
            for n, quad in enumerate(pack_quads(first, second, side)):
                at = pl.multiple_of((i * (group // 2) + n) * levels + lt * SUB, SUB)
                rows_ref[0, pl.ds(at, SUB), :] = quad
        return carry

    lax.fori_loop(0, level_tiles, body, 0, unroll=True)


def first_edges(table, tracers, levels, side):
    slot_count, channels, cell_count = tracers.shape
    lon_count = lax.axis_size("lon")
    rows = channels * side // LANES
    f32 = jnp.float32
    by_slot = pl.BlockSpec((1, rows, LANES), lambda s, t: (s, 0, 0))
    return pl.pallas_call(
        functools.partial(edges_kernel, levels, side),
        out_shape=[
            jax.ShapeDtypeStruct((lon_count, 4 * rows, LANES), f32),
            jax.ShapeDtypeStruct((slot_count, rows, LANES), f32),
            jax.ShapeDtypeStruct((slot_count, rows, LANES), f32),
        ],
        grid_spec=pltpu.PrefetchScalarGridSpec(
            num_scalar_prefetch=1,
            grid=(slot_count,),
            in_specs=[pl.BlockSpec((1, channels, cell_count), lambda s, t: (s, 0, 0))],
            out_specs=[
                pl.BlockSpec((1, 4 * rows, LANES), lambda s, t: (t[SLOT_TILE, s], 0, 0)),
                by_slot,
                by_slot,
            ],
        ),
        compiler_params=pltpu.CompilerParams(vmem_limit_bytes=VMEM_LIMIT),
        name="first_edges",
    )(table, tracers)


def growth(
    nitrogen,
    phosphate,
    silicate,
    iron_free,
    nano_carbon,
    diat_carbon,
    micro_zoo,
    meso_zoo,
    par_light,
    warm_factor,
):
    limit_nitro = nitrogen / (0.5 + nitrogen)
    limit_phos = positive(phosphate) / (0.3 + positive(phosphate))
    limit_iron = positive(iron_free) / (0.2 + positive(iron_free))
    limit_sil = positive(silicate) / (1.0 + positive(silicate))
    nutr_nano = jnp.minimum(jnp.minimum(limit_nitro, limit_phos), limit_iron)
    nutr_diat = jnp.minimum(nutr_nano, limit_sil)
    lit = warm_factor * par_light
    prod_nano = 0.1 * lit / (par_light + 0.5) * nutr_nano * nano_carbon
    prod_diat = 0.12 * lit / (par_light + 1.0) * nutr_diat * diat_carbon
    graze_nano = 0.08 * warm_factor * micro_zoo / (1.0 + positive(nano_carbon))
    graze_diat = 0.06 * warm_factor * meso_zoo / (1.0 + positive(diat_carbon))
    return prod_nano, prod_diat, graze_nano, graze_diat


CHL_TRACERS = (3, 4, 5, 6, 7, 8, 9, 10, 11, 15, 16)
CHL_RUN = 3
CHL_BLOCKS = sorted({tracer // CHL_RUN for tracer in CHL_TRACERS})


def chl_after(mixed, par_light, warm_factor):
    (
        nitrate,
        ammonium,
        phosphate,
        silicate,
        iron_free,
        nano_carbon,
        diat_carbon,
        nano_chl,
        diat_chl,
        micro_zoo,
        meso_zoo,
    ) = mixed
    prod_nano, prod_diat, graze_nano, graze_diat = growth(
        positive(nitrate) + positive(ammonium),
        phosphate,
        silicate,
        iron_free,
        nano_carbon,
        diat_carbon,
        micro_zoo,
        meso_zoo,
        par_light,
        warm_factor,
    )
    nano_chl = nano_chl + 0.03 * prod_nano - (graze_nano + 0.02) * nano_chl
    diat_chl = diat_chl + 0.03 * prod_diat - (graze_diat + 0.02) * diat_chl
    return nano_chl, diat_chl


def react(mixed, par_light, warm_factor):
    (
        carbon_dis,
        alkalinity,
        oxygen,
        nitrate,
        ammonium,
        phosphate,
        silicate,
        iron_free,
        nano_carbon,
        diat_carbon,
        nano_chl,
        diat_chl,
        nano_iron,
        diat_iron,
        diat_silica,
        micro_zoo,
        meso_zoo,
        dissolved_org,
        small_part,
        big_part,
        small_iron,
        big_iron,
        big_silica,
        calcite,
    ) = mixed
    nitrogen = positive(nitrate) + positive(ammonium)
    ammon_share = (positive(ammonium) + 0.01) / (nitrogen + 0.02)
    prod_nano, prod_diat, graze_nano, graze_diat = growth(
        nitrogen,
        phosphate,
        silicate,
        iron_free,
        nano_carbon,
        diat_carbon,
        micro_zoo,
        meso_zoo,
        par_light,
        warm_factor,
    )
    loss_nano = graze_nano + 0.02
    loss_diat = graze_diat + 0.02
    eaten_nano = graze_nano * nano_carbon
    eaten_diat = graze_diat * diat_carbon
    death_micro = 0.03 * micro_zoo * positive(micro_zoo)
    death_meso = 0.03 * meso_zoo * positive(meso_zoo)
    remin_doc = 0.03 * warm_factor * dissolved_org
    remin_poc = 0.02 * warm_factor * small_part
    remin_goc = 0.01 * warm_factor * big_part
    nitrify = 0.05 * ammonium
    melt_si = 0.02 * big_silica
    melt_cal = 0.01 * calcite
    melt_sfe = 0.02 * small_iron
    melt_bfe = 0.01 * big_iron
    uptake = prod_nano + prod_diat
    remin_total = remin_doc + remin_poc + remin_goc
    calcify = 0.02 * prod_nano
    gained = remin_total - uptake
    shell = melt_cal - calcify
    by_ammon = ammon_share * uptake
    by_nitrate = 0.16 * (uptake - by_ammon - nitrify)
    return [
        carbon_dis + gained + shell,
        alkalinity + 2.0 * shell + by_nitrate,
        oxygen - 1.3 * gained - 0.32 * nitrify,
        nitrate - by_nitrate,
        ammonium + 0.16 * (remin_total - by_ammon - nitrify),
        phosphate + 0.01 * gained,
        silicate + melt_si - 0.15 * prod_diat,
        iron_free + melt_sfe + melt_bfe - 0.005 * uptake,
        nano_carbon + prod_nano - loss_nano * nano_carbon,
        diat_carbon + prod_diat - loss_diat * diat_carbon,
        nano_chl + 0.03 * prod_nano - loss_nano * nano_chl,
        diat_chl + 0.03 * prod_diat - loss_diat * diat_chl,
        nano_iron + 0.005 * prod_nano - loss_nano * nano_iron,
        diat_iron + 0.005 * prod_diat - loss_diat * diat_iron,
        diat_silica + 0.15 * prod_diat - loss_diat * diat_silica,
        micro_zoo + 0.3 * eaten_nano - death_micro,
        meso_zoo + 0.3 * eaten_diat - death_meso,
        dissolved_org + 0.3 * eaten_nano + 0.02 * nano_carbon - remin_doc,
        small_part + 0.4 * eaten_nano + death_micro - remin_poc,
        big_part + 0.4 * eaten_diat + 0.02 * diat_carbon + death_meso - remin_goc,
        small_iron + loss_nano * nano_iron - melt_sfe,
        big_iron + loss_diat * diat_iron - melt_bfe,
        big_silica + loss_diat * diat_silica - melt_si,
        calcite + calcify - melt_cal,
    ]


def transport(faces, opens):
    flow_e, flow_n, flow_w, flow_s = (face * is_open for face, is_open in zip(faces, opens))
    open_e, open_n, open_w, open_s = opens
    out_e, in_e = jnp.maximum(flow_e, 0.0), jnp.minimum(flow_e, 0.0)
    out_n, in_n = jnp.maximum(flow_n, 0.0), jnp.minimum(flow_n, 0.0)
    in_w, out_w = jnp.maximum(flow_w, 0.0), jnp.minimum(flow_w, 0.0)
    in_s, out_s = jnp.maximum(flow_s, 0.0), jnp.minimum(flow_s, 0.0)
    drift = diffuse_rate * (open_w + open_e + open_s + open_n)
    return (
        1.0 - (out_e - out_w) - (out_n - out_s) - drift,
        diffuse_rate * open_e - in_e,
        diffuse_rate * open_w + in_w,
        diffuse_rate * open_n - in_n,
        diffuse_rate * open_s + in_s,
    )


def set_mixing(coef_ref, at, span, mix, above, bottom):
    sub = lax.broadcasted_iota(jnp.int32, (SUB, LANES), 0)
    mix_up = pltpu.roll(jnp.where(sub == SUB - 1, above, mix), 1, 0)
    if bottom:
        mix = jnp.where(sub == SUB - 1, 0.0, mix)
    coef_ref[5, at, span] = 1.0 - mix - mix_up
    coef_ref[6, at, span] = mix
    coef_ref[7, at, span] = mix_up


def set_blank(moved_ref, channels):
    blank = jnp.zeros((SUB, moved_ref.shape[1]), jnp.float32)
    moved_ref[0:SUB, :] = blank
    moved_ref[SUB + channels : 2 * SUB + channels, :] = blank


def mixed_at(levels, count, span, moved_ref, coef_ref, lt):
    sub = lax.broadcasted_iota(jnp.int32, (SUB, LANES), 0)
    at = pl.multiple_of(lt * SUB, SUB)
    mix_c, mix_d, mix_u = (coef_ref[n, pl.ds(at, SUB), span] for n in (5, 6, 7))
    mixed = []
    for t in range(count):
        base = t * levels + lt * SUB
        before = moved_ref[pl.ds(pl.multiple_of(base, SUB), SUB), span]
        now = moved_ref[pl.ds(pl.multiple_of(base + SUB, SUB), SUB), span]
        after = moved_ref[pl.ds(pl.multiple_of(base + 2 * SUB, SUB), SUB), span]
        up = pltpu.roll(jnp.where(sub == SUB - 1, before, now), 1, 0)
        down = pltpu.roll(jnp.where(sub == 0, after, now), SUB - 1, 0)
        mixed.append(mix_c * now + mix_d * down + mix_u * up)
    return mixed


def lit_at(nano_chl, diat_chl, light, depth):
    sub = lax.broadcasted_iota(jnp.int32, (SUB, LANES), 0)
    absorb = 0.04 + 0.02 * (positive(nano_chl) + positive(diat_chl))
    total = absorb
    for by in (1, 2, 4):
        total = total + jnp.where(sub >= by, pltpu.roll(total, by, 0), 0.0)
    above = depth + (total - absorb)
    return light * jnp.exp(-(above + 0.5 * absorb)), depth + total[SUB - 1 : SUB, :]


def mix_and_react(levels, tracer_count, spans, moved_ref, coef_ref, light, wet, warm_at, store):
    def reacting(lt, carry):
        depths = []
        halves_new = []
        for h, span in enumerate(spans):
            mixed = mixed_at(levels, tracer_count, span, moved_ref, coef_ref, lt)
            par_light, depth = lit_at(mixed[nano_chl_index], mixed[diat_chl_index], light[h], carry[h])
            depths.append(depth)
            halves_new.append([value * wet[h] for value in react(mixed, par_light, warm_at(lt, h))])
            for t in range(tracer_count):
                store(t, pl.multiple_of(t * levels + lt * SUB, SUB), h, halves_new[h][t])
        store(None, lt, None, halves_new)
        return tuple(depths)

    start = tuple(jnp.zeros((1, LANES), jnp.float32) for _ in spans)
    lax.fori_loop(0, levels // SUB, reacting, start, unroll=True)


def block_faces(phys_ref, spans, levels, side, lt):
    group = LANES // side
    pack_at = 4 * levels + SUB
    lane = lane_ids()
    first_col = (lane & (side - 1)) == 0
    first_row = lane < side
    west_pack = phys_ref[0, pack_at : pack_at + SUB, spans[0]]
    south_pack = phys_ref[0, pack_at : pack_at + SUB, spans[1]]
    east = [phys_ref[0, lt * SUB : (lt + 1) * SUB, span] for span in spans]
    north = [phys_ref[0, levels + lt * SUB : levels + (lt + 1) * SUB, span] for span in spans]
    faces = []
    for h in range(len(spans)):
        west = jnp.where(first_col, turned(west_pack, -(h * group + lt)), turned(east[h], 1))
        before = turned(south_pack, -side * lt) if h == 0 else turned(north[h - 1], side)
        south = jnp.where(first_row, before, turned(north[h], side))
        faces.append((east[h], north[h], west, south))
    return faces


def inner_kernel(levels, side, table_ref, cell_ref, phys_ref, out_ref, coef_ref):
    channels, cell_count = cell_ref.shape[1:]
    tracer_count = channels // levels
    halves = cell_count // LANES
    level_tiles = levels // SUB
    spans = [slice(h * LANES, (h + 1) * LANES) for h in range(halves)]
    full = table_ref[SLOT_FULL, pl.program_id(0)] == 1

    @pl.when(jnp.logical_not(full))
    def _():
        out_ref[...] = jnp.zeros_like(out_ref)

    @pl.when(full)
    def _():
        lane = lane_ids()
        col = lane & (side - 1)
        first_row = lane < side
        last_row = lane >= LANES - side
        flag_row = 4 * levels

        def flag(f, h):
            return phys_ref[0, flag_row + f : flag_row + f + 1, spans[h]]

        for lt in range(level_tiles):
            at = slice(lt * SUB, (lt + 1) * SUB)
            for h, faces in enumerate(block_faces(phys_ref, spans, levels, side, lt)):
                c, e, w, n, s = transport(faces, [flag(f, h) for f in range(4)])
                e = jnp.where(col == side - 1, 0.0, e)
                w = jnp.where(col == 0, 0.0, w)
                if h == halves - 1:
                    n = jnp.where(last_row, 0.0, n)
                if h == 0:
                    s = jnp.where(first_row, 0.0, s)
                for k, value in enumerate((c, e, w, n, s)):
                    coef_ref[k, at, spans[h]] = value

        def advect(lt, carry):
            at = pl.multiple_of(lt * SUB, SUB)
            coef = [[coef_ref[n, pl.ds(at, SUB), span] for n in range(5)] for span in spans]
            for t in range(tracer_count):
                chan = pl.multiple_of(t * levels + lt * SUB, SUB)
                here = [cell_ref[0, pl.ds(chan, SUB), span] for span in spans]
                up = [turned(value, side) for value in here]
                down = [turned(value, -side) for value in here]
                for h in range(halves):
                    south = up[h] if h == 0 else jnp.where(first_row, up[h - 1], up[h])
                    north = down[h] if h == halves - 1 else jnp.where(last_row, down[h + 1], down[h])
                    c, e, w, n, s = coef[h]
                    out_ref[0, pl.ds(chan, SUB), spans[h]] = (
                        c * here[h]
                        + (e * turned(here[h], -1) + w * turned(here[h], 1))
                        + (n * north + s * south)
                    )
            return carry

        lax.fori_loop(0, level_tiles, advect, 0, unroll=True)


def inner(table, cells, phys, levels, side):
    slot_count, channels, cell_count = cells.shape
    phys_rows = phys.shape[1]
    by_slot = pl.BlockSpec((1, channels, cell_count), lambda s, t: (s, 0, 0))
    return pl.pallas_call(
        functools.partial(inner_kernel, levels, side),
        out_shape=jax.ShapeDtypeStruct(cells.shape, jnp.float32),
        grid_spec=pltpu.PrefetchScalarGridSpec(
            num_scalar_prefetch=1,
            grid=(slot_count,),
            in_specs=[
                by_slot,
                pl.BlockSpec((1, phys_rows, cell_count), lambda s, t: (t[SLOT_TILE, s], 0, 0)),
            ],
            out_specs=by_slot,
            scratch_shapes=[pltpu.VMEM((5, levels, cell_count), jnp.float32)],
        ),
        compiler_params=pltpu.CompilerParams(vmem_limit_bytes=VMEM_LIMIT),
        name="inner",
    )(table, cells, phys)


def add_rims(
    levels, side, spans, tracers, part_at, phys_ref, rim_ref, rim_w_ref, rim_e_ref, coef_ref, moved_ref, ends_ref
):
    group = LANES // side
    halves = len(spans)
    rows = rim_w_ref.shape[1]
    rounds = rows // levels
    level_tiles = levels // SUB
    lane = lane_ids()
    col = lane & (side - 1)
    first_row = lane < side
    last_row = lane >= LANES - side
    odd = (lane & 1) == 1
    flag_row = 4 * levels

    def flag(f, h):
        return phys_ref[0, flag_row + f : flag_row + f + 1, spans[h]]

    above_mix = [jnp.zeros((SUB, LANES), jnp.float32)] * halves
    for lt in range(level_tiles):
        at = slice(lt * SUB, (lt + 1) * SUB)
        for h, faces in enumerate(block_faces(phys_ref, spans, levels, side, lt)):
            _, e, w, n, s = transport(faces, [flag(f, h) for f in range(4)])
            coef_ref[0, at, spans[h]] = jnp.where(col == 0, w, jnp.where(col == side - 1, e, 0.0))
            if h == 0:
                coef_ref[1, at, spans[h]] = jnp.where(first_row, s, 0.0)
            if h == halves - 1:
                coef_ref[1, at, spans[h]] = jnp.where(last_row, n, 0.0)
            mix = phys_ref[0, 3 * levels + lt * SUB : 3 * levels + (lt + 1) * SUB, spans[h]]
            set_mixing(coef_ref, at, spans[h], mix, above_mix[h], lt == level_tiles - 1)
            above_mix[h] = mix

    for at in range(0, rows, SUB):
        ends_ref[at : at + SUB, :] = turned(rim_w_ref[0, at : at + SUB, :], 2 - 2 * side)
    set_blank(moved_ref, len(tracers) * levels)

    def gather(lt, carry):
        at = pl.multiple_of(lt * SUB, SUB)
        for i in range(rounds):
            row = pl.multiple_of(i * levels + lt * SUB, SUB)
            rims = [
                rim_ref[0, pl.ds(row, SUB), :],
                rim_ref[0, pl.ds(pl.multiple_of(rows + row, SUB), SUB), :],
            ]
            ends_w = ends_ref[pl.ds(row, SUB), :]
            ends_e = rim_e_ref[0, pl.ds(row, SUB), :]
            sides = [jnp.where(odd, ends_e, ends_w), jnp.where(odd, ends_w, ends_e)]
            for g in range(group):
                if i * group + g not in tracers:
                    continue
                place = tracers.index(i * group + g)
                chan = pl.multiple_of(place * levels + lt * SUB, SUB)
                rim = turned(rims[2 * g // group], -side - 2 * side * (g % (group // 2)))
                for h in range(halves):
                    ends = turned(sides[h], side - 2 + h - 2 * g)
                    moved = part_at(place, lt, spans[h])
                    moved = moved + coef_ref[0, pl.ds(at, SUB), spans[h]] * ends
                    if h in (0, halves - 1):
                        moved = moved + coef_ref[1, pl.ds(at, SUB), spans[h]] * rim
                    moved_ref[pl.ds(pl.multiple_of(SUB + chan, SUB), SUB), spans[h]] = moved
        return carry

    lax.fori_loop(0, level_tiles, gather, 0, unroll=True)


def step_kernel(levels, side, last, table_ref, part_ref, phys_ref, rim_ref, rim_w_ref, rim_e_ref, *refs):
    if last:
        out_ref, coef_ref, moved_ref, ends_ref = refs
        edge_refs = ()
    else:
        out_ref, west_ref, east_ref, coef_ref, moved_ref, ends_ref = refs
        edge_refs = (west_ref, east_ref)
    channels, cell_count = part_ref.shape[1:]
    tracer_count = channels // levels
    group = LANES // side
    halves = cell_count // LANES
    rounds = tracer_count // group
    slot = pl.program_id(0)
    full = table_ref[SLOT_FULL, slot] == 1
    spans = [slice(h * LANES, (h + 1) * LANES) for h in range(halves)]

    @pl.when(jnp.logical_not(full))
    def _():
        out_ref[...] = jnp.zeros_like(out_ref)
        for ref in edge_refs:
            ref[...] = jnp.zeros_like(ref)

    @pl.when(full)
    def _():
        flag_row = 4 * levels

        def flag(f, h):
            return phys_ref[0, flag_row + f : flag_row + f + 1, spans[h]]

        def part_at(t, lt, span):
            return part_ref[0, pl.ds(pl.multiple_of(t * levels + lt * SUB, SUB), SUB), span]

        add_rims(
            levels,
            side,
            spans,
            list(range(tracer_count)),
            part_at,
            phys_ref,
            rim_ref,
            rim_w_ref,
            rim_e_ref,
            coef_ref,
            moved_ref,
            ends_ref,
        )

        def store(t, at, h, value):
            if t is not None:
                out_ref[0, pl.ds(at, SUB), spans[h]] = value
            elif not last:
                for i in range(rounds):
                    row = pl.multiple_of(i * levels + at * SUB, SUB)
                    first, second = (new[i * group : (i + 1) * group] for new in value)
                    west, east = pack_columns(first, second, side)
                    west_ref[0, pl.ds(row, SUB), :] = west
                    east_ref[0, pl.ds(row, SUB), :] = east

        def warm_at(lt, h):
            return phys_ref[0, pl.ds(pl.multiple_of(2 * levels + lt * SUB, SUB), SUB), spans[h]]

        light = [flag(LIGHT, h) for h in range(halves)]
        wet = [flag(WET, h) for h in range(halves)]
        mix_and_react(levels, tracer_count, spans, moved_ref, coef_ref, light, wet, warm_at, store)


def step(table, cells, phys, rims, rim_w, rim_e, levels, side, last):
    slot_count, channels, cell_count = cells.shape
    lon_count = lax.axis_size("lon")
    rows = channels * side // LANES
    phys_rows = phys.shape[1]
    f32 = jnp.float32
    by_slot = pl.BlockSpec((1, channels, cell_count), lambda s, t: (s, 0, 0))
    shapes = [jax.ShapeDtypeStruct(cells.shape, f32)]
    specs = [by_slot]
    if not last:
        beside = jax.ShapeDtypeStruct((slot_count, rows, LANES), f32)
        shapes += [beside, beside]
        specs += [pl.BlockSpec((1, rows, LANES), lambda s, t: (s, 0, 0))] * 2
    return pl.pallas_call(
        functools.partial(step_kernel, levels, side, last),
        out_shape=shapes,
        grid_spec=pltpu.PrefetchScalarGridSpec(
            num_scalar_prefetch=1,
            grid=(slot_count,),
            in_specs=[
                by_slot,
                pl.BlockSpec((1, phys_rows, cell_count), lambda s, t: (t[SLOT_TILE, s], 0, 0)),
                pl.BlockSpec((1, 2 * rows, LANES), lambda s, t: (t[SLOT_TILE, s], 0, 0)),
                pl.BlockSpec((1, rows, LANES), lambda s, t: (t[SLOT_WEST, s], 0, 0)),
                pl.BlockSpec((1, rows, LANES), lambda s, t: (t[SLOT_EAST, s], 0, 0)),
            ],
            out_specs=specs,
            scratch_shapes=[
                pltpu.VMEM((8, levels, cell_count), f32),
                pltpu.VMEM((channels + 2 * SUB, cell_count), f32),
                pltpu.VMEM((rows, LANES), f32),
            ],
        ),
        compiler_params=pltpu.CompilerParams(vmem_limit_bytes=VMEM_LIMIT),
        name="step",
    )(table, cells, phys, rims, rim_w, rim_e)


def chl_kernel(levels, side, table_ref, *refs):
    count = len(CHL_TRACERS)
    part_refs = refs[: len(CHL_BLOCKS)]
    phys_ref, rim_ref, rim_w_ref, rim_e_ref, chl_ref, coef_ref, moved_ref, ends_ref = refs[len(CHL_BLOCKS) :]
    halves = chl_ref.shape[2] // LANES
    spans = [slice(h * LANES, (h + 1) * LANES) for h in range(halves)]
    full = table_ref[SLOT_FULL, pl.program_id(0)] == 1
    flag_row = 4 * levels

    @pl.when(jnp.logical_not(full))
    def _():
        chl_ref[...] = jnp.zeros_like(chl_ref)

    @pl.when(full)
    def _():
        def part_at(place, lt, span):
            tracer = CHL_TRACERS[place]
            at = (tracer % CHL_RUN) * levels + lt * SUB
            return part_refs[CHL_BLOCKS.index(tracer // CHL_RUN)][0, pl.ds(pl.multiple_of(at, SUB), SUB), span]

        add_rims(
            levels,
            side,
            spans,
            list(CHL_TRACERS),
            part_at,
            phys_ref,
            rim_ref,
            rim_w_ref,
            rim_e_ref,
            coef_ref,
            moved_ref,
            ends_ref,
        )
        nano = CHL_TRACERS.index(nano_chl_index)
        diat = CHL_TRACERS.index(diat_chl_index)

        def greening(lt, carry):
            at = pl.multiple_of(lt * SUB, SUB)
            depths = []
            for h, span in enumerate(spans):
                mixed = mixed_at(levels, count, span, moved_ref, coef_ref, lt)
                light = phys_ref[0, flag_row + LIGHT : flag_row + LIGHT + 1, span]
                wet = phys_ref[0, flag_row + WET : flag_row + WET + 1, span]
                warm = phys_ref[0, pl.ds(pl.multiple_of(2 * levels + lt * SUB, SUB), SUB), span]
                par_light, depth = lit_at(mixed[nano], mixed[diat], light, carry[h])
                depths.append(depth)
                nano_chl, diat_chl = chl_after(mixed, par_light, warm)
                chl_ref[0, pl.ds(at, SUB), span] = positive(nano_chl * wet) + positive(diat_chl * wet)
            return tuple(depths)

        start = tuple(jnp.zeros((1, LANES), jnp.float32) for _ in spans)
        lax.fori_loop(0, levels // SUB, greening, start, unroll=True)


def last_chl(table, cells, phys, rims, rim_w, rim_e, levels, side):
    slot_count, channels, cell_count = cells.shape
    lon_count = lax.axis_size("lon")
    rows = channels * side // LANES
    count = len(CHL_TRACERS)
    f32 = jnp.float32

    def level_block(number):
        return pl.BlockSpec((1, CHL_RUN * levels, cell_count), lambda s, t: (s, number, 0))

    return pl.pallas_call(
        functools.partial(chl_kernel, levels, side),
        out_shape=jax.ShapeDtypeStruct((lon_count, levels, cell_count), f32),
        grid_spec=pltpu.PrefetchScalarGridSpec(
            num_scalar_prefetch=1,
            grid=(slot_count,),
            in_specs=[level_block(n) for n in CHL_BLOCKS]
            + [
                pl.BlockSpec((1, phys.shape[1], cell_count), lambda s, t: (t[SLOT_TILE, s], 0, 0)),
                pl.BlockSpec((1, 2 * rows, LANES), lambda s, t: (t[SLOT_TILE, s], 0, 0)),
                pl.BlockSpec((1, rows, LANES), lambda s, t: (t[SLOT_WEST, s], 0, 0)),
                pl.BlockSpec((1, rows, LANES), lambda s, t: (t[SLOT_EAST, s], 0, 0)),
            ],
            out_specs=pl.BlockSpec((1, levels, cell_count), lambda s, t: (t[SLOT_TILE, s], 0, 0)),
            scratch_shapes=[
                pltpu.VMEM((8, levels, cell_count), f32),
                pltpu.VMEM((count * levels + 2 * SUB, cell_count), f32),
                pltpu.VMEM((rows, LANES), f32),
            ],
        ),
        compiler_params=pltpu.CompilerParams(vmem_limit_bytes=VMEM_LIMIT),
        name="last_chl",
    )(table, *([cells] * len(CHL_BLOCKS)), phys, rims, rim_w, rim_e)


def rows_kernel(levels, factor, fine_ref, mix_ref, pick_ref, rows_ref):
    f32 = jnp.float32
    picks = pick_ref[...]
    east_face = jnp.zeros((levels, LANES), f32)
    temp_mean = jnp.zeros((levels, LANES), f32)
    for r in range(factor):
        got = jnp.dot(fine_ref[r], picks, preferred_element_type=f32)
        east_face += got[0:levels, 0:LANES]
        temp_mean += got[2 * levels : 3 * levels, LANES : 2 * LANES]
        if r == factor - 1:
            north_face = got[levels : 2 * levels, LANES : 2 * LANES]
    rows_ref[0, 0:levels, :] = east_face * (1.0 / factor)
    rows_ref[0, levels : 2 * levels, :] = north_face * (1.0 / factor)
    rows_ref[0, 2 * levels : 3 * levels, :] = jnp.exp(0.0639 * (temp_mean * (1.0 / (factor * factor))))
    rows_ref[0, 3 * levels : 4 * levels, :] = mix_ref[0].astype(f32)


def coarse_rows(fine, mix, picks):
    side, levels, tile_cols = mix.shape
    factor = fine.shape[0] // side
    fine_cols = fine.shape[2]
    return pl.pallas_call(
        functools.partial(rows_kernel, levels, factor),
        out_shape=jax.ShapeDtypeStruct((side, 4 * levels, tile_cols), jnp.float32),
        grid=(side,),
        in_specs=[
            pl.BlockSpec((factor, 3 * levels, fine_cols), lambda i: (i, 0, 0)),
            pl.BlockSpec((1, levels, tile_cols), lambda i: (i, 0, 0)),
            pl.BlockSpec(picks.shape, lambda i: (0, 0)),
        ],
        out_specs=pl.BlockSpec((1, 4 * levels, tile_cols), lambda i: (i, 0, 0)),
        compiler_params=pltpu.CompilerParams(vmem_limit_bytes=VMEM_LIMIT),
        name="coarse_rows",
    )(fine, mix, picks)


def place_kernel(
    levels,
    side,
    factor,
    table_ref,
    rows_ref,
    light_ref,
    land_ref,
    south_ref,
    north_ref,
    west_ref,
    east_ref,
    pick_ref,
    out_ref,
    line_ref,
    flags_ref,
):
    tile_blocks = land_ref.shape[1] // side
    halves = side * side // LANES
    group = LANES // side
    fine_cols = light_ref.shape[1]
    f32 = jnp.float32
    picks = pick_ref[...]
    lane = lane_ids()
    group_id = lane >> (side.bit_length() - 1)
    col_id = lane & (side - 1)
    flag_row = 4 * levels
    pack_at = flag_row + SUB
    wet = land_ref[...].astype(f32)
    sides = wet.shape
    lane2 = lax.broadcasted_iota(jnp.int32, sides, 1)
    sub2 = lax.broadcasted_iota(jnp.int32, sides, 0)
    diagonal = lane2 == sub2
    rim_w = jnp.sum(jnp.where(diagonal, west_ref[SUB : SUB + 1, :], 0.0), axis=1, keepdims=True)
    rim_e = jnp.sum(jnp.where(diagonal, east_ref[0:1, :], 0.0), axis=1, keepdims=True)
    wet_w = jnp.where(lane2 == 0, rim_w, pltpu.roll(wet, 1, 1))
    wet_e = jnp.where(lane2 == LANES - 1, rim_e, pltpu.roll(wet, LANES - 1, 1))
    wet_s = jnp.where(sub2 == 0, south_ref[levels : levels + 1, 0:LANES], pltpu.roll(wet, 1, 0))
    wet_n = jnp.where(sub2 == side - 1, north_ref[0:1, 0:LANES], pltpu.roll(wet, side - 1, 0))
    fold_r = lax.broadcasted_iota(jnp.int32, (side, side * factor), 0)
    fold_c = lax.broadcasted_iota(jnp.int32, (side, side * factor), 1)
    fold_d = fold_c - factor * fold_r
    fold = jnp.where((fold_d >= 0) & (fold_d < factor), 1.0, 0.0)
    narrow = picks[:, LANES : 2 * LANES].astype(f32)
    light_rows = jnp.dot(fold, light_ref[...], precision=lax.Precision.HIGHEST, preferred_element_type=f32)
    light_mean = jnp.dot(
        light_rows, narrow, precision=lax.Precision.HIGHEST, preferred_element_type=f32
    ) * (1.0 / (factor * factor))
    flags = [wet * wet_e, wet * wet_n, wet * wet_w, wet * wet_s, light_mean, wet]
    for r in range(side):
        for f, value in enumerate(flags):
            flags_ref[r, f : f + 1, :] = value[r : r + 1, :]
        flags_ref[r, len(flags) : SUB, :] = jnp.zeros((SUB - len(flags), LANES), f32)

    def place(ref, frm, to):
        for h in range(halves):
            values = [ref[h * group + r, pl.ds(frm, SUB), :] for r in range(group)]
            for b, block in enumerate(regroup(values, side)):
                owner = table_ref[TILE_OWNER, b]
                out_ref[owner, pl.ds(to, SUB), h * LANES : (h + 1) * LANES] = block

    def place_four(q, carry):
        for n in range(4):
            at = pl.multiple_of(n * levels + q * SUB, SUB)
            place(rows_ref, at, at)
        return carry

    lax.fori_loop(0, levels // SUB, place_four, 0)
    place(flags_ref, 0, flag_row)

    fine_v = south_ref[0:levels, 0:fine_cols].astype(jnp.bfloat16)
    north_below = jnp.dot(fine_v, picks, preferred_element_type=f32)[:, LANES : 2 * LANES] * (1.0 / factor)
    for h, r in enumerate((0, side - 1)):
        span = slice(h * LANES, (h + 1) * LANES)
        line_ref[0 : 4 * levels, span] = rows_ref[r, 0 : 4 * levels, :]
        line_ref[6 * levels : 6 * levels + SUB, span] = flags_ref[r]
        line_ref[5 * levels : 6 * levels, span] = (
            north_below if h == 0 else rows_ref[r - 1, levels : 2 * levels, :]
        )
        from_lane = side * (r % group) + group * (r // group)
        for lt in range(levels // SUB):
            face = rows_ref[r, lt * SUB : (lt + 1) * SUB, :]
            line_ref[4 * levels + lt * SUB : 4 * levels + (lt + 1) * SUB, span] = jnp.where(
                lane == 0, turned(west_ref[0:SUB, :], -(from_lane + lt)), turned(face, 1)
            )
    for b in range(tile_blocks):
        owner = table_ref[TILE_OWNER, b]
        south_pack = jnp.zeros((SUB, LANES), f32)
        for lt in range(levels // SUB):
            piece = turned(north_below[lt * SUB : (lt + 1) * SUB, :], side * (lt - b))
            south_pack = jnp.where(group_id == lt, piece, south_pack)
        if b == 0:
            west_pack = west_ref[0:SUB, :]
        else:
            beside = table_ref[TILE_OWNER, b - 1]
            west_pack = jnp.zeros((SUB, LANES), f32)
            for h in range(halves):
                for lt in range(levels // SUB):
                    face = out_ref[beside, lt * SUB : (lt + 1) * SUB, h * LANES : (h + 1) * LANES]
                    piece = turned(face, h * group + lt - (side - 1))
                    west_pack = jnp.where(col_id == h * group + lt, piece, west_pack)
        out_ref[owner, pack_at : pack_at + SUB, 0:LANES] = west_pack
        out_ref[owner, pack_at : pack_at + SUB, LANES : 2 * LANES] = south_pack


def coarsen(table, rows, light, land, from_south, from_north, from_west, from_east, picks):
    lon_count = lax.axis_size("lon")
    side, tile_cols = land.shape
    levels = rows.shape[1] // 4
    factor = light.shape[0] // side
    phys_rows = 4 * levels + 2 * SUB
    f32 = jnp.float32
    vmem = pl.BlockSpec(memory_space=pltpu.VMEM)
    return pl.pallas_call(
        functools.partial(place_kernel, levels, side, factor),
        out_shape=[
            jax.ShapeDtypeStruct((lon_count, phys_rows, side * side), f32),
            jax.ShapeDtypeStruct((6 * levels + SUB, 2 * LANES), f32),
        ],
        in_specs=[pl.BlockSpec(memory_space=pltpu.SMEM)] + [vmem] * 8,
        out_specs=[vmem, vmem],
        scratch_shapes=[pltpu.VMEM((side, SUB, LANES), f32)],
        compiler_params=pltpu.CompilerParams(vmem_limit_bytes=VMEM_LIMIT),
        name="coarsen",
    )(table, rows, light, land, from_south, from_north, from_west, from_east, picks)


def lines_kernel(levels, side, table_ref, quad_ref, low_ref, high_ref, low_in_ref, high_in_ref, ends_ref):
    tile_blocks = LANES // side
    pairs = quad_ref.shape[1] // levels
    lane = lane_ids()
    spot = lane >> 1

    def body(lt, carry):
        packed = jnp.zeros((SUB, LANES), jnp.float32)
        for m in range(pairs):
            at = pl.multiple_of(m * levels + lt * SUB, SUB)
            blocks = []
            for b in range(tile_blocks):
                value = quad_ref[table_ref[TILE_OWNER, b], pl.ds(at, SUB), :]
                blocks.append(jnp.where(table_ref[TILE_WET, b] == 1, value, 0.0))
            parts = regroup(blocks, side)
            for p in range(2):
                t = 2 * m + p
                chan = pl.ds(pl.multiple_of(t * levels + lt * SUB, SUB), SUB)
                high_in, high, low, low_in = parts[4 * p : 4 * p + 4]
                low_ref[chan, :] = low
                high_ref[chan, :] = high
                low_in_ref[chan, :] = low_in
                high_in_ref[chan, :] = high_in
                for k, line in ((2 * t, low), (2 * t + 1, high)):
                    packed = jnp.where(spot == k, turned(line, 1 + 2 * k), packed)
        ends_ref[pl.ds(pl.multiple_of(lt * SUB, SUB), SUB), :] = packed
        return carry

    lax.fori_loop(0, levels // SUB, body, 0)


def tile_lines(table, quads, levels, side):
    channels = quads.shape[1] // levels * 2 * levels
    vmem = pl.BlockSpec(memory_space=pltpu.VMEM)
    line = jax.ShapeDtypeStruct((channels, LANES), jnp.float32)
    return pl.pallas_call(
        functools.partial(lines_kernel, levels, side),
        out_shape=[line] * 4 + [jax.ShapeDtypeStruct((levels, LANES), jnp.float32)],
        in_specs=[pl.BlockSpec(memory_space=pltpu.SMEM), vmem],
        out_specs=[vmem] * 5,
        compiler_params=pltpu.CompilerParams(vmem_limit_bytes=VMEM_LIMIT),
        name="tile_lines",
    )(table, quads)


def line_kernel(
    levels,
    low_ref,
    high_ref,
    low_in_ref,
    high_in_ref,
    below_ref,
    above_ref,
    west_ref,
    east_ref,
    phys_ref,
    low_out_ref,
    high_out_ref,
    coef_ref,
    moved_ref,
    ends_ref,
):
    channels = low_ref.shape[0]
    tracer_count = channels // levels
    level_tiles = levels // SUB
    lane = lane_ids()
    odd = (lane & 1) == 1
    spans = [slice(0, LANES), slice(LANES, 2 * LANES)]
    flag_row = 6 * levels
    lines = (
        (low_ref, low_in_ref, below_ref, low_out_ref),
        (high_ref, above_ref, high_in_ref, high_out_ref),
    )

    def flag(f, h):
        return phys_ref[flag_row + f : flag_row + f + 1, spans[h]]

    above_mix = [jnp.zeros((SUB, LANES), jnp.float32)] * 2
    for lt in range(level_tiles):
        at = slice(lt * SUB, (lt + 1) * SUB)
        from_west = west_ref[lt * SUB : (lt + 1) * SUB, :]
        from_east = east_ref[lt * SUB : (lt + 1) * SUB, :]
        ends_ref[at, :] = jnp.where(odd, turned(from_east, -2), from_west)
        for h in range(2):
            faces = [
                phys_ref[n * levels + lt * SUB : n * levels + (lt + 1) * SUB, spans[h]] for n in (0, 1, 4, 5)
            ]
            for n, value in enumerate(transport(faces, [flag(f, h) for f in range(4)])):
                coef_ref[n, at, spans[h]] = value
            mix = phys_ref[3 * levels + lt * SUB : 3 * levels + (lt + 1) * SUB, spans[h]]
            set_mixing(coef_ref, at, spans[h], mix, above_mix[h], lt == level_tiles - 1)
            above_mix[h] = mix
    set_blank(moved_ref, channels)

    def advect(lt, carry):
        at = pl.multiple_of(lt * SUB, SUB)
        ends = ends_ref[pl.ds(at, SUB), :]
        for h in range(2):
            here_ref, north_ref, south_ref, _ = lines[h]
            c, e, w, n, s = (coef_ref[k, pl.ds(at, SUB), spans[h]] for k in range(5))
            for t in range(tracer_count):
                chan = pl.multiple_of(t * levels + lt * SUB, SUB)
                here = here_ref[pl.ds(chan, SUB), :]
                end = turned(ends, -2 * (2 * t + h))
                west = jnp.where(lane == 0, end, turned(here, 1))
                east = jnp.where(lane == LANES - 1, end, turned(here, -1))
                moved_ref[pl.ds(pl.multiple_of(SUB + chan, SUB), SUB), spans[h]] = (
                    c * here
                    + (e * east + w * west)
                    + (n * north_ref[pl.ds(chan, SUB), :] + s * south_ref[pl.ds(chan, SUB), :])
                )
        return carry

    lax.fori_loop(0, level_tiles, advect, 0, unroll=True)

    def store(t, at, h, value):
        if t is not None:
            lines[h][3][pl.ds(at, SUB), :] = value

    def warm_at(lt, h):
        return phys_ref[pl.ds(pl.multiple_of(2 * levels + lt * SUB, SUB), SUB), spans[h]]

    light = [flag(LIGHT, h) for h in range(2)]
    wet = [flag(WET, h) for h in range(2)]
    mix_and_react(levels, tracer_count, spans, moved_ref, coef_ref, light, wet, warm_at, store)


def line_step(low, high, low_in, high_in, below, above, from_west, from_east, phys, levels):
    channels = low.shape[0]
    vmem = pl.BlockSpec(memory_space=pltpu.VMEM)
    f32 = jnp.float32
    line = jax.ShapeDtypeStruct((channels, LANES), f32)
    return pl.pallas_call(
        functools.partial(line_kernel, levels),
        out_shape=[line, line],
        in_specs=[vmem] * 9,
        out_specs=[vmem, vmem],
        scratch_shapes=[
            pltpu.VMEM((8, levels, 2 * LANES), f32),
            pltpu.VMEM((channels + 2 * SUB, 2 * LANES), f32),
            pltpu.VMEM((levels, LANES), f32),
        ],
        compiler_params=pltpu.CompilerParams(vmem_limit_bytes=VMEM_LIMIT),
        name="line_step",
    )(low, high, low_in, high_in, below, above, from_west, from_east, phys)


def hand_kernel(levels, side, table_ref, below_ref, above_ref, *refs):
    out_ref = refs[-1]
    group = LANES // side
    rounds = below_ref.shape[0] // levels // group
    half = group // 2

    def body(lt, carry):
        for i in range(rounds):
            for part in range(2):
                lines = []
                for g in range(half):
                    t = i * group + part * half + g
                    chan = pl.ds(pl.multiple_of(t * levels + lt * SUB, SUB), SUB)
                    lines += [above_ref[chan, :], below_ref[chan, :]]
                row = pl.multiple_of((part * rounds + i) * levels + lt * SUB, SUB)
                for b, value in enumerate(regroup(lines, side)):
                    out_ref[table_ref[TILE_OWNER, b], pl.ds(row, SUB), :] = value
        return carry

    lax.fori_loop(0, levels // SUB, body, 0)


def hand_on(table, below, above, levels, side, *after):
    lon_count = lax.axis_size("lon")
    rows = 2 * below.shape[0] * side // LANES
    vmem = pl.BlockSpec(memory_space=pltpu.VMEM)
    return pl.pallas_call(
        functools.partial(hand_kernel, levels, side),
        out_shape=jax.ShapeDtypeStruct((lon_count, rows, LANES), jnp.float32),
        in_specs=[pl.BlockSpec(memory_space=pltpu.SMEM), vmem, vmem]
        + [pl.BlockSpec(memory_space=pl.ANY)] * len(after),
        out_specs=vmem,
        compiler_params=pltpu.CompilerParams(vmem_limit_bytes=VMEM_LIMIT),
        name="hand_on",
    )(table, below, above, *after)


def gate_kernel(*refs):
    pass


def gate(values, *others):
    anywhere = pl.BlockSpec(memory_space=pl.ANY)
    count = len(values)
    return pl.pallas_call(
        gate_kernel,
        out_shape=[jax.ShapeDtypeStruct(x.shape, x.dtype) for x in values],
        in_specs=[anywhere] * (count + len(others)),
        out_specs=[anywhere] * count,
        input_output_aliases={i: i for i in range(count)},
        name="gate",
    )(*values, *others)


def heat_kernel(
    levels,
    side,
    factor,
    table_ref,
    chl_ref,
    light_ref,
    land_ref,
    widen_ref,
    after_ref,
    out_ref,
    rows_ref,
    wide_ref,
):
    tile_blocks = land_ref.shape[1] // side
    halves = side * side // LANES
    group = LANES // side
    fine_cols = light_ref.shape[1]
    fine_rows = light_ref.shape[0]
    f32 = jnp.float32
    group_id = lane_ids() >> (side.bit_length() - 1)

    def place(lt, carry):
        at = pl.multiple_of(lt * SUB, SUB)
        for h in range(halves):
            blocks = []
            for b in range(tile_blocks):
                owner = table_ref[TILE_OWNER, b]
                values = chl_ref[owner, pl.ds(at, SUB), h * LANES : (h + 1) * LANES]
                blocks.append(jnp.where(table_ref[TILE_WET, b] == 1, values, 0.0))
            for r in range(group):
                line = None
                for b in range(tile_blocks):
                    piece = turned(blocks[b], side * (b - r))
                    line = piece if line is None else jnp.where(group_id == b, piece, line)
                rows_ref[pl.ds(pl.multiple_of((h * group + r) * levels + lt * SUB, SUB), SUB), :] = line
        return carry

    lax.fori_loop(0, levels // SUB, place, 0, unroll=True)
    wet = land_ref[...].astype(f32)
    widen = widen_ref[...]
    above = jnp.zeros_like(wet)
    passing = jnp.ones_like(wet)
    for l in range(levels):
        chl = rows_ref[pl.ds(l, side, stride=levels), :]
        above = above + (0.04 + 0.02 * chl)
        through = jnp.exp(-above)
        kept = (passing - through) * wet
        passing = through
        high = kept.astype(jnp.bfloat16)
        low = (kept - high.astype(f32)).astype(jnp.bfloat16)
        wide_ref[l * side : (l + 1) * side, :] = jnp.dot(
            high, widen, preferred_element_type=f32
        ) + jnp.dot(low, widen, preferred_element_type=f32)

    sub = lax.broadcasted_iota(jnp.int32, (SUB, LANES), 0)
    sources = []
    for m in range(fine_rows // SUB):
        start = (m * SUB // factor) // SUB * SUB
        index = jnp.zeros_like(sub)
        for r in range(1, side):
            index = index + jnp.where(sub + m * SUB >= r * factor, 1, 0)
        sources.append((start, index - start))

    def spread(l, carry):
        for c in range(fine_cols // LANES):
            span = slice(c * LANES, (c + 1) * LANES)
            for m in range(0, fine_rows // SUB, 2):
                both = []
                for n in (m, m + 1):
                    start, index = sources[n]
                    lines = wide_ref[pl.ds(pl.multiple_of(l * side + start, SUB), SUB), span]
                    lines = jnp.take_along_axis(lines, index, axis=0)
                    both.append(lines * light_ref[n * SUB : (n + 1) * SUB, span])
                out_ref[l, m * SUB : (m + 2) * SUB, span] = jnp.concatenate(both, axis=0).astype(jnp.bfloat16)
        return carry

    lax.fori_loop(0, levels, spread, 0, unroll=4)


def heat(table, chl, light, land, levels, widen, after):
    side = land.shape[0]
    factor = light.shape[0] // side
    vmem = pl.BlockSpec(memory_space=pltpu.VMEM)
    return pl.pallas_call(
        functools.partial(heat_kernel, levels, side, factor),
        out_shape=jax.ShapeDtypeStruct((levels,) + light.shape, jnp.bfloat16),
        in_specs=[pl.BlockSpec(memory_space=pltpu.SMEM), vmem, vmem, vmem, vmem]
        + [pl.BlockSpec(memory_space=pl.ANY)],
        out_specs=vmem,
        scratch_shapes=[
            pltpu.VMEM((side * levels, LANES), jnp.float32),
            pltpu.VMEM((side * levels, light.shape[1]), jnp.float32),
        ],
        compiler_params=pltpu.CompilerParams(vmem_limit_bytes=VMEM_LIMIT),
        name="heat",
    )(table, chl, light, land, widen, after)


def widened(x, rows, width):
    return jnp.pad(x, ((0, rows - x.shape[0]), (0, width - x.shape[1])))


def on_device(tracers, phys_fine, mix_coarse, surf_light, land_mask, owner_map):
    f32 = jnp.float32
    slot_count = tracers.shape[0]
    side = land_mask.shape[0]
    levels = mix_coarse.shape[2]
    tile_blocks = land_mask.shape[1] // side
    factor = phys_fine.shape[0] // side
    fine_cols = phys_fine.shape[1]
    group = LANES // side

    fine = jnp.transpose(phys_fine, (0, 2, 1))
    mix = jnp.transpose(mix_coarse, (0, 2, 1))
    wet = land_mask.astype(f32)
    width = fine_cols

    northward = jnp.concatenate(
        [
            widened(fine[-1, levels : 2 * levels, :].astype(f32), levels, width),
            widened(wet[-1:], 1, width),
        ],
        axis=0,
    )
    southward = widened(wet[:1], 1, width)
    last_face = jnp.mean(
        fine[:, :levels, fine_cols - 1].astype(f32).reshape(side, factor, levels), axis=1
    )
    face_pack = jnp.pad(
        last_face.reshape(side // group, group, levels // SUB, SUB).transpose(3, 1, 0, 2),
        ((0, 0), (0, 0), (0, 0), (0, group - levels // SUB)),
    ).reshape(SUB, LANES)
    eastward = jnp.concatenate([face_pack, widened(wet[:, -1][None], 1, LANES)], axis=0)
    westward = widened(wet[:, 0][None], 1, LANES)

    from_south = lax.ppermute(northward, "lat", along("lat", 1, False))
    from_north = lax.ppermute(southward, "lat", along("lat", -1, False))
    from_west = lax.ppermute(eastward, "lon", along("lon", 1, True))
    from_east = lax.ppermute(westward, "lon", along("lon", -1, True))

    fine_id = jnp.arange(fine_cols)[:, None]
    coarse_id = jnp.arange(land_mask.shape[1])[None, :]
    member = (fine_id // factor == coarse_id).astype(jnp.bfloat16)
    final = (fine_id == factor * coarse_id + factor - 1).astype(jnp.bfloat16)
    picks = jnp.concatenate([final, member], axis=1)

    table = routing(owner_map, slot_count, tile_blocks)
    def to_north(x):
        return lax.ppermute(x, "lat", along("lat", 1, False))

    def to_south(x):
        return lax.ppermute(x, "lat", along("lat", -1, False))

    def to_east(x):
        return lax.ppermute(x, "lon", along("lon", 1, True))

    def to_west(x):
        return lax.ppermute(x, "lon", along("lon", -1, True))

    def across(x):
        return lax.all_to_all(x, "lon", 0, 0, tiled=True)

    quads, west, east = first_edges(table, tracers, levels, side)
    quads = across(quads)
    rows = coarse_rows(fine, mix, picks)
    phys, line_phys = coarsen(
        table, rows, surf_light, land_mask, from_south, from_north, from_west, from_east, picks
    )
    phys = across(phys)
    low, high, low_in, high_in, ends = tile_lines(table, quads, levels, side)
    below, above = to_north(high), to_south(low)
    west, east = gate((west, east), phys)
    rim_w, rim_e = to_east(east), to_west(west)
    ends_w, ends_e = to_east(ends), to_west(ends)
    rims = across(hand_on(table, below, above, levels, side, phys, ends_w, ends_e))
    new_low, new_high = line_step(
        low, high, low_in, high_in, below, above, ends_w, ends_e, line_phys, levels
    )
    below, above = to_north(new_high), to_south(new_low)
    partial = inner(table, tracers, phys, levels, side)
    (handed,) = gate((hand_on(table, below, above, levels, side),), rims, rim_w, rim_e, partial)
    new_rims = across(handed)
    current, west, east = step(table, partial, phys, rims, rim_w, rim_e, levels, side, False)
    rim_w, rim_e = to_east(east), to_west(west)
    partial = inner(table, current, phys, levels, side)
    chl = across(last_chl(table, partial, phys, new_rims, rim_w, rim_e, levels, side))
    (current,) = step(table, partial, phys, new_rims, rim_w, rim_e, levels, side, True)
    heating = heat(table, chl, surf_light, land_mask, levels, jnp.transpose(member), current)
    return current, heating


def solution(mesh):
    in_specs = (
        P(("lat", "lon"), None, None),
        P("lat", "lon", None),
        P("lat", "lon", None),
        P("lat", "lon"),
        P("lat", "lon"),
        P("lat", None),
    )
    out_specs = (P(("lat", "lon"), None, None), P(None, "lat", "lon"))
    return jax.shard_map(
        on_device, mesh=mesh, in_specs=in_specs, out_specs=out_specs, check_vma=False
    )
```

```python
import functools

import jax
import jax.numpy as jnp
from jax import lax
from jax.experimental import pallas as pl
from jax.experimental.pallas import tpu as pltpu
from jax.sharding import PartitionSpec as P

LANES = 128
SUB = 8

diffuse_rate = 0.08
nano_chl_index = 10
diat_chl_index = 11

SLOT_TILE, SLOT_FULL, SLOT_WEST, SLOT_EAST, TILE_OWNER, TILE_WET, TILE_BASE = range(7)
TABLE_ROWS = 8

OPEN_EAST, OPEN_NORTH, OPEN_WEST, OPEN_SOUTH, LIGHT, WET = range(6)

VMEM_LIMIT = 48 * 1024 * 1024


def positive(value):
    return jnp.maximum(value, 0.0)


def lane_ids(rows=SUB):
    return lax.broadcasted_iota(jnp.int32, (rows, LANES), 1)


def turned(value, by):
    by = by % LANES
    return value if by == 0 else pltpu.roll(value, by, 1)


def quotient(value, by):
    if by & (by - 1) == 0:
        return lax.shift_right_logical(value, jnp.int32(by.bit_length() - 1))
    return lax.div(value, jnp.int32(by))


def remainder(value, by):
    if by & (by - 1) == 0:
        return value & (by - 1)
    return lax.rem(value, jnp.int32(by))


def along(axis, by, closed):
    size = lax.axis_size(axis)
    pairs = [(i, (i + by) % size) for i in range(size)]
    return [p for p in pairs if closed or p[1] == p[0] + by]


def table_kernel(slot_count, tile_blocks, lon_count, row_ref, out_ref, used_ref):
    me = lax.axis_index("lon")
    block_count = row_ref.shape[1]
    width = out_ref.shape[1]

    def clear(i, carry):
        for r in range(TABLE_ROWS):
            out_ref[r, i] = 0
        return carry

    lax.fori_loop(0, width, clear, 0)

    def unuse(i, carry):
        used_ref[0, i] = 0
        used_ref[1, i] = 0
        return carry

    lax.fori_loop(0, lon_count, unuse, 0)
    out_ref[TILE_BASE, 0] = me * tile_blocks

    def visit(k, carry):
        code = row_ref[0, k]
        safe = jnp.maximum(code, 0)
        owner = remainder(quotient(safe, slot_count), lon_count)
        slot = remainder(safe, slot_count)
        tile = quotient(k, tile_blocks)

        @pl.when((code >= 0) & (owner == me))
        def _():
            west = row_ref[0, remainder(k + block_count - 1, block_count)]
            east = row_ref[0, remainder(k + 1, block_count)]
            out_ref[SLOT_TILE, slot] = tile
            out_ref[SLOT_FULL, slot] = 1
            out_ref[SLOT_WEST, slot] = remainder(jnp.maximum(west, 0), slot_count)
            out_ref[SLOT_EAST, slot] = remainder(jnp.maximum(east, 0), slot_count)
            used_ref[0, tile] = 1

        @pl.when((code >= 0) & (tile == me))
        def _():
            local = remainder(k, tile_blocks)
            out_ref[TILE_OWNER, local] = owner
            out_ref[TILE_WET, local] = 1
            used_ref[1, owner] = 1

        return carry

    lax.fori_loop(0, block_count, visit, 0, unroll=8)

    def give(target, filled, line, count):
        def one(i, carry):
            def look(j, done):
                take = (done == 0) & (used_ref[line, j] == 0)

                @pl.when(take)
                def _():
                    out_ref[target, i] = j
                    used_ref[line, j] = 1

                return jnp.where(take, 1, done)

            @pl.when(out_ref[filled, i] == 0)
            def _():
                lax.fori_loop(0, lon_count, look, 0)

            return carry

        lax.fori_loop(0, count, one, 0)

    give(SLOT_TILE, SLOT_FULL, 0, slot_count)
    give(TILE_OWNER, TILE_WET, 1, tile_blocks)


def routing(row, slot_count, tile_blocks):
    lon_count = lax.axis_size("lon")
    width = max(slot_count, tile_blocks, lon_count)
    return pl.pallas_call(
        functools.partial(table_kernel, slot_count, tile_blocks, lon_count),
        out_shape=jax.ShapeDtypeStruct((TABLE_ROWS, width), jnp.int32),
        in_specs=[pl.BlockSpec(memory_space=pltpu.SMEM)],
        out_specs=pl.BlockSpec(memory_space=pltpu.SMEM),
        scratch_shapes=[pltpu.SMEM((2, lon_count), jnp.int32)],
        name="routing",
    )(row)


def merged(pieces, ids):
    packed = pieces[0]
    for g in range(1, len(pieces)):
        packed = jnp.where(ids == g, pieces[g], packed)
    return packed


def pack_columns(first, second, side):
    lane = lane_ids()
    odd = (lane & 1) == 1
    here = (lane & (side - 1)) >> 1
    there = ((lane + 1) & (side - 1)) >> 1
    even_ends = merged([turned(v, 1 + 2 * g) for g, v in enumerate(first)], here)
    odd_ends = merged([turned(v, 2 * g) for g, v in enumerate(second)], there)
    return jnp.where(odd, even_ends, odd_ends), jnp.where(odd, odd_ends, even_ends)


def pack_quads(first, second, side):
    low = lane_ids() < LANES // 2
    both = [jnp.where(low, a, b) for a, b in zip(first, second)]
    turns = [turned(v, 2 * side + (g % 2) * (LANES // 2)) for g, v in enumerate(both)]
    return [jnp.where(low, turns[g], turns[g + 1]) for g in range(0, len(turns), 2)]


def regroup(values, side):
    values = list(values)
    ids = lane_ids() >> (side.bit_length() - 1)
    bit = 1
    while bit < len(values):
        keep = (ids & bit) == 0
        for n in range(len(values)):
            if n & bit == 0:
                a, b = values[n], values[n + bit]
                values[n] = jnp.where(keep, a, turned(b, side * bit))
                values[n + bit] = jnp.where(keep, turned(a, -side * bit), b)
        bit *= 2
    return values


def edges_kernel(levels, side, table_ref, cell_ref, rows_ref, west_ref, east_ref):
    group = LANES // side
    rounds = cell_ref.shape[1] // levels // group
    level_tiles = levels // SUB

    def body(lt, carry):
        for i in range(rounds):
            row = pl.multiple_of(i * levels + lt * SUB, SUB)
            first, second = [], []
            for g in range(group):
                at = pl.multiple_of((i * group + g) * levels + lt * SUB, SUB)
                first.append(cell_ref[0, pl.ds(at, SUB), 0:LANES])
                second.append(cell_ref[0, pl.ds(at, SUB), LANES : 2 * LANES])
            west, east = pack_columns(first, second, side)
            west_ref[0, pl.ds(row, SUB), :] = west
            east_ref[0, pl.ds(row, SUB), :] = east
            for n, quad in enumerate(pack_quads(first, second, side)):
                at = pl.multiple_of((i * (group // 2) + n) * levels + lt * SUB, SUB)
                rows_ref[0, pl.ds(at, SUB), :] = quad
        return carry

    lax.fori_loop(0, level_tiles, body, 0, unroll=True)


def first_edges(table, tracers, levels, side):
    slot_count, channels, cell_count = tracers.shape
    lon_count = lax.axis_size("lon")
    rows = channels * side // LANES
    f32 = jnp.float32
    by_slot = pl.BlockSpec((1, rows, LANES), lambda s, t: (s, 0, 0))
    return pl.pallas_call(
        functools.partial(edges_kernel, levels, side),
        out_shape=[
            jax.ShapeDtypeStruct((lon_count, 4 * rows, LANES), f32),
            jax.ShapeDtypeStruct((slot_count, rows, LANES), f32),
            jax.ShapeDtypeStruct((slot_count, rows, LANES), f32),
        ],
        grid_spec=pltpu.PrefetchScalarGridSpec(
            num_scalar_prefetch=1,
            grid=(slot_count,),
            in_specs=[pl.BlockSpec((1, channels, cell_count), lambda s, t: (s, 0, 0))],
            out_specs=[
                pl.BlockSpec((1, 4 * rows, LANES), lambda s, t: (t[SLOT_TILE, s], 0, 0)),
                by_slot,
                by_slot,
            ],
        ),
        compiler_params=pltpu.CompilerParams(vmem_limit_bytes=VMEM_LIMIT),
        name="first_edges",
    )(table, tracers)


def growth(
    nitrogen,
    phosphate,
    silicate,
    iron_free,
    nano_carbon,
    diat_carbon,
    micro_zoo,
    meso_zoo,
    par_light,
    warm_factor,
):
    limit_nitro = nitrogen / (0.5 + nitrogen)
    limit_phos = positive(phosphate) / (0.3 + positive(phosphate))
    limit_iron = positive(iron_free) / (0.2 + positive(iron_free))
    limit_sil = positive(silicate) / (1.0 + positive(silicate))
    nutr_nano = jnp.minimum(jnp.minimum(limit_nitro, limit_phos), limit_iron)
    nutr_diat = jnp.minimum(nutr_nano, limit_sil)
    lit = warm_factor * par_light
    prod_nano = 0.1 * lit / (par_light + 0.5) * nutr_nano * nano_carbon
    prod_diat = 0.12 * lit / (par_light + 1.0) * nutr_diat * diat_carbon
    graze_nano = 0.08 * warm_factor * micro_zoo / (1.0 + positive(nano_carbon))
    graze_diat = 0.06 * warm_factor * meso_zoo / (1.0 + positive(diat_carbon))
    return prod_nano, prod_diat, graze_nano, graze_diat


CHL_TRACERS = (3, 4, 5, 6, 7, 8, 9, 10, 11, 15, 16)
CHL_RUN = 3
CHL_BLOCKS = sorted({tracer // CHL_RUN for tracer in CHL_TRACERS})


def chl_after(mixed, par_light, warm_factor):
    (
        nitrate,
        ammonium,
        phosphate,
        silicate,
        iron_free,
        nano_carbon,
        diat_carbon,
        nano_chl,
        diat_chl,
        micro_zoo,
        meso_zoo,
    ) = mixed
    prod_nano, prod_diat, graze_nano, graze_diat = growth(
        positive(nitrate) + positive(ammonium),
        phosphate,
        silicate,
        iron_free,
        nano_carbon,
        diat_carbon,
        micro_zoo,
        meso_zoo,
        par_light,
        warm_factor,
    )
    nano_chl = nano_chl + 0.03 * prod_nano - (graze_nano + 0.02) * nano_chl
    diat_chl = diat_chl + 0.03 * prod_diat - (graze_diat + 0.02) * diat_chl
    return nano_chl, diat_chl


def react(mixed, par_light, warm_factor):
    (
        carbon_dis,
        alkalinity,
        oxygen,
        nitrate,
        ammonium,
        phosphate,
        silicate,
        iron_free,
        nano_carbon,
        diat_carbon,
        nano_chl,
        diat_chl,
        nano_iron,
        diat_iron,
        diat_silica,
        micro_zoo,
        meso_zoo,
        dissolved_org,
        small_part,
        big_part,
        small_iron,
        big_iron,
        big_silica,
        calcite,
    ) = mixed
    nitrogen = positive(nitrate) + positive(ammonium)
    ammon_share = (positive(ammonium) + 0.01) / (nitrogen + 0.02)
    prod_nano, prod_diat, graze_nano, graze_diat = growth(
        nitrogen,
        phosphate,
        silicate,
        iron_free,
        nano_carbon,
        diat_carbon,
        micro_zoo,
        meso_zoo,
        par_light,
        warm_factor,
    )
    loss_nano = graze_nano + 0.02
    loss_diat = graze_diat + 0.02
    eaten_nano = graze_nano * nano_carbon
    eaten_diat = graze_diat * diat_carbon
    death_micro = 0.03 * micro_zoo * positive(micro_zoo)
    death_meso = 0.03 * meso_zoo * positive(meso_zoo)
    remin_doc = 0.03 * warm_factor * dissolved_org
    remin_poc = 0.02 * warm_factor * small_part
    remin_goc = 0.01 * warm_factor * big_part
    nitrify = 0.05 * ammonium
    melt_si = 0.02 * big_silica
    melt_cal = 0.01 * calcite
    melt_sfe = 0.02 * small_iron
    melt_bfe = 0.01 * big_iron
    uptake = prod_nano + prod_diat
    remin_total = remin_doc + remin_poc + remin_goc
    calcify = 0.02 * prod_nano
    gained = remin_total - uptake
    shell = melt_cal - calcify
    by_ammon = ammon_share * uptake
    by_nitrate = 0.16 * (uptake - by_ammon - nitrify)
    return [
        carbon_dis + gained + shell,
        alkalinity + 2.0 * shell + by_nitrate,
        oxygen - 1.3 * gained - 0.32 * nitrify,
        nitrate - by_nitrate,
        ammonium + 0.16 * (remin_total - by_ammon - nitrify),
        phosphate + 0.01 * gained,
        silicate + melt_si - 0.15 * prod_diat,
        iron_free + melt_sfe + melt_bfe - 0.005 * uptake,
        nano_carbon + prod_nano - loss_nano * nano_carbon,
        diat_carbon + prod_diat - loss_diat * diat_carbon,
        nano_chl + 0.03 * prod_nano - loss_nano * nano_chl,
        diat_chl + 0.03 * prod_diat - loss_diat * diat_chl,
        nano_iron + 0.005 * prod_nano - loss_nano * nano_iron,
        diat_iron + 0.005 * prod_diat - loss_diat * diat_iron,
        diat_silica + 0.15 * prod_diat - loss_diat * diat_silica,
        micro_zoo + 0.3 * eaten_nano - death_micro,
        meso_zoo + 0.3 * eaten_diat - death_meso,
        dissolved_org + 0.3 * eaten_nano + 0.02 * nano_carbon - remin_doc,
        small_part + 0.4 * eaten_nano + death_micro - remin_poc,
        big_part + 0.4 * eaten_diat + 0.02 * diat_carbon + death_meso - remin_goc,
        small_iron + loss_nano * nano_iron - melt_sfe,
        big_iron + loss_diat * diat_iron - melt_bfe,
        big_silica + loss_diat * diat_silica - melt_si,
        calcite + calcify - melt_cal,
    ]


def transport(faces, opens):
    flow_e, flow_n, flow_w, flow_s = (face * is_open for face, is_open in zip(faces, opens))
    open_e, open_n, open_w, open_s = opens
    out_e, in_e = jnp.maximum(flow_e, 0.0), jnp.minimum(flow_e, 0.0)
    out_n, in_n = jnp.maximum(flow_n, 0.0), jnp.minimum(flow_n, 0.0)
    in_w, out_w = jnp.maximum(flow_w, 0.0), jnp.minimum(flow_w, 0.0)
    in_s, out_s = jnp.maximum(flow_s, 0.0), jnp.minimum(flow_s, 0.0)
    drift = diffuse_rate * (open_w + open_e + open_s + open_n)
    return (
        1.0 - (out_e - out_w) - (out_n - out_s) - drift,
        diffuse_rate * open_e - in_e,
        diffuse_rate * open_w + in_w,
        diffuse_rate * open_n - in_n,
        diffuse_rate * open_s + in_s,
    )


def set_mixing(coef_ref, at, span, mix, above, bottom):
    sub = lax.broadcasted_iota(jnp.int32, (SUB, LANES), 0)
    mix_up = pltpu.roll(jnp.where(sub == SUB - 1, above, mix), 1, 0)
    if bottom:
        mix = jnp.where(sub == SUB - 1, 0.0, mix)
    coef_ref[5, at, span] = 1.0 - mix - mix_up
    coef_ref[6, at, span] = mix
    coef_ref[7, at, span] = mix_up


def set_blank(moved_ref, channels):
    blank = jnp.zeros((SUB, moved_ref.shape[1]), jnp.float32)
    moved_ref[0:SUB, :] = blank
    moved_ref[SUB + channels : 2 * SUB + channels, :] = blank


def mixed_at(levels, count, span, moved_ref, coef_ref, lt):
    sub = lax.broadcasted_iota(jnp.int32, (SUB, LANES), 0)
    at = pl.multiple_of(lt * SUB, SUB)
    mix_c, mix_d, mix_u = (coef_ref[n, pl.ds(at, SUB), span] for n in (5, 6, 7))
    mixed = []
    for t in range(count):
        base = t * levels + lt * SUB
        before = moved_ref[pl.ds(pl.multiple_of(base, SUB), SUB), span]
        now = moved_ref[pl.ds(pl.multiple_of(base + SUB, SUB), SUB), span]
        after = moved_ref[pl.ds(pl.multiple_of(base + 2 * SUB, SUB), SUB), span]
        up = pltpu.roll(jnp.where(sub == SUB - 1, before, now), 1, 0)
        down = pltpu.roll(jnp.where(sub == 0, after, now), SUB - 1, 0)
        mixed.append(mix_c * now + mix_d * down + mix_u * up)
    return mixed


def lit_at(nano_chl, diat_chl, light, depth):
    sub = lax.broadcasted_iota(jnp.int32, (SUB, LANES), 0)
    absorb = 0.04 + 0.02 * (positive(nano_chl) + positive(diat_chl))
    total = absorb
    for by in (1, 2, 4):
        total = total + jnp.where(sub >= by, pltpu.roll(total, by, 0), 0.0)
    above = depth + (total - absorb)
    return light * jnp.exp(-(above + 0.5 * absorb)), depth + total[SUB - 1 : SUB, :]


def mix_and_react(levels, tracer_count, spans, moved_ref, coef_ref, light, wet, warm_at, store):
    def reacting(lt, carry):
        depths = []
        halves_new = []
        for h, span in enumerate(spans):
            mixed = mixed_at(levels, tracer_count, span, moved_ref, coef_ref, lt)
            par_light, depth = lit_at(mixed[nano_chl_index], mixed[diat_chl_index], light[h], carry[h])
            depths.append(depth)
            halves_new.append([value * wet[h] for value in react(mixed, par_light, warm_at(lt, h))])
            for t in range(tracer_count):
                store(t, pl.multiple_of(t * levels + lt * SUB, SUB), h, halves_new[h][t])
        store(None, lt, None, halves_new)
        return tuple(depths)

    start = tuple(jnp.zeros((1, LANES), jnp.float32) for _ in spans)
    lax.fori_loop(0, levels // SUB, reacting, start, unroll=True)


def block_faces(phys_ref, spans, levels, side, lt):
    group = LANES // side
    pack_at = 4 * levels + SUB
    lane = lane_ids()
    first_col = (lane & (side - 1)) == 0
    first_row = lane < side
    west_pack = phys_ref[0, pack_at : pack_at + SUB, spans[0]]
    south_pack = phys_ref[0, pack_at : pack_at + SUB, spans[1]]
    east = [phys_ref[0, lt * SUB : (lt + 1) * SUB, span] for span in spans]
    north = [phys_ref[0, levels + lt * SUB : levels + (lt + 1) * SUB, span] for span in spans]
    faces = []
    for h in range(len(spans)):
        west = jnp.where(first_col, turned(west_pack, -(h * group + lt)), turned(east[h], 1))
        before = turned(south_pack, -side * lt) if h == 0 else turned(north[h - 1], side)
        south = jnp.where(first_row, before, turned(north[h], side))
        faces.append((east[h], north[h], west, south))
    return faces


def inner_kernel(levels, side, table_ref, cell_ref, phys_ref, out_ref, coef_ref):
    channels, cell_count = cell_ref.shape[1:]
    tracer_count = channels // levels
    halves = cell_count // LANES
    level_tiles = levels // SUB
    spans = [slice(h * LANES, (h + 1) * LANES) for h in range(halves)]
    full = table_ref[SLOT_FULL, pl.program_id(0)] == 1

    @pl.when(jnp.logical_not(full))
    def _():
        out_ref[...] = jnp.zeros_like(out_ref)

    @pl.when(full)
    def _():
        lane = lane_ids()
        col = lane & (side - 1)
        first_row = lane < side
        last_row = lane >= LANES - side
        flag_row = 4 * levels

        def flag(f, h):
            return phys_ref[0, flag_row + f : flag_row + f + 1, spans[h]]

        for lt in range(level_tiles):
            at = slice(lt * SUB, (lt + 1) * SUB)
            for h, faces in enumerate(block_faces(phys_ref, spans, levels, side, lt)):
                c, e, w, n, s = transport(faces, [flag(f, h) for f in range(4)])
                e = jnp.where(col == side - 1, 0.0, e)
                w = jnp.where(col == 0, 0.0, w)
                if h == halves - 1:
                    n = jnp.where(last_row, 0.0, n)
                if h == 0:
                    s = jnp.where(first_row, 0.0, s)
                for k, value in enumerate((c, e, w, n, s)):
                    coef_ref[k, at, spans[h]] = value

        def advect(lt, carry):
            at = pl.multiple_of(lt * SUB, SUB)
            coef = [[coef_ref[n, pl.ds(at, SUB), span] for n in range(5)] for span in spans]
            for t in range(tracer_count):
                chan = pl.multiple_of(t * levels + lt * SUB, SUB)
                here = [cell_ref[0, pl.ds(chan, SUB), span] for span in spans]
                up = [turned(value, side) for value in here]
                down = [turned(value, -side) for value in here]
                for h in range(halves):
                    south = up[h] if h == 0 else jnp.where(first_row, up[h - 1], up[h])
                    north = down[h] if h == halves - 1 else jnp.where(last_row, down[h + 1], down[h])
                    c, e, w, n, s = coef[h]
                    out_ref[0, pl.ds(chan, SUB), spans[h]] = (
                        c * here[h]
                        + (e * turned(here[h], -1) + w * turned(here[h], 1))
                        + (n * north + s * south)
                    )
            return carry

        lax.fori_loop(0, level_tiles, advect, 0, unroll=True)


def inner(table, cells, phys, levels, side):
    slot_count, channels, cell_count = cells.shape
    phys_rows = phys.shape[1]
    by_slot = pl.BlockSpec((1, channels, cell_count), lambda s, t: (s, 0, 0))
    return pl.pallas_call(
        functools.partial(inner_kernel, levels, side),
        out_shape=jax.ShapeDtypeStruct(cells.shape, jnp.float32),
        grid_spec=pltpu.PrefetchScalarGridSpec(
            num_scalar_prefetch=1,
            grid=(slot_count,),
            in_specs=[
                by_slot,
                pl.BlockSpec((1, phys_rows, cell_count), lambda s, t: (t[SLOT_TILE, s], 0, 0)),
            ],
            out_specs=by_slot,
            scratch_shapes=[pltpu.VMEM((5, levels, cell_count), jnp.float32)],
        ),
        compiler_params=pltpu.CompilerParams(vmem_limit_bytes=VMEM_LIMIT),
        name="inner",
    )(table, cells, phys)


def add_rims(
    levels, side, spans, tracers, part_at, phys_ref, rim_ref, rim_w_ref, rim_e_ref, coef_ref, moved_ref, ends_ref
):
    group = LANES // side
    halves = len(spans)
    rows = rim_w_ref.shape[1]
    rounds = rows // levels
    level_tiles = levels // SUB
    lane = lane_ids()
    col = lane & (side - 1)
    first_row = lane < side
    last_row = lane >= LANES - side
    odd = (lane & 1) == 1
    flag_row = 4 * levels

    def flag(f, h):
        return phys_ref[0, flag_row + f : flag_row + f + 1, spans[h]]

    above_mix = [jnp.zeros((SUB, LANES), jnp.float32)] * halves
    for lt in range(level_tiles):
        at = slice(lt * SUB, (lt + 1) * SUB)
        for h, faces in enumerate(block_faces(phys_ref, spans, levels, side, lt)):
            _, e, w, n, s = transport(faces, [flag(f, h) for f in range(4)])
            coef_ref[0, at, spans[h]] = jnp.where(col == 0, w, jnp.where(col == side - 1, e, 0.0))
            if h == 0:
                coef_ref[1, at, spans[h]] = jnp.where(first_row, s, 0.0)
            if h == halves - 1:
                coef_ref[1, at, spans[h]] = jnp.where(last_row, n, 0.0)
            mix = phys_ref[0, 3 * levels + lt * SUB : 3 * levels + (lt + 1) * SUB, spans[h]]
            set_mixing(coef_ref, at, spans[h], mix, above_mix[h], lt == level_tiles - 1)
            above_mix[h] = mix

    for at in range(0, rows, SUB):
        ends_ref[at : at + SUB, :] = turned(rim_w_ref[0, at : at + SUB, :], 2 - 2 * side)
    set_blank(moved_ref, len(tracers) * levels)

    def gather(lt, carry):
        at = pl.multiple_of(lt * SUB, SUB)
        for i in range(rounds):
            row = pl.multiple_of(i * levels + lt * SUB, SUB)
            rims = [
                rim_ref[0, pl.ds(row, SUB), :],
                rim_ref[0, pl.ds(pl.multiple_of(rows + row, SUB), SUB), :],
            ]
            ends_w = ends_ref[pl.ds(row, SUB), :]
            ends_e = rim_e_ref[0, pl.ds(row, SUB), :]
            sides = [jnp.where(odd, ends_e, ends_w), jnp.where(odd, ends_w, ends_e)]
            for g in range(group):
                if i * group + g not in tracers:
                    continue
                place = tracers.index(i * group + g)
                chan = pl.multiple_of(place * levels + lt * SUB, SUB)
                rim = turned(rims[2 * g // group], -side - 2 * side * (g % (group // 2)))
                for h in range(halves):
                    ends = turned(sides[h], side - 2 + h - 2 * g)
                    moved = part_at(place, lt, spans[h])
                    moved = moved + coef_ref[0, pl.ds(at, SUB), spans[h]] * ends
                    if h in (0, halves - 1):
                        moved = moved + coef_ref[1, pl.ds(at, SUB), spans[h]] * rim
                    moved_ref[pl.ds(pl.multiple_of(SUB + chan, SUB), SUB), spans[h]] = moved
        return carry

    lax.fori_loop(0, level_tiles, gather, 0, unroll=True)


def step_kernel(levels, side, last, table_ref, part_ref, phys_ref, rim_ref, rim_w_ref, rim_e_ref, *refs):
    if last:
        out_ref, coef_ref, moved_ref, ends_ref = refs
        edge_refs = ()
    else:
        out_ref, west_ref, east_ref, coef_ref, moved_ref, ends_ref = refs
        edge_refs = (west_ref, east_ref)
    channels, cell_count = part_ref.shape[1:]
    tracer_count = channels // levels
    group = LANES // side
    halves = cell_count // LANES
    rounds = tracer_count // group
    slot = pl.program_id(0)
    full = table_ref[SLOT_FULL, slot] == 1
    spans = [slice(h * LANES, (h + 1) * LANES) for h in range(halves)]

    @pl.when(jnp.logical_not(full))
    def _():
        out_ref[...] = jnp.zeros_like(out_ref)
        for ref in edge_refs:
            ref[...] = jnp.zeros_like(ref)

    @pl.when(full)
    def _():
        flag_row = 4 * levels

        def flag(f, h):
            return phys_ref[0, flag_row + f : flag_row + f + 1, spans[h]]

        def part_at(t, lt, span):
            return part_ref[0, pl.ds(pl.multiple_of(t * levels + lt * SUB, SUB), SUB), span]

        add_rims(
            levels,
            side,
            spans,
            list(range(tracer_count)),
            part_at,
            phys_ref,
            rim_ref,
            rim_w_ref,
            rim_e_ref,
            coef_ref,
            moved_ref,
            ends_ref,
        )

        def store(t, at, h, value):
            if t is not None:
                out_ref[0, pl.ds(at, SUB), spans[h]] = value
            elif not last:
                for i in range(rounds):
                    row = pl.multiple_of(i * levels + at * SUB, SUB)
                    first, second = (new[i * group : (i + 1) * group] for new in value)
                    west, east = pack_columns(first, second, side)
                    west_ref[0, pl.ds(row, SUB), :] = west
                    east_ref[0, pl.ds(row, SUB), :] = east

        def warm_at(lt, h):
            return phys_ref[0, pl.ds(pl.multiple_of(2 * levels + lt * SUB, SUB), SUB), spans[h]]

        light = [flag(LIGHT, h) for h in range(halves)]
        wet = [flag(WET, h) for h in range(halves)]
        mix_and_react(levels, tracer_count, spans, moved_ref, coef_ref, light, wet, warm_at, store)


def step(table, cells, phys, rims, rim_w, rim_e, levels, side, last):
    slot_count, channels, cell_count = cells.shape
    lon_count = lax.axis_size("lon")
    rows = channels * side // LANES
    phys_rows = phys.shape[1]
    f32 = jnp.float32
    by_slot = pl.BlockSpec((1, channels, cell_count), lambda s, t: (s, 0, 0))
    shapes = [jax.ShapeDtypeStruct(cells.shape, f32)]
    specs = [by_slot]
    if not last:
        beside = jax.ShapeDtypeStruct((slot_count, rows, LANES), f32)
        shapes += [beside, beside]
        specs += [pl.BlockSpec((1, rows, LANES), lambda s, t: (s, 0, 0))] * 2
    return pl.pallas_call(
        functools.partial(step_kernel, levels, side, last),
        out_shape=shapes,
        grid_spec=pltpu.PrefetchScalarGridSpec(
            num_scalar_prefetch=1,
            grid=(slot_count,),
            in_specs=[
                by_slot,
                pl.BlockSpec((1, phys_rows, cell_count), lambda s, t: (t[SLOT_TILE, s], 0, 0)),
                pl.BlockSpec((1, 2 * rows, LANES), lambda s, t: (t[SLOT_TILE, s], 0, 0)),
                pl.BlockSpec((1, rows, LANES), lambda s, t: (t[SLOT_WEST, s], 0, 0)),
                pl.BlockSpec((1, rows, LANES), lambda s, t: (t[SLOT_EAST, s], 0, 0)),
            ],
            out_specs=specs,
            scratch_shapes=[
                pltpu.VMEM((8, levels, cell_count), f32),
                pltpu.VMEM((channels + 2 * SUB, cell_count), f32),
                pltpu.VMEM((rows, LANES), f32),
            ],
        ),
        compiler_params=pltpu.CompilerParams(vmem_limit_bytes=VMEM_LIMIT),
        name="step",
    )(table, cells, phys, rims, rim_w, rim_e)


def chl_kernel(levels, side, table_ref, *refs):
    count = len(CHL_TRACERS)
    part_refs = refs[: len(CHL_BLOCKS)]
    phys_ref, rim_ref, rim_w_ref, rim_e_ref, chl_ref, coef_ref, moved_ref, ends_ref = refs[len(CHL_BLOCKS) :]
    halves = chl_ref.shape[2] // LANES
    spans = [slice(h * LANES, (h + 1) * LANES) for h in range(halves)]
    full = table_ref[SLOT_FULL, pl.program_id(0)] == 1
    flag_row = 4 * levels

    @pl.when(jnp.logical_not(full))
    def _():
        chl_ref[...] = jnp.zeros_like(chl_ref)

    @pl.when(full)
    def _():
        def part_at(place, lt, span):
            tracer = CHL_TRACERS[place]
            at = (tracer % CHL_RUN) * levels + lt * SUB
            return part_refs[CHL_BLOCKS.index(tracer // CHL_RUN)][0, pl.ds(pl.multiple_of(at, SUB), SUB), span]

        add_rims(
            levels,
            side,
            spans,
            list(CHL_TRACERS),
            part_at,
            phys_ref,
            rim_ref,
            rim_w_ref,
            rim_e_ref,
            coef_ref,
            moved_ref,
            ends_ref,
        )
        nano = CHL_TRACERS.index(nano_chl_index)
        diat = CHL_TRACERS.index(diat_chl_index)

        def greening(lt, carry):
            at = pl.multiple_of(lt * SUB, SUB)
            depths = []
            for h, span in enumerate(spans):
                mixed = mixed_at(levels, count, span, moved_ref, coef_ref, lt)
                light = phys_ref[0, flag_row + LIGHT : flag_row + LIGHT + 1, span]
                wet = phys_ref[0, flag_row + WET : flag_row + WET + 1, span]
                warm = phys_ref[0, pl.ds(pl.multiple_of(2 * levels + lt * SUB, SUB), SUB), span]
                par_light, depth = lit_at(mixed[nano], mixed[diat], light, carry[h])
                depths.append(depth)
                nano_chl, diat_chl = chl_after(mixed, par_light, warm)
                chl_ref[0, pl.ds(at, SUB), span] = positive(nano_chl * wet) + positive(diat_chl * wet)
            return tuple(depths)

        start = tuple(jnp.zeros((1, LANES), jnp.float32) for _ in spans)
        lax.fori_loop(0, levels // SUB, greening, start, unroll=True)


def last_chl(table, cells, phys, rims, rim_w, rim_e, levels, side):
    slot_count, channels, cell_count = cells.shape
    lon_count = lax.axis_size("lon")
    rows = channels * side // LANES
    count = len(CHL_TRACERS)
    f32 = jnp.float32

    def level_block(number):
        return pl.BlockSpec((1, CHL_RUN * levels, cell_count), lambda s, t: (s, number, 0))

    return pl.pallas_call(
        functools.partial(chl_kernel, levels, side),
        out_shape=jax.ShapeDtypeStruct((lon_count, levels, cell_count), f32),
        grid_spec=pltpu.PrefetchScalarGridSpec(
            num_scalar_prefetch=1,
            grid=(slot_count,),
            in_specs=[level_block(n) for n in CHL_BLOCKS]
            + [
                pl.BlockSpec((1, phys.shape[1], cell_count), lambda s, t: (t[SLOT_TILE, s], 0, 0)),
                pl.BlockSpec((1, 2 * rows, LANES), lambda s, t: (t[SLOT_TILE, s], 0, 0)),
                pl.BlockSpec((1, rows, LANES), lambda s, t: (t[SLOT_WEST, s], 0, 0)),
                pl.BlockSpec((1, rows, LANES), lambda s, t: (t[SLOT_EAST, s], 0, 0)),
            ],
            out_specs=pl.BlockSpec((1, levels, cell_count), lambda s, t: (t[SLOT_TILE, s], 0, 0)),
            scratch_shapes=[
                pltpu.VMEM((8, levels, cell_count), f32),
                pltpu.VMEM((count * levels + 2 * SUB, cell_count), f32),
                pltpu.VMEM((rows, LANES), f32),
            ],
        ),
        compiler_params=pltpu.CompilerParams(vmem_limit_bytes=VMEM_LIMIT),
        name="last_chl",
    )(table, *([cells] * len(CHL_BLOCKS)), phys, rims, rim_w, rim_e)


def rows_kernel(levels, factor, fine_ref, mix_ref, pick_ref, rows_ref):
    f32 = jnp.float32
    picks = pick_ref[...]
    east_face = jnp.zeros((levels, LANES), f32)
    temp_mean = jnp.zeros((levels, LANES), f32)
    for r in range(factor):
        got = jnp.dot(fine_ref[r], picks, preferred_element_type=f32)
        east_face += got[0:levels, 0:LANES]
        temp_mean += got[2 * levels : 3 * levels, LANES : 2 * LANES]
        if r == factor - 1:
            north_face = got[levels : 2 * levels, LANES : 2 * LANES]
    rows_ref[0, 0:levels, :] = east_face * (1.0 / factor)
    rows_ref[0, levels : 2 * levels, :] = north_face * (1.0 / factor)
    rows_ref[0, 2 * levels : 3 * levels, :] = jnp.exp(0.0639 * (temp_mean * (1.0 / (factor * factor))))
    rows_ref[0, 3 * levels : 4 * levels, :] = mix_ref[0].astype(f32)


def coarse_rows(fine, mix, picks):
    side, levels, tile_cols = mix.shape
    factor = fine.shape[0] // side
    fine_cols = fine.shape[2]
    return pl.pallas_call(
        functools.partial(rows_kernel, levels, factor),
        out_shape=jax.ShapeDtypeStruct((side, 4 * levels, tile_cols), jnp.float32),
        grid=(side,),
        in_specs=[
            pl.BlockSpec((factor, 3 * levels, fine_cols), lambda i: (i, 0, 0)),
            pl.BlockSpec((1, levels, tile_cols), lambda i: (i, 0, 0)),
            pl.BlockSpec(picks.shape, lambda i: (0, 0)),
        ],
        out_specs=pl.BlockSpec((1, 4 * levels, tile_cols), lambda i: (i, 0, 0)),
        compiler_params=pltpu.CompilerParams(vmem_limit_bytes=VMEM_LIMIT),
        name="coarse_rows",
    )(fine, mix, picks)


def place_kernel(
    levels,
    side,
    factor,
    table_ref,
    rows_ref,
    light_ref,
    land_ref,
    south_ref,
    north_ref,
    west_ref,
    east_ref,
    pick_ref,
    out_ref,
    line_ref,
    flags_ref,
):
    tile_blocks = land_ref.shape[1] // side
    halves = side * side // LANES
    group = LANES // side
    fine_cols = light_ref.shape[1]
    f32 = jnp.float32
    picks = pick_ref[...]
    lane = lane_ids()
    group_id = lane >> (side.bit_length() - 1)
    col_id = lane & (side - 1)
    flag_row = 4 * levels
    pack_at = flag_row + SUB
    wet = land_ref[...].astype(f32)
    sides = wet.shape
    lane2 = lax.broadcasted_iota(jnp.int32, sides, 1)
    sub2 = lax.broadcasted_iota(jnp.int32, sides, 0)
    diagonal = lane2 == sub2
    rim_w = jnp.sum(jnp.where(diagonal, west_ref[SUB : SUB + 1, :], 0.0), axis=1, keepdims=True)
    rim_e = jnp.sum(jnp.where(diagonal, east_ref[0:1, :], 0.0), axis=1, keepdims=True)
    wet_w = jnp.where(lane2 == 0, rim_w, pltpu.roll(wet, 1, 1))
    wet_e = jnp.where(lane2 == LANES - 1, rim_e, pltpu.roll(wet, LANES - 1, 1))
    wet_s = jnp.where(sub2 == 0, south_ref[levels : levels + 1, 0:LANES], pltpu.roll(wet, 1, 0))
    wet_n = jnp.where(sub2 == side - 1, north_ref[0:1, 0:LANES], pltpu.roll(wet, side - 1, 0))
    fold_r = lax.broadcasted_iota(jnp.int32, (side, side * factor), 0)
    fold_c = lax.broadcasted_iota(jnp.int32, (side, side * factor), 1)
    fold_d = fold_c - factor * fold_r
    fold = jnp.where((fold_d >= 0) & (fold_d < factor), 1.0, 0.0)
    narrow = picks[:, LANES : 2 * LANES].astype(f32)
    light_rows = jnp.dot(fold, light_ref[...], precision=lax.Precision.HIGHEST, preferred_element_type=f32)
    light_mean = jnp.dot(
        light_rows, narrow, precision=lax.Precision.HIGHEST, preferred_element_type=f32
    ) * (1.0 / (factor * factor))
    flags = [wet * wet_e, wet * wet_n, wet * wet_w, wet * wet_s, light_mean, wet]
    for r in range(side):
        for f, value in enumerate(flags):
            flags_ref[r, f : f + 1, :] = value[r : r + 1, :]
        flags_ref[r, len(flags) : SUB, :] = jnp.zeros((SUB - len(flags), LANES), f32)

    def place(ref, frm, to):
        for h in range(halves):
            values = [ref[h * group + r, pl.ds(frm, SUB), :] for r in range(group)]
            for b, block in enumerate(regroup(values, side)):
                owner = table_ref[TILE_OWNER, b]
                out_ref[owner, pl.ds(to, SUB), h * LANES : (h + 1) * LANES] = block

    def place_four(q, carry):
        for n in range(4):
            at = pl.multiple_of(n * levels + q * SUB, SUB)
            place(rows_ref, at, at)
        return carry

    lax.fori_loop(0, levels // SUB, place_four, 0)
    place(flags_ref, 0, flag_row)

    fine_v = south_ref[0:levels, 0:fine_cols].astype(jnp.bfloat16)
    north_below = jnp.dot(fine_v, picks, preferred_element_type=f32)[:, LANES : 2 * LANES] * (1.0 / factor)
    for h, r in enumerate((0, side - 1)):
        span = slice(h * LANES, (h + 1) * LANES)
        line_ref[0 : 4 * levels, span] = rows_ref[r, 0 : 4 * levels, :]
        line_ref[6 * levels : 6 * levels + SUB, span] = flags_ref[r]
        line_ref[5 * levels : 6 * levels, span] = (
            north_below if h == 0 else rows_ref[r - 1, levels : 2 * levels, :]
        )
        from_lane = side * (r % group) + group * (r // group)
        for lt in range(levels // SUB):
            face = rows_ref[r, lt * SUB : (lt + 1) * SUB, :]
            line_ref[4 * levels + lt * SUB : 4 * levels + (lt + 1) * SUB, span] = jnp.where(
                lane == 0, turned(west_ref[0:SUB, :], -(from_lane + lt)), turned(face, 1)
            )
    for b in range(tile_blocks):
        owner = table_ref[TILE_OWNER, b]
        south_pack = jnp.zeros((SUB, LANES), f32)
        for lt in range(levels // SUB):
            piece = turned(north_below[lt * SUB : (lt + 1) * SUB, :], side * (lt - b))
            south_pack = jnp.where(group_id == lt, piece, south_pack)
        if b == 0:
            west_pack = west_ref[0:SUB, :]
        else:
            beside = table_ref[TILE_OWNER, b - 1]
            west_pack = jnp.zeros((SUB, LANES), f32)
            for h in range(halves):
                for lt in range(levels // SUB):
                    face = out_ref[beside, lt * SUB : (lt + 1) * SUB, h * LANES : (h + 1) * LANES]
                    piece = turned(face, h * group + lt - (side - 1))
                    west_pack = jnp.where(col_id == h * group + lt, piece, west_pack)
        out_ref[owner, pack_at : pack_at + SUB, 0:LANES] = west_pack
        out_ref[owner, pack_at : pack_at + SUB, LANES : 2 * LANES] = south_pack


def coarsen(table, rows, light, land, from_south, from_north, from_west, from_east, picks):
    lon_count = lax.axis_size("lon")
    side, tile_cols = land.shape
    levels = rows.shape[1] // 4
    factor = light.shape[0] // side
    phys_rows = 4 * levels + 2 * SUB
    f32 = jnp.float32
    vmem = pl.BlockSpec(memory_space=pltpu.VMEM)
    return pl.pallas_call(
        functools.partial(place_kernel, levels, side, factor),
        out_shape=[
            jax.ShapeDtypeStruct((lon_count, phys_rows, side * side), f32),
            jax.ShapeDtypeStruct((6 * levels + SUB, 2 * LANES), f32),
        ],
        in_specs=[pl.BlockSpec(memory_space=pltpu.SMEM)] + [vmem] * 8,
        out_specs=[vmem, vmem],
        scratch_shapes=[pltpu.VMEM((side, SUB, LANES), f32)],
        compiler_params=pltpu.CompilerParams(vmem_limit_bytes=VMEM_LIMIT),
        name="coarsen",
    )(table, rows, light, land, from_south, from_north, from_west, from_east, picks)


def lines_kernel(levels, side, table_ref, quad_ref, low_ref, high_ref, low_in_ref, high_in_ref, ends_ref):
    tile_blocks = LANES // side
    pairs = quad_ref.shape[1] // levels
    lane = lane_ids()
    spot = lane >> 1

    def body(lt, carry):
        packed = jnp.zeros((SUB, LANES), jnp.float32)
        for m in range(pairs):
            at = pl.multiple_of(m * levels + lt * SUB, SUB)
            blocks = []
            for b in range(tile_blocks):
                value = quad_ref[table_ref[TILE_OWNER, b], pl.ds(at, SUB), :]
                blocks.append(jnp.where(table_ref[TILE_WET, b] == 1, value, 0.0))
            parts = regroup(blocks, side)
            for p in range(2):
                t = 2 * m + p
                chan = pl.ds(pl.multiple_of(t * levels + lt * SUB, SUB), SUB)
                high_in, high, low, low_in = parts[4 * p : 4 * p + 4]
                low_ref[chan, :] = low
                high_ref[chan, :] = high
                low_in_ref[chan, :] = low_in
                high_in_ref[chan, :] = high_in
                for k, line in ((2 * t, low), (2 * t + 1, high)):
                    packed = jnp.where(spot == k, turned(line, 1 + 2 * k), packed)
        ends_ref[pl.ds(pl.multiple_of(lt * SUB, SUB), SUB), :] = packed
        return carry

    lax.fori_loop(0, levels // SUB, body, 0)


def tile_lines(table, quads, levels, side):
    channels = quads.shape[1] // levels * 2 * levels
    vmem = pl.BlockSpec(memory_space=pltpu.VMEM)
    line = jax.ShapeDtypeStruct((channels, LANES), jnp.float32)
    return pl.pallas_call(
        functools.partial(lines_kernel, levels, side),
        out_shape=[line] * 4 + [jax.ShapeDtypeStruct((levels, LANES), jnp.float32)],
        in_specs=[pl.BlockSpec(memory_space=pltpu.SMEM), vmem],
        out_specs=[vmem] * 5,
        compiler_params=pltpu.CompilerParams(vmem_limit_bytes=VMEM_LIMIT),
        name="tile_lines",
    )(table, quads)


def line_kernel(
    levels,
    low_ref,
    high_ref,
    low_in_ref,
    high_in_ref,
    below_ref,
    above_ref,
    west_ref,
    east_ref,
    phys_ref,
    low_out_ref,
    high_out_ref,
    coef_ref,
    moved_ref,
    ends_ref,
):
    channels = low_ref.shape[0]
    tracer_count = channels // levels
    level_tiles = levels // SUB
    lane = lane_ids()
    odd = (lane & 1) == 1
    spans = [slice(0, LANES), slice(LANES, 2 * LANES)]
    flag_row = 6 * levels
    lines = (
        (low_ref, low_in_ref, below_ref, low_out_ref),
        (high_ref, above_ref, high_in_ref, high_out_ref),
    )

    def flag(f, h):
        return phys_ref[flag_row + f : flag_row + f + 1, spans[h]]

    above_mix = [jnp.zeros((SUB, LANES), jnp.float32)] * 2
    for lt in range(level_tiles):
        at = slice(lt * SUB, (lt + 1) * SUB)
        from_west = west_ref[lt * SUB : (lt + 1) * SUB, :]
        from_east = east_ref[lt * SUB : (lt + 1) * SUB, :]
        ends_ref[at, :] = jnp.where(odd, turned(from_east, -2), from_west)
        for h in range(2):
            faces = [
                phys_ref[n * levels + lt * SUB : n * levels + (lt + 1) * SUB, spans[h]] for n in (0, 1, 4, 5)
            ]
            for n, value in enumerate(transport(faces, [flag(f, h) for f in range(4)])):
                coef_ref[n, at, spans[h]] = value
            mix = phys_ref[3 * levels + lt * SUB : 3 * levels + (lt + 1) * SUB, spans[h]]
            set_mixing(coef_ref, at, spans[h], mix, above_mix[h], lt == level_tiles - 1)
            above_mix[h] = mix
    set_blank(moved_ref, channels)

    def advect(lt, carry):
        at = pl.multiple_of(lt * SUB, SUB)
        ends = ends_ref[pl.ds(at, SUB), :]
        for h in range(2):
            here_ref, north_ref, south_ref, _ = lines[h]
            c, e, w, n, s = (coef_ref[k, pl.ds(at, SUB), spans[h]] for k in range(5))
            for t in range(tracer_count):
                chan = pl.multiple_of(t * levels + lt * SUB, SUB)
                here = here_ref[pl.ds(chan, SUB), :]
                end = turned(ends, -2 * (2 * t + h))
                west = jnp.where(lane == 0, end, turned(here, 1))
                east = jnp.where(lane == LANES - 1, end, turned(here, -1))
                moved_ref[pl.ds(pl.multiple_of(SUB + chan, SUB), SUB), spans[h]] = (
                    c * here
                    + (e * east + w * west)
                    + (n * north_ref[pl.ds(chan, SUB), :] + s * south_ref[pl.ds(chan, SUB), :])
                )
        return carry

    lax.fori_loop(0, level_tiles, advect, 0, unroll=True)

    def store(t, at, h, value):
        if t is not None:
            lines[h][3][pl.ds(at, SUB), :] = value

    def warm_at(lt, h):
        return phys_ref[pl.ds(pl.multiple_of(2 * levels + lt * SUB, SUB), SUB), spans[h]]

    light = [flag(LIGHT, h) for h in range(2)]
    wet = [flag(WET, h) for h in range(2)]
    mix_and_react(levels, tracer_count, spans, moved_ref, coef_ref, light, wet, warm_at, store)


def line_step(low, high, low_in, high_in, below, above, from_west, from_east, phys, levels):
    channels = low.shape[0]
    vmem = pl.BlockSpec(memory_space=pltpu.VMEM)
    f32 = jnp.float32
    line = jax.ShapeDtypeStruct((channels, LANES), f32)
    return pl.pallas_call(
        functools.partial(line_kernel, levels),
        out_shape=[line, line],
        in_specs=[vmem] * 9,
        out_specs=[vmem, vmem],
        scratch_shapes=[
            pltpu.VMEM((8, levels, 2 * LANES), f32),
            pltpu.VMEM((channels + 2 * SUB, 2 * LANES), f32),
            pltpu.VMEM((levels, LANES), f32),
        ],
        compiler_params=pltpu.CompilerParams(vmem_limit_bytes=VMEM_LIMIT),
        name="line_step",
    )(low, high, low_in, high_in, below, above, from_west, from_east, phys)


def hand_kernel(levels, side, table_ref, below_ref, above_ref, *refs):
    out_ref = refs[-1]
    group = LANES // side
    rounds = below_ref.shape[0] // levels // group
    half = group // 2

    def body(lt, carry):
        for i in range(rounds):
            for part in range(2):
                lines = []
                for g in range(half):
                    t = i * group + part * half + g
                    chan = pl.ds(pl.multiple_of(t * levels + lt * SUB, SUB), SUB)
                    lines += [above_ref[chan, :], below_ref[chan, :]]
                row = pl.multiple_of((part * rounds + i) * levels + lt * SUB, SUB)
                for b, value in enumerate(regroup(lines, side)):
                    out_ref[table_ref[TILE_OWNER, b], pl.ds(row, SUB), :] = value
        return carry

    lax.fori_loop(0, levels // SUB, body, 0)


def hand_on(table, below, above, levels, side, *after):
    lon_count = lax.axis_size("lon")
    rows = 2 * below.shape[0] * side // LANES
    vmem = pl.BlockSpec(memory_space=pltpu.VMEM)
    return pl.pallas_call(
        functools.partial(hand_kernel, levels, side),
        out_shape=jax.ShapeDtypeStruct((lon_count, rows, LANES), jnp.float32),
        in_specs=[pl.BlockSpec(memory_space=pltpu.SMEM), vmem, vmem]
        + [pl.BlockSpec(memory_space=pl.ANY)] * len(after),
        out_specs=vmem,
        compiler_params=pltpu.CompilerParams(vmem_limit_bytes=VMEM_LIMIT),
        name="hand_on",
    )(table, below, above, *after)


def gate_kernel(*refs):
    pass


def gate(values, *others):
    anywhere = pl.BlockSpec(memory_space=pl.ANY)
    count = len(values)
    return pl.pallas_call(
        gate_kernel,
        out_shape=[jax.ShapeDtypeStruct(x.shape, x.dtype) for x in values],
        in_specs=[anywhere] * (count + len(others)),
        out_specs=[anywhere] * count,
        input_output_aliases={i: i for i in range(count)},
        name="gate",
    )(*values, *others)


def heat_kernel(
    levels,
    side,
    factor,
    table_ref,
    chl_ref,
    light_ref,
    land_ref,
    widen_ref,
    after_ref,
    out_ref,
    rows_ref,
    wide_ref,
):
    tile_blocks = land_ref.shape[1] // side
    halves = side * side // LANES
    group = LANES // side
    fine_cols = light_ref.shape[1]
    fine_rows = light_ref.shape[0]
    f32 = jnp.float32
    group_id = lane_ids() >> (side.bit_length() - 1)

    def place(lt, carry):
        at = pl.multiple_of(lt * SUB, SUB)
        for h in range(halves):
            blocks = []
            for b in range(tile_blocks):
                owner = table_ref[TILE_OWNER, b]
                values = chl_ref[owner, pl.ds(at, SUB), h * LANES : (h + 1) * LANES]
                blocks.append(jnp.where(table_ref[TILE_WET, b] == 1, values, 0.0))
            for r in range(group):
                line = None
                for b in range(tile_blocks):
                    piece = turned(blocks[b], side * (b - r))
                    line = piece if line is None else jnp.where(group_id == b, piece, line)
                rows_ref[pl.ds(pl.multiple_of((h * group + r) * levels + lt * SUB, SUB), SUB), :] = line
        return carry

    lax.fori_loop(0, levels // SUB, place, 0, unroll=True)
    wet = land_ref[...].astype(f32)
    widen = widen_ref[...]
    above = jnp.zeros_like(wet)
    passing = jnp.ones_like(wet)
    for l in range(levels):
        chl = rows_ref[pl.ds(l, side, stride=levels), :]
        above = above + (0.04 + 0.02 * chl)
        through = jnp.exp(-above)
        kept = (passing - through) * wet
        passing = through
        high = kept.astype(jnp.bfloat16)
        low = (kept - high.astype(f32)).astype(jnp.bfloat16)
        wide_ref[l * side : (l + 1) * side, :] = jnp.dot(
            high, widen, preferred_element_type=f32
        ) + jnp.dot(low, widen, preferred_element_type=f32)

    sub = lax.broadcasted_iota(jnp.int32, (SUB, LANES), 0)
    sources = []
    for m in range(fine_rows // SUB):
        start = (m * SUB // factor) // SUB * SUB
        index = jnp.zeros_like(sub)
        for r in range(1, side):
            index = index + jnp.where(sub + m * SUB >= r * factor, 1, 0)
        sources.append((start, index - start))

    def spread(l, carry):
        for c in range(fine_cols // LANES):
            span = slice(c * LANES, (c + 1) * LANES)
            for m in range(0, fine_rows // SUB, 2):
                both = []
                for n in (m, m + 1):
                    start, index = sources[n]
                    lines = wide_ref[pl.ds(pl.multiple_of(l * side + start, SUB), SUB), span]
                    lines = jnp.take_along_axis(lines, index, axis=0)
                    both.append(lines * light_ref[n * SUB : (n + 1) * SUB, span])
                out_ref[l, m * SUB : (m + 2) * SUB, span] = jnp.concatenate(both, axis=0).astype(jnp.bfloat16)
        return carry

    lax.fori_loop(0, levels, spread, 0, unroll=4)


def heat(table, chl, light, land, levels, widen, after):
    side = land.shape[0]
    factor = light.shape[0] // side
    vmem = pl.BlockSpec(memory_space=pltpu.VMEM)
    return pl.pallas_call(
        functools.partial(heat_kernel, levels, side, factor),
        out_shape=jax.ShapeDtypeStruct((levels,) + light.shape, jnp.bfloat16),
        in_specs=[pl.BlockSpec(memory_space=pltpu.SMEM), vmem, vmem, vmem, vmem]
        + [pl.BlockSpec(memory_space=pl.ANY)],
        out_specs=vmem,
        scratch_shapes=[
            pltpu.VMEM(((side + 1) * levels, LANES), jnp.float32),
            pltpu.VMEM((side * levels, light.shape[1]), jnp.float32),
        ],
        compiler_params=pltpu.CompilerParams(vmem_limit_bytes=VMEM_LIMIT),
        name="heat",
    )(table, chl, light, land, widen, after)


def widened(x, rows, width):
    return jnp.pad(x, ((0, rows - x.shape[0]), (0, width - x.shape[1])))


def on_device(tracers, phys_fine, mix_coarse, surf_light, land_mask, owner_map):
    f32 = jnp.float32
    slot_count = tracers.shape[0]
    side = land_mask.shape[0]
    levels = mix_coarse.shape[2]
    tile_blocks = land_mask.shape[1] // side
    factor = phys_fine.shape[0] // side
    fine_cols = phys_fine.shape[1]
    group = LANES // side

    fine = jnp.transpose(phys_fine, (0, 2, 1))
    mix = jnp.transpose(mix_coarse, (0, 2, 1))
    wet = land_mask.astype(f32)
    width = fine_cols

    northward = jnp.concatenate(
        [
            widened(fine[-1, levels : 2 * levels, :].astype(f32), levels, width),
            widened(wet[-1:], 1, width),
        ],
        axis=0,
    )
    southward = widened(wet[:1], 1, width)
    last_face = jnp.mean(
        fine[:, :levels, fine_cols - 1].astype(f32).reshape(side, factor, levels), axis=1
    )
    face_pack = jnp.pad(
        last_face.reshape(side // group, group, levels // SUB, SUB).transpose(3, 1, 0, 2),
        ((0, 0), (0, 0), (0, 0), (0, group - levels // SUB)),
    ).reshape(SUB, LANES)
    eastward = jnp.concatenate([face_pack, widened(wet[:, -1][None], 1, LANES)], axis=0)
    westward = widened(wet[:, 0][None], 1, LANES)

    from_south = lax.ppermute(northward, "lat", along("lat", 1, False))
    from_north = lax.ppermute(southward, "lat", along("lat", -1, False))
    from_west = lax.ppermute(eastward, "lon", along("lon", 1, True))
    from_east = lax.ppermute(westward, "lon", along("lon", -1, True))

    fine_id = jnp.arange(fine_cols)[:, None]
    coarse_id = jnp.arange(land_mask.shape[1])[None, :]
    member = (fine_id // factor == coarse_id).astype(jnp.bfloat16)
    final = (fine_id == factor * coarse_id + factor - 1).astype(jnp.bfloat16)
    picks = jnp.concatenate([final, member], axis=1)

    table = routing(owner_map, slot_count, tile_blocks)
    def to_north(x):
        return lax.ppermute(x, "lat", along("lat", 1, False))

    def to_south(x):
        return lax.ppermute(x, "lat", along("lat", -1, False))

    def to_east(x):
        return lax.ppermute(x, "lon", along("lon", 1, True))

    def to_west(x):
        return lax.ppermute(x, "lon", along("lon", -1, True))

    def across(x):
        return lax.all_to_all(x, "lon", 0, 0, tiled=True)

    quads, west, east = first_edges(table, tracers, levels, side)
    quads = across(quads)
    rows = coarse_rows(fine, mix, picks)
    phys, line_phys = coarsen(
        table, rows, surf_light, land_mask, from_south, from_north, from_west, from_east, picks
    )
    phys = across(phys)
    low, high, low_in, high_in, ends = tile_lines(table, quads, levels, side)
    below, above = to_north(high), to_south(low)
    west, east = gate((west, east), phys)
    rim_w, rim_e = to_east(east), to_west(west)
    ends_w, ends_e = to_east(ends), to_west(ends)
    rims = across(hand_on(table, below, above, levels, side, phys, ends_w, ends_e))
    new_low, new_high = line_step(
        low, high, low_in, high_in, below, above, ends_w, ends_e, line_phys, levels
    )
    below, above = to_north(new_high), to_south(new_low)
    partial = inner(table, tracers, phys, levels, side)
    (handed,) = gate((hand_on(table, below, above, levels, side),), rims, rim_w, rim_e, partial)
    new_rims = across(handed)
    current, west, east = step(table, partial, phys, rims, rim_w, rim_e, levels, side, False)
    rim_w, rim_e = to_east(east), to_west(west)
    partial = inner(table, current, phys, levels, side)
    chl = across(last_chl(table, partial, phys, new_rims, rim_w, rim_e, levels, side))
    (current,) = step(table, partial, phys, new_rims, rim_w, rim_e, levels, side, True)
    heating = heat(table, chl, surf_light, land_mask, levels, jnp.transpose(member), current)
    return current, heating


def solution(mesh):
    in_specs = (
        P(("lat", "lon"), None, None),
        P("lat", "lon", None),
        P("lat", "lon", None),
        P("lat", "lon"),
        P("lat", "lon"),
        P("lat", None),
    )
    out_specs = (P(("lat", "lon"), None, None), P(None, "lat", "lon"))
    return jax.shard_map(
        on_device, mesh=mesh, in_specs=in_specs, out_specs=out_specs, check_vma=False
    )
```

```python
import functools

import jax
import jax.numpy as jnp
from jax import lax
from jax.experimental import pallas as pl
from jax.experimental.pallas import tpu as pltpu
from jax.sharding import PartitionSpec as P

LANES = 128
SUB = 8

diffuse_rate = 0.08
nano_chl_index = 10
diat_chl_index = 11

SLOT_TILE, SLOT_FULL, SLOT_WEST, SLOT_EAST, TILE_OWNER, TILE_WET, TILE_BASE = range(7)
TABLE_ROWS = 8

OPEN_EAST, OPEN_NORTH, OPEN_WEST, OPEN_SOUTH, LIGHT, WET = range(6)

VMEM_LIMIT = 48 * 1024 * 1024


def positive(value):
    return jnp.maximum(value, 0.0)


def lane_ids(rows=SUB):
    return lax.broadcasted_iota(jnp.int32, (rows, LANES), 1)


def turned(value, by):
    by = by % LANES
    return value if by == 0 else pltpu.roll(value, by, 1)


def quotient(value, by):
    if by & (by - 1) == 0:
        return lax.shift_right_logical(value, jnp.int32(by.bit_length() - 1))
    return lax.div(value, jnp.int32(by))


def remainder(value, by):
    if by & (by - 1) == 0:
        return value & (by - 1)
    return lax.rem(value, jnp.int32(by))


def along(axis, by, closed):
    size = lax.axis_size(axis)
    pairs = [(i, (i + by) % size) for i in range(size)]
    return [p for p in pairs if closed or p[1] == p[0] + by]


def table_kernel(slot_count, tile_blocks, lon_count, row_ref, out_ref, used_ref):
    me = lax.axis_index("lon")
    block_count = row_ref.shape[1]
    width = out_ref.shape[1]

    def clear(i, carry):
        for r in range(TABLE_ROWS):
            out_ref[r, i] = 0
        return carry

    lax.fori_loop(0, width, clear, 0)

    def unuse(i, carry):
        used_ref[0, i] = 0
        used_ref[1, i] = 0
        return carry

    lax.fori_loop(0, lon_count, unuse, 0)
    out_ref[TILE_BASE, 0] = me * tile_blocks

    def visit(k, carry):
        code = row_ref[0, k]
        safe = jnp.maximum(code, 0)
        owner = remainder(quotient(safe, slot_count), lon_count)
        slot = remainder(safe, slot_count)
        tile = quotient(k, tile_blocks)

        @pl.when((code >= 0) & (owner == me))
        def _():
            west = row_ref[0, remainder(k + block_count - 1, block_count)]
            east = row_ref[0, remainder(k + 1, block_count)]
            out_ref[SLOT_TILE, slot] = tile
            out_ref[SLOT_FULL, slot] = 1
            out_ref[SLOT_WEST, slot] = remainder(jnp.maximum(west, 0), slot_count)
            out_ref[SLOT_EAST, slot] = remainder(jnp.maximum(east, 0), slot_count)
            used_ref[0, tile] = 1

        @pl.when((code >= 0) & (tile == me))
        def _():
            local = remainder(k, tile_blocks)
            out_ref[TILE_OWNER, local] = owner
            out_ref[TILE_WET, local] = 1
            used_ref[1, owner] = 1

        return carry

    lax.fori_loop(0, block_count, visit, 0, unroll=8)

    def give(target, filled, line, count):
        def one(i, carry):
            def look(j, done):
                take = (done == 0) & (used_ref[line, j] == 0)

                @pl.when(take)
                def _():
                    out_ref[target, i] = j
                    used_ref[line, j] = 1

                return jnp.where(take, 1, done)

            @pl.when(out_ref[filled, i] == 0)
            def _():
                lax.fori_loop(0, lon_count, look, 0)

            return carry

        lax.fori_loop(0, count, one, 0)

    give(SLOT_TILE, SLOT_FULL, 0, slot_count)
    give(TILE_OWNER, TILE_WET, 1, tile_blocks)


def routing(row, slot_count, tile_blocks):
    lon_count = lax.axis_size("lon")
    width = max(slot_count, tile_blocks, lon_count)
    return pl.pallas_call(
        functools.partial(table_kernel, slot_count, tile_blocks, lon_count),
        out_shape=jax.ShapeDtypeStruct((TABLE_ROWS, width), jnp.int32),
        in_specs=[pl.BlockSpec(memory_space=pltpu.SMEM)],
        out_specs=pl.BlockSpec(memory_space=pltpu.SMEM),
        scratch_shapes=[pltpu.SMEM((2, lon_count), jnp.int32)],
        name="routing",
    )(row)


def merged(pieces, ids):
    packed = pieces[0]
    for g in range(1, len(pieces)):
        packed = jnp.where(ids == g, pieces[g], packed)
    return packed


def pack_columns(first, second, side):
    lane = lane_ids()
    odd = (lane & 1) == 1
    here = (lane & (side - 1)) >> 1
    there = ((lane + 1) & (side - 1)) >> 1
    even_ends = merged([turned(v, 1 + 2 * g) for g, v in enumerate(first)], here)
    odd_ends = merged([turned(v, 2 * g) for g, v in enumerate(second)], there)
    return jnp.where(odd, even_ends, odd_ends), jnp.where(odd, odd_ends, even_ends)


def pack_quads(first, second, side):
    low = lane_ids() < LANES // 2
    both = [jnp.where(low, a, b) for a, b in zip(first, second)]
    turns = [turned(v, 2 * side + (g % 2) * (LANES // 2)) for g, v in enumerate(both)]
    return [jnp.where(low, turns[g], turns[g + 1]) for g in range(0, len(turns), 2)]


def regroup(values, side):
    values = list(values)
    ids = lane_ids() >> (side.bit_length() - 1)
    bit = 1
    while bit < len(values):
        keep = (ids & bit) == 0
        for n in range(len(values)):
            if n & bit == 0:
                a, b = values[n], values[n + bit]
                values[n] = jnp.where(keep, a, turned(b, side * bit))
                values[n + bit] = jnp.where(keep, turned(a, -side * bit), b)
        bit *= 2
    return values


def edges_kernel(levels, side, table_ref, cell_ref, *refs):
    group = LANES // side
    rounds = cell_ref.shape[1] // levels // group
    level_tiles = levels // SUB

    def body(lt, carry):
        for i in range(rounds):
            row = pl.multiple_of(i * levels + lt * SUB, SUB)
            first, second = [], []
            for g in range(group):
                at = pl.multiple_of((i * group + g) * levels + lt * SUB, SUB)
                first.append(cell_ref[0, pl.ds(at, SUB), 0:LANES])
                second.append(cell_ref[0, pl.ds(at, SUB), LANES : 2 * LANES])
            if len(refs) == 2:
                for ref, column in zip(refs, pack_columns(first, second, side)):
                    ref[0, pl.ds(row, SUB), :] = column
                continue
            for n, quad in enumerate(pack_quads(first, second, side)):
                at = pl.multiple_of((i * (group // 2) + n) * levels + lt * SUB, SUB)
                refs[0][0, pl.ds(at, SUB), :] = quad
        return carry

    lax.fori_loop(0, level_tiles, body, 0, unroll=True)


def first_edges(table, tracers, levels, side, columns):
    slot_count, channels, cell_count = tracers.shape
    lon_count = lax.axis_size("lon")
    rows = channels * side // LANES
    f32 = jnp.float32
    if columns:
        shapes = [jax.ShapeDtypeStruct((slot_count, rows, LANES), f32)] * 2
        specs = [pl.BlockSpec((1, rows, LANES), lambda s, t: (s, 0, 0))] * 2
    else:
        shapes = [jax.ShapeDtypeStruct((lon_count, 4 * rows, LANES), f32)]
        specs = [pl.BlockSpec((1, 4 * rows, LANES), lambda s, t: (t[SLOT_TILE, s], 0, 0))]
    return pl.pallas_call(
        functools.partial(edges_kernel, levels, side),
        out_shape=shapes,
        grid_spec=pltpu.PrefetchScalarGridSpec(
            num_scalar_prefetch=1,
            grid=(slot_count,),
            in_specs=[pl.BlockSpec((1, channels, cell_count), lambda s, t: (s, 0, 0))],
            out_specs=specs,
        ),
        compiler_params=pltpu.CompilerParams(vmem_limit_bytes=VMEM_LIMIT),
        name="first_columns" if columns else "first_rows",
    )(table, tracers)


def growth(
    nitrogen,
    phosphate,
    silicate,
    iron_free,
    nano_carbon,
    diat_carbon,
    micro_zoo,
    meso_zoo,
    par_light,
    warm_factor,
):
    limit_nitro = nitrogen / (0.5 + nitrogen)
    limit_phos = positive(phosphate) / (0.3 + positive(phosphate))
    limit_iron = positive(iron_free) / (0.2 + positive(iron_free))
    limit_sil = positive(silicate) / (1.0 + positive(silicate))
    nutr_nano = jnp.minimum(jnp.minimum(limit_nitro, limit_phos), limit_iron)
    nutr_diat = jnp.minimum(nutr_nano, limit_sil)
    lit = warm_factor * par_light
    prod_nano = 0.1 * lit / (par_light + 0.5) * nutr_nano * nano_carbon
    prod_diat = 0.12 * lit / (par_light + 1.0) * nutr_diat * diat_carbon
    graze_nano = 0.08 * warm_factor * micro_zoo / (1.0 + positive(nano_carbon))
    graze_diat = 0.06 * warm_factor * meso_zoo / (1.0 + positive(diat_carbon))
    return prod_nano, prod_diat, graze_nano, graze_diat


CHL_TRACERS = (3, 4, 5, 6, 7, 8, 9, 10, 11, 15, 16)
CHL_RUN = 3
CHL_BLOCKS = sorted({tracer // CHL_RUN for tracer in CHL_TRACERS})


def chl_after(mixed, par_light, warm_factor):
    (
        nitrate,
        ammonium,
        phosphate,
        silicate,
        iron_free,
        nano_carbon,
        diat_carbon,
        nano_chl,
        diat_chl,
        micro_zoo,
        meso_zoo,
    ) = mixed
    prod_nano, prod_diat, graze_nano, graze_diat = growth(
        positive(nitrate) + positive(ammonium),
        phosphate,
        silicate,
        iron_free,
        nano_carbon,
        diat_carbon,
        micro_zoo,
        meso_zoo,
        par_light,
        warm_factor,
    )
    nano_chl = nano_chl + 0.03 * prod_nano - (graze_nano + 0.02) * nano_chl
    diat_chl = diat_chl + 0.03 * prod_diat - (graze_diat + 0.02) * diat_chl
    return nano_chl, diat_chl


def react(mixed, par_light, warm_factor):
    (
        carbon_dis,
        alkalinity,
        oxygen,
        nitrate,
        ammonium,
        phosphate,
        silicate,
        iron_free,
        nano_carbon,
        diat_carbon,
        nano_chl,
        diat_chl,
        nano_iron,
        diat_iron,
        diat_silica,
        micro_zoo,
        meso_zoo,
        dissolved_org,
        small_part,
        big_part,
        small_iron,
        big_iron,
        big_silica,
        calcite,
    ) = mixed
    nitrogen = positive(nitrate) + positive(ammonium)
    ammon_share = (positive(ammonium) + 0.01) / (nitrogen + 0.02)
    prod_nano, prod_diat, graze_nano, graze_diat = growth(
        nitrogen,
        phosphate,
        silicate,
        iron_free,
        nano_carbon,
        diat_carbon,
        micro_zoo,
        meso_zoo,
        par_light,
        warm_factor,
    )
    loss_nano = graze_nano + 0.02
    loss_diat = graze_diat + 0.02
    eaten_nano = graze_nano * nano_carbon
    eaten_diat = graze_diat * diat_carbon
    death_micro = 0.03 * micro_zoo * positive(micro_zoo)
    death_meso = 0.03 * meso_zoo * positive(meso_zoo)
    remin_doc = 0.03 * warm_factor * dissolved_org
    remin_poc = 0.02 * warm_factor * small_part
    remin_goc = 0.01 * warm_factor * big_part
    nitrify = 0.05 * ammonium
    melt_si = 0.02 * big_silica
    melt_cal = 0.01 * calcite
    melt_sfe = 0.02 * small_iron
    melt_bfe = 0.01 * big_iron
    uptake = prod_nano + prod_diat
    remin_total = remin_doc + remin_poc + remin_goc
    calcify = 0.02 * prod_nano
    gained = remin_total - uptake
    shell = melt_cal - calcify
    by_ammon = ammon_share * uptake
    by_nitrate = 0.16 * (uptake - by_ammon - nitrify)
    return [
        carbon_dis + gained + shell,
        alkalinity + 2.0 * shell + by_nitrate,
        oxygen - 1.3 * gained - 0.32 * nitrify,
        nitrate - by_nitrate,
        ammonium + 0.16 * (remin_total - by_ammon - nitrify),
        phosphate + 0.01 * gained,
        silicate + melt_si - 0.15 * prod_diat,
        iron_free + melt_sfe + melt_bfe - 0.005 * uptake,
        nano_carbon + prod_nano - loss_nano * nano_carbon,
        diat_carbon + prod_diat - loss_diat * diat_carbon,
        nano_chl + 0.03 * prod_nano - loss_nano * nano_chl,
        diat_chl + 0.03 * prod_diat - loss_diat * diat_chl,
        nano_iron + 0.005 * prod_nano - loss_nano * nano_iron,
        diat_iron + 0.005 * prod_diat - loss_diat * diat_iron,
        diat_silica + 0.15 * prod_diat - loss_diat * diat_silica,
        micro_zoo + 0.3 * eaten_nano - death_micro,
        meso_zoo + 0.3 * eaten_diat - death_meso,
        dissolved_org + 0.3 * eaten_nano + 0.02 * nano_carbon - remin_doc,
        small_part + 0.4 * eaten_nano + death_micro - remin_poc,
        big_part + 0.4 * eaten_diat + 0.02 * diat_carbon + death_meso - remin_goc,
        small_iron + loss_nano * nano_iron - melt_sfe,
        big_iron + loss_diat * diat_iron - melt_bfe,
        big_silica + loss_diat * diat_silica - melt_si,
        calcite + calcify - melt_cal,
    ]


def transport(faces, opens):
    flow_e, flow_n, flow_w, flow_s = (face * is_open for face, is_open in zip(faces, opens))
    open_e, open_n, open_w, open_s = opens
    out_e, in_e = jnp.maximum(flow_e, 0.0), jnp.minimum(flow_e, 0.0)
    out_n, in_n = jnp.maximum(flow_n, 0.0), jnp.minimum(flow_n, 0.0)
    in_w, out_w = jnp.maximum(flow_w, 0.0), jnp.minimum(flow_w, 0.0)
    in_s, out_s = jnp.maximum(flow_s, 0.0), jnp.minimum(flow_s, 0.0)
    drift = diffuse_rate * (open_w + open_e + open_s + open_n)
    return (
        1.0 - (out_e - out_w) - (out_n - out_s) - drift,
        diffuse_rate * open_e - in_e,
        diffuse_rate * open_w + in_w,
        diffuse_rate * open_n - in_n,
        diffuse_rate * open_s + in_s,
    )


def set_mixing(coef_ref, at, span, mix, above, bottom):
    sub = lax.broadcasted_iota(jnp.int32, (SUB, LANES), 0)
    mix_up = pltpu.roll(jnp.where(sub == SUB - 1, above, mix), 1, 0)
    if bottom:
        mix = jnp.where(sub == SUB - 1, 0.0, mix)
    coef_ref[5, at, span] = 1.0 - mix - mix_up
    coef_ref[6, at, span] = mix
    coef_ref[7, at, span] = mix_up


def set_blank(moved_ref, channels):
    blank = jnp.zeros((SUB, moved_ref.shape[1]), jnp.float32)
    moved_ref[0:SUB, :] = blank
    moved_ref[SUB + channels : 2 * SUB + channels, :] = blank


def mixed_at(levels, count, span, moved_ref, coef_ref, lt):
    sub = lax.broadcasted_iota(jnp.int32, (SUB, LANES), 0)
    at = pl.multiple_of(lt * SUB, SUB)
    mix_c, mix_d, mix_u = (coef_ref[n, pl.ds(at, SUB), span] for n in (5, 6, 7))
    mixed = []
    for t in range(count):
        base = t * levels + lt * SUB
        before = moved_ref[pl.ds(pl.multiple_of(base, SUB), SUB), span]
        now = moved_ref[pl.ds(pl.multiple_of(base + SUB, SUB), SUB), span]
        after = moved_ref[pl.ds(pl.multiple_of(base + 2 * SUB, SUB), SUB), span]
        up = pltpu.roll(jnp.where(sub == SUB - 1, before, now), 1, 0)
        down = pltpu.roll(jnp.where(sub == 0, after, now), SUB - 1, 0)
        mixed.append(mix_c * now + mix_d * down + mix_u * up)
    return mixed


def lit_at(nano_chl, diat_chl, light, depth):
    sub = lax.broadcasted_iota(jnp.int32, (SUB, LANES), 0)
    absorb = 0.04 + 0.02 * (positive(nano_chl) + positive(diat_chl))
    total = absorb
    for by in (1, 2, 4):
        total = total + jnp.where(sub >= by, pltpu.roll(total, by, 0), 0.0)
    above = depth + (total - absorb)
    return light * jnp.exp(-(above + 0.5 * absorb)), depth + total[SUB - 1 : SUB, :]


def mix_and_react(levels, tracer_count, spans, moved_ref, coef_ref, light, wet, warm_at, store):
    def reacting(lt, carry):
        depths = []
        halves_new = []
        for h, span in enumerate(spans):
            mixed = mixed_at(levels, tracer_count, span, moved_ref, coef_ref, lt)
            par_light, depth = lit_at(mixed[nano_chl_index], mixed[diat_chl_index], light[h], carry[h])
            depths.append(depth)
            halves_new.append([value * wet[h] for value in react(mixed, par_light, warm_at(lt, h))])
            for t in range(tracer_count):
                store(t, pl.multiple_of(t * levels + lt * SUB, SUB), h, halves_new[h][t])
        store(None, lt, None, halves_new)
        return tuple(depths)

    start = tuple(jnp.zeros((1, LANES), jnp.float32) for _ in spans)
    lax.fori_loop(0, levels // SUB, reacting, start, unroll=True)


def block_faces(phys_ref, spans, levels, side, lt):
    group = LANES // side
    pack_at = 4 * levels + SUB
    lane = lane_ids()
    first_col = (lane & (side - 1)) == 0
    first_row = lane < side
    west_pack = phys_ref[0, pack_at : pack_at + SUB, spans[0]]
    south_pack = phys_ref[0, pack_at : pack_at + SUB, spans[1]]
    east = [phys_ref[0, lt * SUB : (lt + 1) * SUB, span] for span in spans]
    north = [phys_ref[0, levels + lt * SUB : levels + (lt + 1) * SUB, span] for span in spans]
    faces = []
    for h in range(len(spans)):
        west = jnp.where(first_col, turned(west_pack, -(h * group + lt)), turned(east[h], 1))
        before = turned(south_pack, -side * lt) if h == 0 else turned(north[h - 1], side)
        south = jnp.where(first_row, before, turned(north[h], side))
        faces.append((east[h], north[h], west, south))
    return faces


def inner_kernel(levels, side, table_ref, cell_ref, phys_ref, out_ref, coef_ref):
    channels, cell_count = cell_ref.shape[1:]
    tracer_count = channels // levels
    halves = cell_count // LANES
    level_tiles = levels // SUB
    spans = [slice(h * LANES, (h + 1) * LANES) for h in range(halves)]
    full = table_ref[SLOT_FULL, pl.program_id(0)] == 1

    @pl.when(jnp.logical_not(full))
    def _():
        out_ref[...] = jnp.zeros_like(out_ref)

    @pl.when(full)
    def _():
        lane = lane_ids()
        col = lane & (side - 1)
        first_row = lane < side
        last_row = lane >= LANES - side
        flag_row = 4 * levels

        def flag(f, h):
            return phys_ref[0, flag_row + f : flag_row + f + 1, spans[h]]

        for lt in range(level_tiles):
            at = slice(lt * SUB, (lt + 1) * SUB)
            for h, faces in enumerate(block_faces(phys_ref, spans, levels, side, lt)):
                c, e, w, n, s = transport(faces, [flag(f, h) for f in range(4)])
                e = jnp.where(col == side - 1, 0.0, e)
                w = jnp.where(col == 0, 0.0, w)
                if h == halves - 1:
                    n = jnp.where(last_row, 0.0, n)
                if h == 0:
                    s = jnp.where(first_row, 0.0, s)
                for k, value in enumerate((c, e, w, n, s)):
                    coef_ref[k, at, spans[h]] = value

        def advect(lt, carry):
            at = pl.multiple_of(lt * SUB, SUB)
            coef = [[coef_ref[n, pl.ds(at, SUB), span] for n in range(5)] for span in spans]
            for t in range(tracer_count):
                chan = pl.multiple_of(t * levels + lt * SUB, SUB)
                here = [cell_ref[0, pl.ds(chan, SUB), span] for span in spans]
                up = [turned(value, side) for value in here]
                down = [turned(value, -side) for value in here]
                for h in range(halves):
                    south = up[h] if h == 0 else jnp.where(first_row, up[h - 1], up[h])
                    north = down[h] if h == halves - 1 else jnp.where(last_row, down[h + 1], down[h])
                    c, e, w, n, s = coef[h]
                    out_ref[0, pl.ds(chan, SUB), spans[h]] = (
                        c * here[h]
                        + (e * turned(here[h], -1) + w * turned(here[h], 1))
                        + (n * north + s * south)
                    )
            return carry

        lax.fori_loop(0, level_tiles, advect, 0, unroll=True)


def inner(table, cells, phys, levels, side):
    slot_count, channels, cell_count = cells.shape
    phys_rows = phys.shape[1]
    by_slot = pl.BlockSpec((1, channels, cell_count), lambda s, t: (s, 0, 0))
    return pl.pallas_call(
        functools.partial(inner_kernel, levels, side),
        out_shape=jax.ShapeDtypeStruct(cells.shape, jnp.float32),
        grid_spec=pltpu.PrefetchScalarGridSpec(
            num_scalar_prefetch=1,
            grid=(slot_count,),
            in_specs=[
                by_slot,
                pl.BlockSpec((1, phys_rows, cell_count), lambda s, t: (t[SLOT_TILE, s], 0, 0)),
            ],
            out_specs=by_slot,
            scratch_shapes=[pltpu.VMEM((5, levels, cell_count), jnp.float32)],
        ),
        compiler_params=pltpu.CompilerParams(vmem_limit_bytes=VMEM_LIMIT),
        name="inner",
    )(table, cells, phys)


def add_rims(
    levels, side, spans, tracers, part_at, phys_ref, rim_ref, rim_w_ref, rim_e_ref, coef_ref, moved_ref, ends_ref
):
    group = LANES // side
    halves = len(spans)
    rows = rim_w_ref.shape[1]
    rounds = rows // levels
    level_tiles = levels // SUB
    lane = lane_ids()
    col = lane & (side - 1)
    first_row = lane < side
    last_row = lane >= LANES - side
    odd = (lane & 1) == 1
    flag_row = 4 * levels

    def flag(f, h):
        return phys_ref[0, flag_row + f : flag_row + f + 1, spans[h]]

    above_mix = [jnp.zeros((SUB, LANES), jnp.float32)] * halves
    for lt in range(level_tiles):
        at = slice(lt * SUB, (lt + 1) * SUB)
        for h, faces in enumerate(block_faces(phys_ref, spans, levels, side, lt)):
            _, e, w, n, s = transport(faces, [flag(f, h) for f in range(4)])
            coef_ref[0, at, spans[h]] = jnp.where(col == 0, w, jnp.where(col == side - 1, e, 0.0))
            if h == 0:
                coef_ref[1, at, spans[h]] = jnp.where(first_row, s, 0.0)
            if h == halves - 1:
                coef_ref[1, at, spans[h]] = jnp.where(last_row, n, 0.0)
            mix = phys_ref[0, 3 * levels + lt * SUB : 3 * levels + (lt + 1) * SUB, spans[h]]
            set_mixing(coef_ref, at, spans[h], mix, above_mix[h], lt == level_tiles - 1)
            above_mix[h] = mix

    for at in range(0, rows, SUB):
        ends_ref[at : at + SUB, :] = turned(rim_w_ref[0, at : at + SUB, :], 2 - 2 * side)
    set_blank(moved_ref, len(tracers) * levels)

    def gather(lt, carry):
        at = pl.multiple_of(lt * SUB, SUB)
        for i in range(rounds):
            row = pl.multiple_of(i * levels + lt * SUB, SUB)
            rims = [
                rim_ref[0, pl.ds(row, SUB), :],
                rim_ref[0, pl.ds(pl.multiple_of(rows + row, SUB), SUB), :],
            ]
            ends_w = ends_ref[pl.ds(row, SUB), :]
            ends_e = rim_e_ref[0, pl.ds(row, SUB), :]
            sides = [jnp.where(odd, ends_e, ends_w), jnp.where(odd, ends_w, ends_e)]
            for g in range(group):
                if i * group + g not in tracers:
                    continue
                place = tracers.index(i * group + g)
                chan = pl.multiple_of(place * levels + lt * SUB, SUB)
                rim = turned(rims[2 * g // group], -side - 2 * side * (g % (group // 2)))
                for h in range(halves):
                    ends = turned(sides[h], side - 2 + h - 2 * g)
                    moved = part_at(place, lt, spans[h])
                    moved = moved + coef_ref[0, pl.ds(at, SUB), spans[h]] * ends
                    if h in (0, halves - 1):
                        moved = moved + coef_ref[1, pl.ds(at, SUB), spans[h]] * rim
                    moved_ref[pl.ds(pl.multiple_of(SUB + chan, SUB), SUB), spans[h]] = moved
        return carry

    lax.fori_loop(0, level_tiles, gather, 0, unroll=True)


def step_kernel(levels, side, last, table_ref, part_ref, phys_ref, rim_ref, rim_w_ref, rim_e_ref, *refs):
    if last:
        out_ref, coef_ref, moved_ref, ends_ref = refs
        edge_refs = ()
    else:
        out_ref, west_ref, east_ref, coef_ref, moved_ref, ends_ref = refs
        edge_refs = (west_ref, east_ref)
    channels, cell_count = part_ref.shape[1:]
    tracer_count = channels // levels
    group = LANES // side
    halves = cell_count // LANES
    rounds = tracer_count // group
    slot = pl.program_id(0)
    full = table_ref[SLOT_FULL, slot] == 1
    spans = [slice(h * LANES, (h + 1) * LANES) for h in range(halves)]

    @pl.when(jnp.logical_not(full))
    def _():
        out_ref[...] = jnp.zeros_like(out_ref)
        for ref in edge_refs:
            ref[...] = jnp.zeros_like(ref)

    @pl.when(full)
    def _():
        flag_row = 4 * levels

        def flag(f, h):
            return phys_ref[0, flag_row + f : flag_row + f + 1, spans[h]]

        def part_at(t, lt, span):
            return part_ref[0, pl.ds(pl.multiple_of(t * levels + lt * SUB, SUB), SUB), span]

        add_rims(
            levels,
            side,
            spans,
            list(range(tracer_count)),
            part_at,
            phys_ref,
            rim_ref,
            rim_w_ref,
            rim_e_ref,
            coef_ref,
            moved_ref,
            ends_ref,
        )

        def store(t, at, h, value):
            if t is not None:
                out_ref[0, pl.ds(at, SUB), spans[h]] = value
            elif not last:
                for i in range(rounds):
                    row = pl.multiple_of(i * levels + at * SUB, SUB)
                    first, second = (new[i * group : (i + 1) * group] for new in value)
                    west, east = pack_columns(first, second, side)
                    west_ref[0, pl.ds(row, SUB), :] = west
                    east_ref[0, pl.ds(row, SUB), :] = east

        def warm_at(lt, h):
            return phys_ref[0, pl.ds(pl.multiple_of(2 * levels + lt * SUB, SUB), SUB), spans[h]]

        light = [flag(LIGHT, h) for h in range(halves)]
        wet = [flag(WET, h) for h in range(halves)]
        mix_and_react(levels, tracer_count, spans, moved_ref, coef_ref, light, wet, warm_at, store)


def step(table, cells, phys, rims, rim_w, rim_e, levels, side, last):
    slot_count, channels, cell_count = cells.shape
    lon_count = lax.axis_size("lon")
    rows = channels * side // LANES
    phys_rows = phys.shape[1]
    f32 = jnp.float32
    by_slot = pl.BlockSpec((1, channels, cell_count), lambda s, t: (s, 0, 0))
    shapes = [jax.ShapeDtypeStruct(cells.shape, f32)]
    specs = [by_slot]
    if not last:
        beside = jax.ShapeDtypeStruct((slot_count, rows, LANES), f32)
        shapes += [beside, beside]
        specs += [pl.BlockSpec((1, rows, LANES), lambda s, t: (s, 0, 0))] * 2
    return pl.pallas_call(
        functools.partial(step_kernel, levels, side, last),
        out_shape=shapes,
        grid_spec=pltpu.PrefetchScalarGridSpec(
            num_scalar_prefetch=1,
            grid=(slot_count,),
            in_specs=[
                by_slot,
                pl.BlockSpec((1, phys_rows, cell_count), lambda s, t: (t[SLOT_TILE, s], 0, 0)),
                pl.BlockSpec((1, 2 * rows, LANES), lambda s, t: (t[SLOT_TILE, s], 0, 0)),
                pl.BlockSpec((1, rows, LANES), lambda s, t: (t[SLOT_WEST, s], 0, 0)),
                pl.BlockSpec((1, rows, LANES), lambda s, t: (t[SLOT_EAST, s], 0, 0)),
            ],
            out_specs=specs,
            scratch_shapes=[
                pltpu.VMEM((8, levels, cell_count), f32),
                pltpu.VMEM((channels + 2 * SUB, cell_count), f32),
                pltpu.VMEM((rows, LANES), f32),
            ],
        ),
        compiler_params=pltpu.CompilerParams(vmem_limit_bytes=VMEM_LIMIT),
        name="step",
    )(table, cells, phys, rims, rim_w, rim_e)


def chl_kernel(levels, side, table_ref, *refs):
    count = len(CHL_TRACERS)
    part_refs = refs[: len(CHL_BLOCKS)]
    phys_ref, rim_ref, rim_w_ref, rim_e_ref, chl_ref, coef_ref, moved_ref, ends_ref = refs[len(CHL_BLOCKS) :]
    halves = chl_ref.shape[2] // LANES
    spans = [slice(h * LANES, (h + 1) * LANES) for h in range(halves)]
    full = table_ref[SLOT_FULL, pl.program_id(0)] == 1
    flag_row = 4 * levels

    @pl.when(jnp.logical_not(full))
    def _():
        chl_ref[...] = jnp.zeros_like(chl_ref)

    @pl.when(full)
    def _():
        def part_at(place, lt, span):
            tracer = CHL_TRACERS[place]
            at = (tracer % CHL_RUN) * levels + lt * SUB
            return part_refs[CHL_BLOCKS.index(tracer // CHL_RUN)][0, pl.ds(pl.multiple_of(at, SUB), SUB), span]

        add_rims(
            levels,
            side,
            spans,
            list(CHL_TRACERS),
            part_at,
            phys_ref,
            rim_ref,
            rim_w_ref,
            rim_e_ref,
            coef_ref,
            moved_ref,
            ends_ref,
        )
        nano = CHL_TRACERS.index(nano_chl_index)
        diat = CHL_TRACERS.index(diat_chl_index)

        def greening(lt, carry):
            at = pl.multiple_of(lt * SUB, SUB)
            depths = []
            for h, span in enumerate(spans):
                mixed = mixed_at(levels, count, span, moved_ref, coef_ref, lt)
                light = phys_ref[0, flag_row + LIGHT : flag_row + LIGHT + 1, span]
                wet = phys_ref[0, flag_row + WET : flag_row + WET + 1, span]
                warm = phys_ref[0, pl.ds(pl.multiple_of(2 * levels + lt * SUB, SUB), SUB), span]
                par_light, depth = lit_at(mixed[nano], mixed[diat], light, carry[h])
                depths.append(depth)
                nano_chl, diat_chl = chl_after(mixed, par_light, warm)
                chl_ref[0, pl.ds(at, SUB), span] = positive(nano_chl * wet) + positive(diat_chl * wet)
            return tuple(depths)

        start = tuple(jnp.zeros((1, LANES), jnp.float32) for _ in spans)
        lax.fori_loop(0, levels // SUB, greening, start, unroll=True)


def last_chl(table, cells, phys, rims, rim_w, rim_e, levels, side):
    slot_count, channels, cell_count = cells.shape
    lon_count = lax.axis_size("lon")
    rows = channels * side // LANES
    count = len(CHL_TRACERS)
    f32 = jnp.float32

    def level_block(number):
        return pl.BlockSpec((1, CHL_RUN * levels, cell_count), lambda s, t: (s, number, 0))

    return pl.pallas_call(
        functools.partial(chl_kernel, levels, side),
        out_shape=jax.ShapeDtypeStruct((lon_count, levels, cell_count), f32),
        grid_spec=pltpu.PrefetchScalarGridSpec(
            num_scalar_prefetch=1,
            grid=(slot_count,),
            in_specs=[level_block(n) for n in CHL_BLOCKS]
            + [
                pl.BlockSpec((1, phys.shape[1], cell_count), lambda s, t: (t[SLOT_TILE, s], 0, 0)),
                pl.BlockSpec((1, 2 * rows, LANES), lambda s, t: (t[SLOT_TILE, s], 0, 0)),
                pl.BlockSpec((1, rows, LANES), lambda s, t: (t[SLOT_WEST, s], 0, 0)),
                pl.BlockSpec((1, rows, LANES), lambda s, t: (t[SLOT_EAST, s], 0, 0)),
            ],
            out_specs=pl.BlockSpec((1, levels, cell_count), lambda s, t: (t[SLOT_TILE, s], 0, 0)),
            scratch_shapes=[
                pltpu.VMEM((8, levels, cell_count), f32),
                pltpu.VMEM((count * levels + 2 * SUB, cell_count), f32),
                pltpu.VMEM((rows, LANES), f32),
            ],
        ),
        compiler_params=pltpu.CompilerParams(vmem_limit_bytes=VMEM_LIMIT),
        name="last_chl",
    )(table, *([cells] * len(CHL_BLOCKS)), phys, rims, rim_w, rim_e)


def rows_kernel(levels, factor, fine_ref, mix_ref, pick_ref, rows_ref):
    f32 = jnp.float32
    picks = pick_ref[...]
    east_face = jnp.zeros((levels, LANES), f32)
    temp_mean = jnp.zeros((levels, LANES), f32)
    for r in range(factor):
        got = jnp.dot(fine_ref[r], picks, preferred_element_type=f32)
        east_face += got[0:levels, 0:LANES]
        temp_mean += got[2 * levels : 3 * levels, LANES : 2 * LANES]
        if r == factor - 1:
            north_face = got[levels : 2 * levels, LANES : 2 * LANES]
    rows_ref[0, 0:levels, :] = east_face * (1.0 / factor)
    rows_ref[0, levels : 2 * levels, :] = north_face * (1.0 / factor)
    rows_ref[0, 2 * levels : 3 * levels, :] = jnp.exp(0.0639 * (temp_mean * (1.0 / (factor * factor))))
    rows_ref[0, 3 * levels : 4 * levels, :] = mix_ref[0].astype(f32)


def coarse_rows(fine, mix, picks):
    side, levels, tile_cols = mix.shape
    factor = fine.shape[0] // side
    fine_cols = fine.shape[2]
    return pl.pallas_call(
        functools.partial(rows_kernel, levels, factor),
        out_shape=jax.ShapeDtypeStruct((side, 4 * levels, tile_cols), jnp.float32),
        grid=(side,),
        in_specs=[
            pl.BlockSpec((factor, 3 * levels, fine_cols), lambda i: (i, 0, 0)),
            pl.BlockSpec((1, levels, tile_cols), lambda i: (i, 0, 0)),
            pl.BlockSpec(picks.shape, lambda i: (0, 0)),
        ],
        out_specs=pl.BlockSpec((1, 4 * levels, tile_cols), lambda i: (i, 0, 0)),
        compiler_params=pltpu.CompilerParams(vmem_limit_bytes=VMEM_LIMIT),
        name="coarse_rows",
    )(fine, mix, picks)


def place_kernel(
    levels,
    side,
    factor,
    table_ref,
    rows_ref,
    light_ref,
    land_ref,
    south_ref,
    north_ref,
    west_ref,
    east_ref,
    pick_ref,
    out_ref,
    line_ref,
    flags_ref,
):
    tile_blocks = land_ref.shape[1] // side
    halves = side * side // LANES
    group = LANES // side
    fine_cols = light_ref.shape[1]
    f32 = jnp.float32
    picks = pick_ref[...]
    lane = lane_ids()
    group_id = lane >> (side.bit_length() - 1)
    col_id = lane & (side - 1)
    flag_row = 4 * levels
    pack_at = flag_row + SUB
    wet = land_ref[...].astype(f32)
    sides = wet.shape
    lane2 = lax.broadcasted_iota(jnp.int32, sides, 1)
    sub2 = lax.broadcasted_iota(jnp.int32, sides, 0)
    diagonal = lane2 == sub2
    rim_w = jnp.sum(jnp.where(diagonal, west_ref[SUB : SUB + 1, :], 0.0), axis=1, keepdims=True)
    rim_e = jnp.sum(jnp.where(diagonal, east_ref[0:1, :], 0.0), axis=1, keepdims=True)
    wet_w = jnp.where(lane2 == 0, rim_w, pltpu.roll(wet, 1, 1))
    wet_e = jnp.where(lane2 == LANES - 1, rim_e, pltpu.roll(wet, LANES - 1, 1))
    wet_s = jnp.where(sub2 == 0, south_ref[levels : levels + 1, 0:LANES], pltpu.roll(wet, 1, 0))
    wet_n = jnp.where(sub2 == side - 1, north_ref[0:1, 0:LANES], pltpu.roll(wet, side - 1, 0))
    fold_r = lax.broadcasted_iota(jnp.int32, (side, side * factor), 0)
    fold_c = lax.broadcasted_iota(jnp.int32, (side, side * factor), 1)
    fold_d = fold_c - factor * fold_r
    fold = jnp.where((fold_d >= 0) & (fold_d < factor), 1.0, 0.0)
    narrow = picks[:, LANES : 2 * LANES].astype(f32)
    light_rows = jnp.dot(fold, light_ref[...], precision=lax.Precision.HIGHEST, preferred_element_type=f32)
    light_mean = jnp.dot(
        light_rows, narrow, precision=lax.Precision.HIGHEST, preferred_element_type=f32
    ) * (1.0 / (factor * factor))
    flags = [wet * wet_e, wet * wet_n, wet * wet_w, wet * wet_s, light_mean, wet]
    for r in range(side):
        for f, value in enumerate(flags):
            flags_ref[r, f : f + 1, :] = value[r : r + 1, :]
        flags_ref[r, len(flags) : SUB, :] = jnp.zeros((SUB - len(flags), LANES), f32)

    def place(ref, frm, to):
        for h in range(halves):
            values = [ref[h * group + r, pl.ds(frm, SUB), :] for r in range(group)]
            for b, block in enumerate(regroup(values, side)):
                owner = table_ref[TILE_OWNER, b]
                out_ref[owner, pl.ds(to, SUB), h * LANES : (h + 1) * LANES] = block

    def place_four(q, carry):
        for n in range(4):
            at = pl.multiple_of(n * levels + q * SUB, SUB)
            place(rows_ref, at, at)
        return carry

    lax.fori_loop(0, levels // SUB, place_four, 0)
    place(flags_ref, 0, flag_row)

    fine_v = south_ref[0:levels, 0:fine_cols].astype(jnp.bfloat16)
    north_below = jnp.dot(fine_v, picks, preferred_element_type=f32)[:, LANES : 2 * LANES] * (1.0 / factor)
    for h, r in enumerate((0, side - 1)):
        span = slice(h * LANES, (h + 1) * LANES)
        line_ref[0 : 4 * levels, span] = rows_ref[r, 0 : 4 * levels, :]
        line_ref[6 * levels : 6 * levels + SUB, span] = flags_ref[r]
        line_ref[5 * levels : 6 * levels, span] = (
            north_below if h == 0 else rows_ref[r - 1, levels : 2 * levels, :]
        )
        from_lane = side * (r % group) + group * (r // group)
        for lt in range(levels // SUB):
            face = rows_ref[r, lt * SUB : (lt + 1) * SUB, :]
            line_ref[4 * levels + lt * SUB : 4 * levels + (lt + 1) * SUB, span] = jnp.where(
                lane == 0, turned(west_ref[0:SUB, :], -(from_lane + lt)), turned(face, 1)
            )
    for b in range(tile_blocks):
        owner = table_ref[TILE_OWNER, b]
        south_pack = jnp.zeros((SUB, LANES), f32)
        for lt in range(levels // SUB):
            piece = turned(north_below[lt * SUB : (lt + 1) * SUB, :], side * (lt - b))
            south_pack = jnp.where(group_id == lt, piece, south_pack)
        if b == 0:
            west_pack = west_ref[0:SUB, :]
        else:
            beside = table_ref[TILE_OWNER, b - 1]
            west_pack = jnp.zeros((SUB, LANES), f32)
            for h in range(halves):
                for lt in range(levels // SUB):
                    face = out_ref[beside, lt * SUB : (lt + 1) * SUB, h * LANES : (h + 1) * LANES]
                    piece = turned(face, h * group + lt - (side - 1))
                    west_pack = jnp.where(col_id == h * group + lt, piece, west_pack)
        out_ref[owner, pack_at : pack_at + SUB, 0:LANES] = west_pack
        out_ref[owner, pack_at : pack_at + SUB, LANES : 2 * LANES] = south_pack


def coarsen(table, rows, light, land, from_south, from_north, from_west, from_east, picks):
    lon_count = lax.axis_size("lon")
    side, tile_cols = land.shape
    levels = rows.shape[1] // 4
    factor = light.shape[0] // side
    phys_rows = 4 * levels + 2 * SUB
    f32 = jnp.float32
    vmem = pl.BlockSpec(memory_space=pltpu.VMEM)
    return pl.pallas_call(
        functools.partial(place_kernel, levels, side, factor),
        out_shape=[
            jax.ShapeDtypeStruct((lon_count, phys_rows, side * side), f32),
            jax.ShapeDtypeStruct((6 * levels + SUB, 2 * LANES), f32),
        ],
        in_specs=[pl.BlockSpec(memory_space=pltpu.SMEM)] + [vmem] * 8,
        out_specs=[vmem, vmem],
        scratch_shapes=[pltpu.VMEM((side, SUB, LANES), f32)],
        compiler_params=pltpu.CompilerParams(vmem_limit_bytes=VMEM_LIMIT),
        name="coarsen",
    )(table, rows, light, land, from_south, from_north, from_west, from_east, picks)


def lines_kernel(levels, side, table_ref, quad_ref, low_ref, high_ref, low_in_ref, high_in_ref, ends_ref):
    tile_blocks = LANES // side
    pairs = quad_ref.shape[1] // levels
    lane = lane_ids()
    spot = lane >> 1

    def body(lt, carry):
        packed = jnp.zeros((SUB, LANES), jnp.float32)
        for m in range(pairs):
            at = pl.multiple_of(m * levels + lt * SUB, SUB)
            blocks = []
            for b in range(tile_blocks):
                value = quad_ref[table_ref[TILE_OWNER, b], pl.ds(at, SUB), :]
                blocks.append(jnp.where(table_ref[TILE_WET, b] == 1, value, 0.0))
            parts = regroup(blocks, side)
            for p in range(2):
                t = 2 * m + p
                chan = pl.ds(pl.multiple_of(t * levels + lt * SUB, SUB), SUB)
                high_in, high, low, low_in = parts[4 * p : 4 * p + 4]
                low_ref[chan, :] = low
                high_ref[chan, :] = high
                low_in_ref[chan, :] = low_in
                high_in_ref[chan, :] = high_in
                for k, line in ((2 * t, low), (2 * t + 1, high)):
                    packed = jnp.where(spot == k, turned(line, 1 + 2 * k), packed)
        ends_ref[pl.ds(pl.multiple_of(lt * SUB, SUB), SUB), :] = packed
        return carry

    lax.fori_loop(0, levels // SUB, body, 0)


def tile_lines(table, quads, levels, side):
    channels = quads.shape[1] // levels * 2 * levels
    vmem = pl.BlockSpec(memory_space=pltpu.VMEM)
    line = jax.ShapeDtypeStruct((channels, LANES), jnp.float32)
    return pl.pallas_call(
        functools.partial(lines_kernel, levels, side),
        out_shape=[line] * 4 + [jax.ShapeDtypeStruct((levels, LANES), jnp.float32)],
        in_specs=[pl.BlockSpec(memory_space=pltpu.SMEM), vmem],
        out_specs=[vmem] * 5,
        compiler_params=pltpu.CompilerParams(vmem_limit_bytes=VMEM_LIMIT),
        name="tile_lines",
    )(table, quads)


def line_kernel(
    levels,
    low_ref,
    high_ref,
    low_in_ref,
    high_in_ref,
    below_ref,
    above_ref,
    west_ref,
    east_ref,
    phys_ref,
    low_out_ref,
    high_out_ref,
    coef_ref,
    moved_ref,
    ends_ref,
):
    channels = low_ref.shape[0]
    tracer_count = channels // levels
    level_tiles = levels // SUB
    lane = lane_ids()
    odd = (lane & 1) == 1
    spans = [slice(0, LANES), slice(LANES, 2 * LANES)]
    flag_row = 6 * levels
    lines = (
        (low_ref, low_in_ref, below_ref, low_out_ref),
        (high_ref, above_ref, high_in_ref, high_out_ref),
    )

    def flag(f, h):
        return phys_ref[flag_row + f : flag_row + f + 1, spans[h]]

    above_mix = [jnp.zeros((SUB, LANES), jnp.float32)] * 2
    for lt in range(level_tiles):
        at = slice(lt * SUB, (lt + 1) * SUB)
        from_west = west_ref[lt * SUB : (lt + 1) * SUB, :]
        from_east = east_ref[lt * SUB : (lt + 1) * SUB, :]
        ends_ref[at, :] = jnp.where(odd, turned(from_east, -2), from_west)
        for h in range(2):
            faces = [
                phys_ref[n * levels + lt * SUB : n * levels + (lt + 1) * SUB, spans[h]] for n in (0, 1, 4, 5)
            ]
            for n, value in enumerate(transport(faces, [flag(f, h) for f in range(4)])):
                coef_ref[n, at, spans[h]] = value
            mix = phys_ref[3 * levels + lt * SUB : 3 * levels + (lt + 1) * SUB, spans[h]]
            set_mixing(coef_ref, at, spans[h], mix, above_mix[h], lt == level_tiles - 1)
            above_mix[h] = mix
    set_blank(moved_ref, channels)

    def advect(lt, carry):
        at = pl.multiple_of(lt * SUB, SUB)
        ends = ends_ref[pl.ds(at, SUB), :]
        for h in range(2):
            here_ref, north_ref, south_ref, _ = lines[h]
            c, e, w, n, s = (coef_ref[k, pl.ds(at, SUB), spans[h]] for k in range(5))
            for t in range(tracer_count):
                chan = pl.multiple_of(t * levels + lt * SUB, SUB)
                here = here_ref[pl.ds(chan, SUB), :]
                end = turned(ends, -2 * (2 * t + h))
                west = jnp.where(lane == 0, end, turned(here, 1))
                east = jnp.where(lane == LANES - 1, end, turned(here, -1))
                moved_ref[pl.ds(pl.multiple_of(SUB + chan, SUB), SUB), spans[h]] = (
                    c * here
                    + (e * east + w * west)
                    + (n * north_ref[pl.ds(chan, SUB), :] + s * south_ref[pl.ds(chan, SUB), :])
                )
        return carry

    lax.fori_loop(0, level_tiles, advect, 0, unroll=True)

    def store(t, at, h, value):
        if t is not None:
            lines[h][3][pl.ds(at, SUB), :] = value

    def warm_at(lt, h):
        return phys_ref[pl.ds(pl.multiple_of(2 * levels + lt * SUB, SUB), SUB), spans[h]]

    light = [flag(LIGHT, h) for h in range(2)]
    wet = [flag(WET, h) for h in range(2)]
    mix_and_react(levels, tracer_count, spans, moved_ref, coef_ref, light, wet, warm_at, store)


def line_step(low, high, low_in, high_in, below, above, from_west, from_east, phys, levels):
    channels = low.shape[0]
    vmem = pl.BlockSpec(memory_space=pltpu.VMEM)
    f32 = jnp.float32
    line = jax.ShapeDtypeStruct((channels, LANES), f32)
    return pl.pallas_call(
        functools.partial(line_kernel, levels),
        out_shape=[line, line],
        in_specs=[vmem] * 9,
        out_specs=[vmem, vmem],
        scratch_shapes=[
            pltpu.VMEM((8, levels, 2 * LANES), f32),
            pltpu.VMEM((channels + 2 * SUB, 2 * LANES), f32),
            pltpu.VMEM((levels, LANES), f32),
        ],
        compiler_params=pltpu.CompilerParams(vmem_limit_bytes=VMEM_LIMIT),
        name="line_step",
    )(low, high, low_in, high_in, below, above, from_west, from_east, phys)


def hand_kernel(levels, side, table_ref, below_ref, above_ref, *refs):
    out_ref = refs[-1]
    group = LANES // side
    rounds = below_ref.shape[0] // levels // group
    half = group // 2

    def body(lt, carry):
        for i in range(rounds):
            for part in range(2):
                lines = []
                for g in range(half):
                    t = i * group + part * half + g
                    chan = pl.ds(pl.multiple_of(t * levels + lt * SUB, SUB), SUB)
                    lines += [above_ref[chan, :], below_ref[chan, :]]
                row = pl.multiple_of((part * rounds + i) * levels + lt * SUB, SUB)
                for b, value in enumerate(regroup(lines, side)):
                    out_ref[table_ref[TILE_OWNER, b], pl.ds(row, SUB), :] = value
        return carry

    lax.fori_loop(0, levels // SUB, body, 0)


def hand_on(table, below, above, levels, side, *after):
    lon_count = lax.axis_size("lon")
    rows = 2 * below.shape[0] * side // LANES
    vmem = pl.BlockSpec(memory_space=pltpu.VMEM)
    return pl.pallas_call(
        functools.partial(hand_kernel, levels, side),
        out_shape=jax.ShapeDtypeStruct((lon_count, rows, LANES), jnp.float32),
        in_specs=[pl.BlockSpec(memory_space=pltpu.SMEM), vmem, vmem]
        + [pl.BlockSpec(memory_space=pl.ANY)] * len(after),
        out_specs=vmem,
        compiler_params=pltpu.CompilerParams(vmem_limit_bytes=VMEM_LIMIT),
        name="hand_on",
    )(table, below, above, *after)


def gate_kernel(*refs):
    pass


def gate(values, *others):
    anywhere = pl.BlockSpec(memory_space=pl.ANY)
    count = len(values)
    return pl.pallas_call(
        gate_kernel,
        out_shape=[jax.ShapeDtypeStruct(x.shape, x.dtype) for x in values],
        in_specs=[anywhere] * (count + len(others)),
        out_specs=[anywhere] * count,
        input_output_aliases={i: i for i in range(count)},
        name="gate",
    )(*values, *others)


def heat_kernel(
    levels,
    side,
    factor,
    table_ref,
    chl_ref,
    light_ref,
    land_ref,
    widen_ref,
    after_ref,
    out_ref,
    rows_ref,
    wide_ref,
):
    tile_blocks = land_ref.shape[1] // side
    halves = side * side // LANES
    group = LANES // side
    fine_cols = light_ref.shape[1]
    fine_rows = light_ref.shape[0]
    f32 = jnp.float32
    group_id = lane_ids() >> (side.bit_length() - 1)

    def place(lt, carry):
        at = pl.multiple_of(lt * SUB, SUB)
        for h in range(halves):
            blocks = []
            for b in range(tile_blocks):
                owner = table_ref[TILE_OWNER, b]
                values = chl_ref[owner, pl.ds(at, SUB), h * LANES : (h + 1) * LANES]
                blocks.append(jnp.where(table_ref[TILE_WET, b] == 1, values, 0.0))
            for r in range(group):
                line = None
                for b in range(tile_blocks):
                    piece = turned(blocks[b], side * (b - r))
                    line = piece if line is None else jnp.where(group_id == b, piece, line)
                rows_ref[pl.ds(pl.multiple_of((h * group + r) * levels + lt * SUB, SUB), SUB), :] = line
        return carry

    lax.fori_loop(0, levels // SUB, place, 0, unroll=True)
    wet = land_ref[...].astype(f32)
    widen = widen_ref[...]
    above = jnp.zeros_like(wet)
    passing = jnp.ones_like(wet)
    for l in range(levels):
        chl = rows_ref[pl.ds(l, side, stride=levels), :]
        above = above + (0.04 + 0.02 * chl)
        through = jnp.exp(-above)
        kept = (passing - through) * wet
        passing = through
        high = kept.astype(jnp.bfloat16)
        low = (kept - high.astype(f32)).astype(jnp.bfloat16)
        wide_ref[l * side : (l + 1) * side, :] = jnp.dot(
            high, widen, preferred_element_type=f32
        ) + jnp.dot(low, widen, preferred_element_type=f32)

    sub = lax.broadcasted_iota(jnp.int32, (SUB, LANES), 0)
    sources = []
    for m in range(fine_rows // SUB):
        start = (m * SUB // factor) // SUB * SUB
        index = jnp.zeros_like(sub)
        for r in range(1, side):
            index = index + jnp.where(sub + m * SUB >= r * factor, 1, 0)
        sources.append((start, index - start))

    def spread(l, carry):
        for c in range(fine_cols // LANES):
            span = slice(c * LANES, (c + 1) * LANES)
            for m in range(0, fine_rows // SUB, 2):
                both = []
                for n in (m, m + 1):
                    start, index = sources[n]
                    lines = wide_ref[pl.ds(pl.multiple_of(l * side + start, SUB), SUB), span]
                    lines = jnp.take_along_axis(lines, index, axis=0)
                    both.append(lines * light_ref[n * SUB : (n + 1) * SUB, span])
                out_ref[l, m * SUB : (m + 2) * SUB, span] = jnp.concatenate(both, axis=0).astype(jnp.bfloat16)
        return carry

    lax.fori_loop(0, levels, spread, 0, unroll=4)


def heat(table, chl, light, land, levels, widen, after):
    side = land.shape[0]
    factor = light.shape[0] // side
    vmem = pl.BlockSpec(memory_space=pltpu.VMEM)
    return pl.pallas_call(
        functools.partial(heat_kernel, levels, side, factor),
        out_shape=jax.ShapeDtypeStruct((levels,) + light.shape, jnp.bfloat16),
        in_specs=[pl.BlockSpec(memory_space=pltpu.SMEM), vmem, vmem, vmem, vmem]
        + [pl.BlockSpec(memory_space=pl.ANY)],
        out_specs=vmem,
        scratch_shapes=[
            pltpu.VMEM(((side + 1) * levels, LANES), jnp.float32),
            pltpu.VMEM((side * levels, light.shape[1]), jnp.float32),
        ],
        compiler_params=pltpu.CompilerParams(vmem_limit_bytes=VMEM_LIMIT),
        name="heat",
    )(table, chl, light, land, widen, after)


def widened(x, rows, width):
    return jnp.pad(x, ((0, rows - x.shape[0]), (0, width - x.shape[1])))


def on_device(tracers, phys_fine, mix_coarse, surf_light, land_mask, owner_map):
    f32 = jnp.float32
    slot_count = tracers.shape[0]
    side = land_mask.shape[0]
    levels = mix_coarse.shape[2]
    tile_blocks = land_mask.shape[1] // side
    factor = phys_fine.shape[0] // side
    fine_cols = phys_fine.shape[1]
    group = LANES // side

    fine = jnp.transpose(phys_fine, (0, 2, 1))
    mix = jnp.transpose(mix_coarse, (0, 2, 1))
    wet = land_mask.astype(f32)
    width = fine_cols

    northward = jnp.concatenate(
        [
            widened(fine[-1, levels : 2 * levels, :].astype(f32), levels, width),
            widened(wet[-1:], 1, width),
        ],
        axis=0,
    )
    southward = widened(wet[:1], 1, width)
    last_face = jnp.mean(
        fine[:, :levels, fine_cols - 1].astype(f32).reshape(side, factor, levels), axis=1
    )
    face_pack = jnp.pad(
        last_face.reshape(side // group, group, levels // SUB, SUB).transpose(3, 1, 0, 2),
        ((0, 0), (0, 0), (0, 0), (0, group - levels // SUB)),
    ).reshape(SUB, LANES)
    eastward = jnp.concatenate([face_pack, widened(wet[:, -1][None], 1, LANES)], axis=0)
    westward = widened(wet[:, 0][None], 1, LANES)

    from_south = lax.ppermute(northward, "lat", along("lat", 1, False))
    from_north = lax.ppermute(southward, "lat", along("lat", -1, False))
    from_west = lax.ppermute(eastward, "lon", along("lon", 1, True))
    from_east = lax.ppermute(westward, "lon", along("lon", -1, True))

    fine_id = jnp.arange(fine_cols)[:, None]
    coarse_id = jnp.arange(land_mask.shape[1])[None, :]
    member = (fine_id // factor == coarse_id).astype(jnp.bfloat16)
    final = (fine_id == factor * coarse_id + factor - 1).astype(jnp.bfloat16)
    picks = jnp.concatenate([final, member], axis=1)

    table = routing(owner_map, slot_count, tile_blocks)
    def to_north(x):
        return lax.ppermute(x, "lat", along("lat", 1, False))

    def to_south(x):
        return lax.ppermute(x, "lat", along("lat", -1, False))

    def to_east(x):
        return lax.ppermute(x, "lon", along("lon", 1, True))

    def to_west(x):
        return lax.ppermute(x, "lon", along("lon", -1, True))

    def across(x):
        return lax.all_to_all(x, "lon", 0, 0, tiled=True)

    (quads,) = first_edges(table, tracers, levels, side, False)
    quads = across(quads)
    west, east = first_edges(table, tracers, levels, side, True)
    rows = coarse_rows(fine, mix, picks)
    phys, line_phys = coarsen(
        table, rows, surf_light, land_mask, from_south, from_north, from_west, from_east, picks
    )
    phys = across(phys)
    low, high, low_in, high_in, ends = tile_lines(table, quads, levels, side)
    below, above = to_north(high), to_south(low)
    west, east = gate((west, east), phys)
    rim_w, rim_e = to_east(east), to_west(west)
    ends_w, ends_e = to_east(ends), to_west(ends)
    rims = across(hand_on(table, below, above, levels, side, phys, ends_w, ends_e))
    new_low, new_high = line_step(
        low, high, low_in, high_in, below, above, ends_w, ends_e, line_phys, levels
    )
    below, above = to_north(new_high), to_south(new_low)
    partial = inner(table, tracers, phys, levels, side)
    (handed,) = gate((hand_on(table, below, above, levels, side),), rims, rim_w, rim_e, partial)
    new_rims = across(handed)
    current, west, east = step(table, partial, phys, rims, rim_w, rim_e, levels, side, False)
    rim_w, rim_e = to_east(east), to_west(west)
    partial = inner(table, current, phys, levels, side)
    chl = across(last_chl(table, partial, phys, new_rims, rim_w, rim_e, levels, side))
    (current,) = step(table, partial, phys, new_rims, rim_w, rim_e, levels, side, True)
    heating = heat(table, chl, surf_light, land_mask, levels, jnp.transpose(member), current)
    return current, heating


def solution(mesh):
    in_specs = (
        P(("lat", "lon"), None, None),
        P("lat", "lon", None),
        P("lat", "lon", None),
        P("lat", "lon"),
        P("lat", "lon"),
        P("lat", None),
    )
    out_specs = (P(("lat", "lon"), None, None), P(None, "lat", "lon"))
    return jax.shard_map(
        on_device, mesh=mesh, in_specs=in_specs, out_specs=out_specs, check_vma=False
    )
```
